32 devices in a mesh: wide: 16 (over z, x, core), narrow: 2 (over y).
Axes of the slice: x: 2, y: 2, z: 4, core: 2. Of those that a mesh axis runs over, the one named last changes fastest.
Arguments:
- tokens: bfloat16 [32768, 768], P('wide', 'narrow'), may hold values from -6 to 6
- lengths: int32 [256], P('wide'), may hold values from 32 to 128
- mask_pos: int32 [256, 38], P('wide'), may hold values from 0 to 127, as said below
- mask_vector: bfloat16 [768], P('narrow'), may hold values from -6 to 6
- norm1_gain: bfloat16 [768], P('narrow'), may hold values from 0.099609375 to 1.8984375
- in_left: bfloat16 [4, 192, 192], P('narrow'), may hold values from -0.4375 to 0.4375
- in_right: bfloat16 [4, 192, 576], P('narrow'), may hold values from -0.4375 to 0.4375
- filter_weight: bfloat16 [128, 768], P(None, 'narrow'), may hold values from -0.0625 to 0.0625
- decay: float32 [768], P('narrow'), may hold values from 0.005 to 0.1
- skip_gain: bfloat16 [768], P('narrow'), may hold values from -4 to 4
- out_left: bfloat16 [4, 192, 192], P('narrow'), may hold values from -0.4375 to 0.4375
- out_right: bfloat16 [4, 192, 192], P('narrow'), may hold values from -0.4375 to 0.4375
- norm2_gain: bfloat16 [768], P('narrow'), may hold values from 0.099609375 to 1.8984375
- up_left: bfloat16 [4, 192, 192], P('narrow'), may hold values from -0.4375 to 0.4375
- up_right: bfloat16 [4, 192, 1536], P('narrow'), may hold values from -0.4375 to 0.4375
- down_left: bfloat16 [4, 768, 192], P('narrow'), may hold values from -0.21875 to 0.21875
- down_right: bfloat16 [4, 192, 192], P('narrow'), may hold values from -0.4375 to 0.4375
- cotangent: bfloat16 [32768, 768], P('wide', 'narrow'), may hold values from -6 to 6
Outputs:
- output: bfloat16 [32768, 768], P('wide', 'narrow')
- tokens_grad: float32 [32768, 768], P('wide', 'narrow')
- mask_vector_grad: float32 [768], P('narrow')
- norm1_gain_grad: float32 [768], P('narrow')
- in_left_grad: float32 [4, 192, 192], P('narrow')
- in_right_grad: float32 [4, 192, 576], P('narrow')
- filter_weight_grad: float32 [128, 768], P(None, 'narrow')
- decay_grad: float32 [768], P('narrow')
- skip_gain_grad: float32 [768], P('narrow')
- out_left_grad: float32 [4, 192, 192], P('narrow')
- out_right_grad: float32 [4, 192, 192], P('narrow')
- norm2_gain_grad: float32 [768], P('narrow')
- up_left_grad: float32 [4, 192, 192], P('narrow')
- up_right_grad: float32 [4, 192, 1536], P('narrow')
- down_left_grad: float32 [4, 768, 192], P('narrow')
- down_right_grad: float32 [4, 192, 192], P('narrow')
- penalty: float32 [], replicated
The draws below stay inside these ranges and needn't reach their ends.
Inputs may be any that keep to these rules, and one draw needn't show every extreme that they name: `mask_pos`: the 38 positions of one sequence are all different.
All inputs are finite; a program needn't handle non-finite values.
Results may differ from the reference program's by a relative error of at most 0.02.
Values may be sent and summed in bfloat16 or wider, within the bound.
No kernel may reach another device: no remote copies, remote signals or barrier semaphores. Data moves between devices by JAX's collectives and lax.ppermute only.
A program may use at most 256 MiB of HBM per device.

```python
import math
import jax
import jax.numpy as jnp
from jax import lax

D = 768
FF = 3072
NB = 4
ORDER = 128
LEN = 128
NMASK = 38
BS = 192
FB = 768
SEQS = 256
TOKENS = 32768


def draw_mask_pos(key, part):
    key = jax.random.fold_in(key, 1)
    keys = jax.random.split(key, SEQS)

    def one_row(row_key):
        return jax.random.permutation(row_key, LEN)[:NMASK]
    return jax.vmap(one_row)(keys).astype(jnp.int32)


def with_ends(entries, key, smallest, high):
    longest = entries.shape.index(max(entries.shape))
    spots = []
    for shift in (0, 1):
        where = [jax.random.randint(jax.random.fold_in(key, axis), (), 0, length) for axis, length in enumerate(entries.shape)]
        where[longest] = (where[longest] + shift) % entries.shape[longest]
        spots.append(tuple(where))
    return entries.at[spots[0]].set(smallest).at[spots[1]].set(high)


def shard_levels(rng, shape, cuts, low, largest):
    loudness = 1.0
    for dim, shards_of in cuts:
        draws = jax.random.uniform(jax.random.fold_in(jax.random.fold_in(rng, 6), dim), (shards_of,), jnp.float32, low / len(cuts), largest / len(cuts))
        loudness = loudness * jnp.repeat(jnp.exp(draws), shape[dim] // shards_of).reshape((-1,) + (1,) * (len(shape) - 1 - dim))
    return loudness


def gaussian(own_key, dims, deviation, bound, cuts=(), kind=jnp.bfloat16):
    values = deviation * jax.random.normal(own_key, dims, jnp.float32)
    if cuts:
        values = values * shard_levels(own_key, dims, cuts, -0.22, 0.18)
    return jnp.clip(values, -bound, bound).astype(kind)


def setup_inputs(seed: int = 0) -> dict:
    key_list = jax.random.split(jax.random.key(seed), 19)
    tokens = gaussian(key_list[0], (TOKENS, D), 1.0, 6.0, ((0, 16), (1, 2)))
    lengths = with_ends(jax.random.randint(key_list[1], (SEQS,), LEN // 4, LEN + 1), jax.random.fold_in(key_list[1], 1), LEN // 4, LEN).astype(jnp.int32)
    mask_pos = draw_mask_pos(jax.random.fold_in(key_list[18], 71), 0)
    mask_vector = gaussian(key_list[3], (D,), 1.0, 6.0, ((0, 2),))
    norm1_gain = jnp.clip(1.0 + 0.18 * jax.random.normal(key_list[4], (D,), jnp.float32), 0.099609375, 1.8984375).astype(jnp.bfloat16)
    in_left = gaussian(key_list[5], (NB, BS, BS), BS ** -0.5, 0.4375, ((0, 2),))
    in_right = gaussian(key_list[6], (NB, BS, 3 * BS), BS ** -0.5, 0.4375, ((0, 2),))
    filter_weight = gaussian(key_list[7], (ORDER, D), (ORDER * 64) ** -0.5, 0.0625, ((1, 2),))
    decay = jnp.clip(jnp.exp(math.log(0.1) - 2.9957323 * jax.random.uniform(key_list[8], (D,), jnp.float32) ** shard_levels(key_list[8], (D,), ((0, 2),), -0.2, 0.2)), 0.005, 0.1)
    skip_gain = gaussian(key_list[9], (D,), 1.0, 4.0, ((0, 2),))
    out_left = gaussian(key_list[10], (NB, BS, BS), BS ** -0.5, 0.4375, ((0, 2),))
    out_right = gaussian(key_list[11], (NB, BS, BS), BS ** -0.5, 0.4375, ((0, 2),))
    norm2_gain = jnp.clip(1.0 + 0.18 * jax.random.normal(key_list[12], (D,), jnp.float32), 0.099609375, 1.8984375).astype(jnp.bfloat16)
    up_left = gaussian(key_list[13], (NB, BS, BS), BS ** -0.5, 0.4375, ((0, 2),))
    up_right = gaussian(key_list[14], (NB, BS, 2 * FB), BS ** -0.5, 0.4375, ((0, 2),))
    down_left = gaussian(key_list[15], (NB, FB, BS), FB ** -0.5, 0.21875, ((0, 2),))
    down_right = gaussian(key_list[16], (NB, BS, BS), BS ** -0.5, 0.4375, ((0, 2),))
    cotangent = gaussian(key_list[17], (TOKENS, D), 1.0, 6.0, ((0, 16), (1, 2)))
    return {"tokens": tokens, "lengths": lengths, "mask_pos": mask_pos, "mask_vector": mask_vector, "norm1_gain": norm1_gain, "in_left": in_left, "in_right": in_right, "filter_weight": filter_weight, "decay": decay, "skip_gain": skip_gain, "out_left": out_left, "out_right": out_right, "norm2_gain": norm2_gain, "up_left": up_left, "up_right": up_right, "down_left": down_left, "down_right": down_right, "cotangent": cotangent}


@jax.custom_vjp
def low(v):
    return lax.optimization_barrier(v.astype(jnp.bfloat16)).astype(jnp.float32)

@jax.custom_vjp
def low_back(v):
    return v

def low_keep(v):
    return (low(v), None)

def low_pass(kept, grad):
    return (grad,)

def back_keep(v):
    return (v, None)

def back_low(kept, grad):
    return (low(grad),)
low.defvjp(low_keep, low_pass)
low_back.defvjp(back_keep, back_low)
epsilon = 1e-05
penalty_weight = 0.005
highest = lax.Precision.HIGHEST

def features():
    positions = jnp.arange(LEN, dtype=jnp.float32)[:, None]
    freqs = (jnp.arange(ORDER // 2, dtype=jnp.float32)[None, :] + 1.0) * (3.1 / (ORDER // 2))
    return jnp.concatenate([jnp.sin(positions * freqs), jnp.cos(positions * freqs)], axis=1)

def filter_values(filter_weight, decay):
    positions = jnp.arange(LEN, dtype=jnp.float32)[:, None]
    basis = jnp.dot(features(), filter_weight, precision=highest)
    return basis * jnp.exp(-decay[None, :] * positions)

def lag_table():
    positions = jnp.arange(LEN, dtype=jnp.int32)
    lagged = positions[:, None] - positions[None, :]
    return (lagged.reshape(LEN * LEN, 1) == positions[None, :]).astype(jnp.float32)

def layer_norm(inputs, gain):
    center = inputs - lax.optimization_barrier(jnp.mean(inputs, axis=1, keepdims=True))
    spread = lax.optimization_barrier(jnp.mean(center * center, axis=1, keepdims=True))
    return center * lax.rsqrt(spread + epsilon) * gain[None, :]

def monarch_left(inputs, left):
    row_count = inputs.shape[0]
    pieces = inputs.reshape(row_count, NB, -1)
    shaped = left.reshape(NB, left.shape[1], NB, -1)
    mixed = jnp.einsum('tbi,bigm->tgbm', pieces, shaped, precision=highest)
    return mixed.reshape(row_count, NB, -1)

def monarch_right(moved, right):
    return jnp.einsum('tgk,gko->tgo', moved, right, precision=highest)

def forward(tokens_in, valid_mask, masked, mask_vector, norm1_gain, in_left, in_right, filter_weight, decay, skip_gain, out_left, out_right, norm2_gain, up_left, up_right, down_left, down_right):
    row_count = tokens_in.shape[0]
    seq_count = row_count // LEN
    entered = tokens_in + masked * (mask_vector[None, :] - tokens_in)
    normed_one = low(layer_norm(entered, norm1_gain))
    moved_one = low_back(low(monarch_left(normed_one, in_left)))
    projected = low_back(monarch_right(moved_one, in_right))
    gate_first = projected[:, :, :BS].reshape(row_count, D)
    gate_second = projected[:, :, BS:2 * BS].reshape(row_count, D)
    values_in = projected[:, :, 2 * BS:].reshape(row_count, D)
    source = low(gate_first * values_in * valid_mask)
    filter_low = low(filter_values(filter_weight, decay))
    kernel = jnp.dot(lag_table(), filter_low, precision=highest).reshape(LEN, LEN, D)
    convolved = jnp.einsum('tjc,sjc->stc', kernel, source.reshape(seq_count, LEN, D), precision=highest)
    convolved = low_back(convolved.reshape(row_count, D))
    mixed_low = low(gate_second * (convolved + skip_gain[None, :] * source))
    moved_two = low_back(low(monarch_left(mixed_low, out_left)))
    middle = entered + low_back(monarch_right(moved_two, out_right)).reshape(row_count, D)
    normed_two = low(layer_norm(middle, norm2_gain))
    moved_three = low_back(low(monarch_left(normed_two, up_left)))
    gated_proj = low_back(monarch_right(moved_three, up_right))
    activated = jax.nn.gelu(gated_proj[:, :, :FB], approximate=False) * gated_proj[:, :, FB:]
    hidden = low(activated.reshape(row_count, FF))
    moved_four = low_back(low(monarch_left(hidden, down_left)))
    return middle + monarch_right(moved_four, down_right).reshape(row_count, D)

def penalty_of(filter_weight, decay):
    taps = filter_values(filter_weight, decay)
    return penalty_weight * jnp.sum(taps * taps)

def reference(tokens, lengths, mask_pos, mask_vector, norm1_gain, in_left, in_right, filter_weight, decay, skip_gain, out_left, out_right, norm2_gain, up_left, up_right, down_left, down_right, cotangent):
    params = tuple((item.astype(jnp.float32) for item in (mask_vector, norm1_gain, in_left, in_right, filter_weight, decay, skip_gain, out_left, out_right, norm2_gain, up_left, up_right, down_left, down_right)))
    group = math.gcd(SEQS, 32)
    steps = SEQS // group
    row_count = group * LEN
    positions = jnp.arange(LEN, dtype=jnp.int32)
    valid_all = (positions[None, :] < lengths[:, None]).astype(jnp.float32).reshape(steps, row_count, 1)
    masked_all = jnp.any(mask_pos[:, :, None] == positions[None, None, :], axis=1).astype(jnp.float32).reshape(steps, row_count, 1)
    inputs = tokens.astype(jnp.float32).reshape(steps, row_count, D)
    cotangents = cotangent.astype(jnp.float32).reshape(steps, row_count, D)

    def one_group(totals, pieces):
        tokens_in, cotangent_in, valid_mask, masked = pieces

        def run(tokens_arg, *weights):
            return forward(tokens_arg, valid_mask, masked, *weights)
        result, pull = jax.vjp(run, tokens_in, *params)
        grads = pull(cotangent_in)
        totals = tuple((total + grad for total, grad in zip(totals, grads[1:])))
        return (totals, (result.astype(jnp.bfloat16), grads[0]))
    zeros = tuple((jnp.zeros_like(item) for item in params))
    totals, (outputs, token_grads) = lax.scan(one_group, zeros, (inputs, cotangents, valid_all, masked_all))
    penalty, pen_pull = jax.vjp(penalty_of, params[4], params[5])
    pen_weight, pen_decay = pen_pull(jnp.ones((), jnp.float32))
    grads = list(totals)
    grads[4] = grads[4] + pen_weight
    grads[5] = grads[5] + pen_decay
    return (outputs.reshape(TOKENS, D), token_grads.reshape(TOKENS, D), grads[0], grads[1], grads[2], grads[3], grads[4], grads[5], grads[6], grads[7], grads[8], grads[9], grads[10], grads[11], grads[12], grads[13], penalty)
```

```python
import functools

import jax
import jax.numpy as jnp
import numpy as np
from jax import lax
from jax.experimental import pallas as pl
from jax.experimental.pallas import tpu as pltpu
from jax.sharding import PartitionSpec as P

D = 768
NB = 4
ORDER = 128
LEN = 128
BS = 192
FB = 768
GROUP = BS // NB
HALF = D // 2
QUARTER = BS // 4

epsilon = 1e-05
penalty_weight = 0.005

bf16 = jnp.bfloat16
f32 = jnp.float32

TILE = 256
CHUNKS = 2
VMEM = 60 << 20

MIX_W = 6 * QUARTER
FFN_W = 8 * QUARTER + 4 * QUARTER + 2 * QUARTER
FFN_G = 2560
MIX_G = 1536


def transform_tables():
    t = np.arange(LEN, dtype=np.float64)[:, None]
    k = np.arange(LEN, dtype=np.float64)[None, :]
    angle = np.pi * (2 * k + 1) * t / (2 * LEN)
    forward = np.concatenate([np.cos(angle), np.sin(angle)], axis=1)
    return forward.astype(bf16), (forward.T / LEN).astype(bf16)


def feature_parts():
    t = np.arange(LEN, dtype=np.float64)[None, :]
    freqs = (np.arange(ORDER // 2, dtype=np.float64)[:, None] + 1.0) * (3.1 / (ORDER // 2))
    table = np.concatenate([np.sin(t * freqs), np.cos(t * freqs)], axis=0)
    parts = []
    for _ in range(3):
        part = table.astype(bf16)
        parts.append(part)
        table = table - part.astype(np.float64)
    return np.stack(parts)


def nn(a, b):
    return lax.dot_general(a, b, (((1,), (0,)), ((), ())), preferred_element_type=f32)


def nt(a, b):
    return lax.dot_general(a, b, (((1,), (1,)), ((), ())), preferred_element_type=f32)


def tn(a, b):
    return lax.dot_general(a, b, (((0,), (0,)), ((), ())), preferred_element_type=f32)


def exact_nt(a, b):
    return lax.dot_general(
        a,
        b,
        (((1,), (1,)), ((), ())),
        preferred_element_type=f32,
        precision=lax.Precision.HIGHEST,
    )


def fold(values):
    out = values[:, :LEN]
    for start in range(LEN, values.shape[1], LEN):
        out = out + values[:, start : start + LEN]
    return out


def rows_of(block, size):
    return pl.ds(pl.multiple_of(block * size, size), size)


def column(cols_ref, index):
    return cols_ref[:, index : index + 1]


def place_halves(dst_ref, side, own, other):
    dst_ref[rows_of(side, HALF), :] = own
    dst_ref[rows_of(1 - side, HALF), :] = other


def regroup(dst_ref, block, values):
    for g in range(NB):
        dst_ref[g * BS + block * GROUP : g * BS + (block + 1) * GROUP, :] = values[
            g * GROUP : (g + 1) * GROUP, :
        ]


def block(ref, index, size=BS):
    return ref[index * size : (index + 1) * size, :]


def norm_stats(values):
    center = values - jnp.sum(values, axis=0, keepdims=True) * (1.0 / D)
    spread = jnp.sum(center * center, axis=0, keepdims=True) * (1.0 / D)
    scale_row = lax.rsqrt(spread + epsilon)
    return center * scale_row, scale_row


def norm_back(grad, normed, scale_row, gain):
    scaled = grad * gain
    first = jnp.sum(scaled, axis=0, keepdims=True) * (1.0 / D)
    second = jnp.sum(scaled * normed, axis=0, keepdims=True) * (1.0 / D)
    return scale_row * (scaled - first - normed * second)


def pack_kernel(s_ref, il, ir, ol, orr, ul, ur, dl, dr, mix_ref, ffn_ref):
    def pairs(ref):
        return jnp.concatenate([ref[0], ref[1]], axis=1)

    q = QUARTER
    mix_ref[0:q, :] = pairs(il)
    wide_in = pairs(ir)
    for c in range(3):
        mix_ref[(1 + c) * q : (2 + c) * q, :] = wide_in[:, c * HALF : (c + 1) * HALF]
    mix_ref[4 * q : 5 * q, :] = pairs(ol)
    mix_ref[5 * q : 6 * q, :] = pairs(orr)
    for j in range(2):
        for c in range(4):
            ffn_ref[(4 * j + c) * q : (4 * j + c + 1) * q, :] = ur[j][:, c * HALF : (c + 1) * HALF]
    ffn_ref[8 * q : 12 * q, :] = pairs(dl)
    ffn_ref[12 * q : 13 * q, :] = pairs(ul)
    ffn_ref[13 * q : 14 * q, :] = pairs(dr)


def pack_weights(quarter, weights):
    def spec(item):
        return pl.BlockSpec(
            (2, item.shape[1] // 4, item.shape[2]), lambda i, s: (0, s[0], 0)
        )

    return pl.pallas_call(
        pack_kernel,
        out_shape=(
            jax.ShapeDtypeStruct((MIX_W, HALF), bf16),
            jax.ShapeDtypeStruct((FFN_W, HALF), bf16),
        ),
        grid_spec=pltpu.PrefetchScalarGridSpec(
            num_scalar_prefetch=1,
            grid=(1,),
            in_specs=[spec(item) for item in weights],
            out_specs=(
                pl.BlockSpec((MIX_W, HALF), lambda i, s: (0, 0)),
                pl.BlockSpec((FFN_W, HALF), lambda i, s: (0, 0)),
            ),
        ),
        name="pack_weights",
    )(quarter, *weights)


def unpack_narrow(dst, other, row, piece, base):
    for j in range(2):
        dst[2 * other + j, pl.ds(row, QUARTER), :] = piece[
            base : base + QUARTER, j * BS : (j + 1) * BS
        ]


def own_blocks(dst, side, src):
    for j in range(2):
        dst[2 * side + j] = src[j]


def filter_kernel(s_ref, own, oth, cols, feats, fwd, taps_ref, spec_ref, pen_ref):
    side = s_ref[0]
    for which, src in ((side, own), (1 - side, oth)):
        weight = src[...]
        basis = tn(weight, feats[2]) + tn(weight, feats[1]) + tn(weight, feats[0])
        taps_ref[rows_of(which, HALF), :] = basis
    positions = lax.broadcasted_iota(jnp.int32, (1, LEN), 1).astype(f32)
    taps = taps_ref[...] * jnp.exp(-column(cols, 4) * positions)
    taps_ref[...] = taps
    spec_ref[...] = nn(taps.astype(bf16), fwd[...])
    total = jnp.sum(jnp.sum(taps * taps, axis=0, keepdims=True), axis=1, keepdims=True)
    pen_ref[...] = jnp.broadcast_to(total * penalty_weight, (8, LEN))


def whole(shape):
    return pl.BlockSpec(shape, lambda *_: (0,) * len(shape))


def filter_call(scalars, own, oth, cols, feats, fwd):
    ins = (own, oth, cols, feats, fwd)
    outs = (
        jax.ShapeDtypeStruct((D, LEN), f32),
        jax.ShapeDtypeStruct((D, 2 * LEN), f32),
        jax.ShapeDtypeStruct((8, LEN), f32),
    )
    return pl.pallas_call(
        filter_kernel,
        out_shape=outs,
        grid_spec=pltpu.PrefetchScalarGridSpec(
            num_scalar_prefetch=1,
            grid=(1,),
            in_specs=[whole(item.shape) for item in ins],
            out_specs=tuple(whole(item.shape) for item in outs),
        ),
        name="filter_spectrum",
    )(scalars, *ins)


def mixer_forward_kernel(
    s_ref,
    own,
    oth,
    marks,
    cols,
    spec,
    fwd,
    inv,
    *refs,
    first,
):
    if first:
        il, ir, ol, orr, p0, p1, p2, p3 = refs[:8]
        refs = refs[8:]
        middle, kept, scale, wil, wir, wol, wor = refs[:7]
        refs = refs[7:]
    else:
        wil, wir, wol, wor = refs[:4]
        middle, kept, scale = refs[4:7]
        refs = refs[7:]
    enter, half, moved, conv = refs
    side = s_ref[0]
    if first:

        @pl.when(pl.program_id(0) == 0)
        def _():
            other = 1 - side
            own_blocks(wil, side, il)
            own_blocks(wir, side, ir)
            own_blocks(wol, side, ol)
            own_blocks(wor, side, orr)
            q = QUARTER
            for p, piece in enumerate((p0, p1, p2, p3)):
                row = pl.multiple_of(jnp.bitwise_xor(s_ref[1], p) * q, q)
                unpack_narrow(wil, other, row, piece, 0)
                at = pl.ds(row, q)
                wir[2 * other, at, 0:HALF] = piece[q : 2 * q, :]
                wir[2 * other, at, HALF : 3 * BS] = piece[2 * q : 3 * q, 0:BS]
                wir[2 * other + 1, at, 0:BS] = piece[2 * q : 3 * q, BS:HALF]
                wir[2 * other + 1, at, BS : 3 * BS] = piece[3 * q : 4 * q, :]
                unpack_narrow(wol, other, row, piece, 4 * q)
                unpack_narrow(wor, other, row, piece, 5 * q)

    place_halves(enter, side, own[...].T.astype(f32), oth[...].T.astype(f32))
    valid = marks[0:1, :]
    masked = marks[1:2, :]
    tokens = enter[...]
    entered = tokens + masked * (column(cols, 0) - tokens)
    enter[...] = entered
    normed, scale_row = norm_stats(entered)
    scale[...] = jnp.broadcast_to(scale_row, scale.shape)
    half[...] = (normed * column(cols, 1)).astype(bf16)
    kept[0] = half[...]
    for b in range(NB):
        regroup(kept.at[1], b, tn(wil[b], block(half, b)).astype(bf16))
    for g in range(NB):
        projected = tn(wir[g], block(kept.at[1], g))
        rows = slice(g * BS, (g + 1) * BS)
        for part in range(3):
            kept[2 + part, rows, :] = projected[part * BS : (part + 1) * BS, :].astype(bf16)
        source = (projected[:BS] * projected[2 * BS :] * valid).astype(bf16)
        half[rows, :] = source
    for s in range(TILE // LEN):
        lanes = slice(s * LEN, (s + 1) * LEN)
        wave = nn(half[:, lanes], fwd[...])
        wc, ws = wave[:, :LEN], wave[:, LEN:]
        hc, hs = spec[:, :LEN], spec[:, LEN:]
        product = jnp.concatenate(
            [(wc * hc - ws * hs).astype(bf16), (wc * hs + ws * hc).astype(bf16)], axis=1
        )
        conv[:, lanes] = nn(product, inv[...])
    inner = conv[...] + column(cols, 3) * half[...].astype(f32)
    kept[5] = inner.astype(bf16)
    half[...] = (kept[3].astype(f32) * inner).astype(bf16)
    for b in range(NB):
        regroup(kept.at[6], b, tn(wol[b], block(half, b)).astype(bf16))
    for g in range(NB):
        rows = slice(g * BS, (g + 1) * BS)
        middle[rows, :] = enter[rows, :] + tn(wor[g], block(kept.at[6], g))


def mixer_forward(chunk, chunks, scalars, own, oth, marks, cols, spec, fwd, inv, weights):
    row_count = own.shape[0] // 2
    per = row_count // chunks
    steps = per // TILE
    whole_steps = row_count // TILE
    first = chunk == 0
    offset = chunk * steps
    ins = (own, oth, marks, cols, spec, fwd, inv) + tuple(weights)
    lane_block = pl.BlockSpec((8, TILE), lambda i, s: (0, offset + i))
    in_specs = [
        pl.BlockSpec((TILE, HALF), lambda i, s: (s[0] * whole_steps + offset + i, 0)),
        pl.BlockSpec((TILE, HALF), lambda i, s: (i, 0)),
        lane_block,
    ] + [whole(item.shape) for item in ins[3:]]
    outs = [
        jax.ShapeDtypeStruct((D, per), f32),
        jax.ShapeDtypeStruct((7, D, per), bf16),
        jax.ShapeDtypeStruct((8, per), f32),
    ]
    out_specs = [
        pl.BlockSpec((D, TILE), lambda i, s: (0, i)),
        pl.BlockSpec((7, D, TILE), lambda i, s: (0, 0, i)),
        pl.BlockSpec((8, TILE), lambda i, s: (0, i)),
    ]
    if first:
        full = [(NB, BS, BS), (NB, BS, 3 * BS), (NB, BS, BS), (NB, BS, BS)]
        outs += [jax.ShapeDtypeStruct(shape, bf16) for shape in full]
        out_specs += [whole(shape) for shape in full]
    return pl.pallas_call(
        functools.partial(mixer_forward_kernel, first=first),
        out_shape=tuple(outs),
        grid_spec=pltpu.PrefetchScalarGridSpec(
            num_scalar_prefetch=1,
            grid=(steps,),
            in_specs=in_specs,
            out_specs=tuple(out_specs),
            scratch_shapes=[
                pltpu.VMEM((D, TILE), f32),
                pltpu.VMEM((D, TILE), bf16),
                pltpu.VMEM((D, TILE), bf16),
                pltpu.VMEM((D, TILE), f32),
            ],
        ),
        compiler_params=pltpu.CompilerParams(vmem_limit_bytes=VMEM),
        name="mixer_forward",
        cost_estimate=pl.CostEstimate(
            flops=per * 2 * 1500000, bytes_accessed=per * 20000, transcendentals=0
        ),
    )(scalars, *ins)


ACC_SHAPES = ((NB, BS, 2 * FB), (NB, FB, BS), (NB, BS, BS), (NB, BS, BS), (D, LEN))


def dense_kernel(
    s_ref,
    middle,
    own,
    oth,
    cols,
    *refs,
    first,
    last,
    steps,
):
    if first:
        ul, ur, dl, dr, p0, p1, p2, p3 = refs[:8]
        refs = refs[8:]
    else:
        prev = refs[:9]
        refs = refs[10:]
    out_own, out_send, grad_middle = refs[:3]
    refs = refs[3:]
    if first:
        wul, wur, wdl, wdr = refs[:4]
        refs = refs[4:]
    else:
        wul, wur, wdl, wdr = prev[:4]
    if last:
        packed, packed_dr = refs[:2]
        refs = refs[2:]
        accs = refs[:5]
        refs = refs[5:]
    else:
        accs = refs[:5]
        refs = refs[5:]
    gur, gdl, gul, gdr, ggain = accs
    top, half, moved3, moved4, hid, act, slope, gated, back, outs = refs
    side = s_ref[0]

    @pl.when(pl.program_id(0) == 0)
    def _():
        if first:
            other = 1 - side
            own_blocks(wul, side, ul)
            own_blocks(wur, side, ur)
            own_blocks(wdl, side, dl)
            own_blocks(wdr, side, dr)
            q = QUARTER
            for p, piece in enumerate((p0, p1, p2, p3)):
                place = jnp.bitwise_xor(s_ref[1], p)
                row = pl.multiple_of(place * q, q)
                for j in range(2):
                    for c in range(4):
                        wur[2 * other + j, pl.ds(row, q), c * HALF : (c + 1) * HALF] = piece[
                            (4 * j + c) * q : (4 * j + c + 1) * q, :
                        ]
                    wdl[2 * other + j, pl.ds(pl.multiple_of(place * BS, BS), BS), :] = piece[
                        8 * q : 12 * q, j * BS : (j + 1) * BS
                    ]
                unpack_narrow(wul, other, row, piece, 12 * q)
                unpack_narrow(wdr, other, row, piece, 13 * q)
            for acc in accs:
                acc[...] = jnp.zeros(acc.shape, f32)
        else:
            for acc, old in zip(accs, prev[4:]):
                acc[...] = old[...]

    gain = column(cols, 2)
    normed, scale_row = norm_stats(middle[...])
    half[...] = (normed * gain).astype(bf16)
    for b in range(NB):
        regroup(moved3, b, tn(wul[b], block(half, b)).astype(bf16))
    for g in range(NB):
        rows = slice(g * FB, (g + 1) * FB)
        both = tn(wur[g], block(moved3, g))
        gate, up = both[:FB], both[FB:]
        chance = 0.5 + 0.5 * lax.erf(gate * 0.7071067811865476)
        density = jnp.exp(gate * gate * -0.5) * 0.3989422804014327
        active = gate * chance
        hid[rows, :] = (active * up).astype(bf16)
        act[rows, :] = active.astype(bf16)
        slope[rows, :] = (up * (chance + gate * density)).astype(bf16)
        regroup(moved4, g, tn(wdl[g], hid[rows, :]).astype(bf16))
    for g in range(NB):
        rows = slice(g * BS, (g + 1) * BS)
        outs[rows, :] = (middle[rows, :] + tn(wdr[g], block(moved4, g))).astype(bf16)
    out_own[...] = outs[rows_of(side, HALF), :].T
    out_send[...] = outs[rows_of(1 - side, HALF), :].T
    place_halves(top, side, own[...].T, oth[...].T)
    for g in range(NB):
        grad = block(top, g)
        regroup(back, g, nn(wdr[g], grad).astype(bf16))
        gdr[g] += nt(block(moved4, g), grad)
    for b in range(NB):
        rows = slice(b * FB, (b + 1) * FB)
        returned = block(back, b)
        grad_hidden = nn(wdl[b], returned)
        gdl[b] += nt(hid[rows, :], returned)
        gated[:FB, :] = (grad_hidden * slope[rows, :].astype(f32)).astype(bf16)
        gated[FB:, :] = (grad_hidden * act[rows, :].astype(f32)).astype(bf16)
        moved = block(moved3, b)
        gur[b] += nt(moved, gated[...])
        regroup(moved4, b, nn(wur[b], gated[...]).astype(bf16))
    grads = []
    for b in range(NB):
        returned = block(moved4, b)
        grads.append(nn(wul[b], returned))
        gul[b] += nt(block(half, b), returned)
    grad_in = jnp.concatenate(grads, axis=0)
    ggain[...] += fold(grad_in * normed)
    grad_middle[...] = top[...].astype(f32) + norm_back(grad_in, normed, scale_row, gain)

    if last:

        @pl.when(pl.program_id(0) == steps - 1)
        def _():
            sums = exact_nt(jnp.ones((16, LEN), f32), ggain[...])
            for y in range(2):
                for j in range(2):
                    lanes = slice(j * BS, (j + 1) * BS)
                    b = 2 * y + j
                    for c in range(4):
                        packed[y, (4 * j + c) * BS : (4 * j + c + 1) * BS, :] = gur[
                            b, :, c * HALF : (c + 1) * HALF
                        ].astype(bf16)
                    packed[y, 8 * BS : 12 * BS, lanes] = gdl[b].astype(bf16)
                    packed[y, 12 * BS : 13 * BS, lanes] = gul[b].astype(bf16)
                    packed_dr[y, :, lanes] = gdr[b].astype(bf16)
                packed[y, 13 * BS : 13 * BS + 16, :] = sums[:, y * HALF : (y + 1) * HALF].astype(
                    bf16
                )
                packed[y, 13 * BS + 16 :, :] = jnp.zeros((FFN_G - 13 * BS - 16, HALF), bf16)


def dense(chunk, chunks, scalars, middle, own, oth, cols, weights, carried, out_buffer):
    row_count = own.shape[0] // 2
    per = row_count // chunks
    steps = per // TILE
    whole_steps = row_count // TILE
    first, last = chunk == 0, chunk == chunks - 1
    offset = chunk * steps

    def own_rows(i, s):
        return (s[0] * whole_steps + offset + i, 0)

    ins = [middle, own, oth, cols]
    in_specs = [
        pl.BlockSpec((D, TILE), lambda i, s: (0, i)),
        pl.BlockSpec((TILE, HALF), own_rows),
        pl.BlockSpec((TILE, HALF), lambda i, s: (i, 0)),
        whole(cols.shape),
    ]
    ins += list(weights)
    in_specs += [whole(item.shape) for item in weights]
    aliases = {}
    if not first:
        ins += list(carried)
        in_specs += [whole(item.shape) for item in carried]
        ins.append(out_buffer)
        in_specs.append(pl.BlockSpec(memory_space=pl.ANY))
        aliases = {len(ins): 0}
    outs = [
        jax.ShapeDtypeStruct((2 * row_count, HALF), bf16),
        jax.ShapeDtypeStruct((per, HALF), bf16),
        jax.ShapeDtypeStruct((D, per), f32),
    ]
    out_specs = [
        pl.BlockSpec((TILE, HALF), own_rows),
        pl.BlockSpec((TILE, HALF), lambda i, s: (i, 0)),
        pl.BlockSpec((D, TILE), lambda i, s: (0, i)),
    ]
    if first:
        full = [(NB, BS, BS), (NB, BS, 2 * FB), (NB, FB, BS), (NB, BS, BS)]
        outs += [jax.ShapeDtypeStruct(shape, bf16) for shape in full]
        out_specs += [whole(shape) for shape in full]
    scratch = []
    if last:
        outs.append(jax.ShapeDtypeStruct((2, FFN_G, HALF), bf16))
        outs.append(jax.ShapeDtypeStruct((2, BS, HALF), bf16))
        out_specs += [whole((2, FFN_G, HALF)), whole((2, BS, HALF))]
        scratch += [pltpu.VMEM(shape, f32) for shape in ACC_SHAPES]
    else:
        outs += [jax.ShapeDtypeStruct(shape, f32) for shape in ACC_SHAPES]
        out_specs += [whole(shape) for shape in ACC_SHAPES]
    scratch += [pltpu.VMEM((D, TILE), bf16) for _ in range(4)]
    scratch += [pltpu.VMEM((NB * FB, TILE), bf16) for _ in range(3)]
    scratch += [pltpu.VMEM((2 * FB, TILE), bf16)]
    scratch += [pltpu.VMEM((D, TILE), bf16) for _ in range(2)]
    return pl.pallas_call(
        functools.partial(dense_kernel, first=first, last=last, steps=steps),
        out_shape=tuple(outs),
        grid_spec=pltpu.PrefetchScalarGridSpec(
            num_scalar_prefetch=1,
            grid=(steps,),
            in_specs=in_specs,
            out_specs=tuple(out_specs),
            scratch_shapes=scratch,
        ),
        input_output_aliases=aliases,
        compiler_params=pltpu.CompilerParams(vmem_limit_bytes=VMEM),
        name="dense",
        cost_estimate=pl.CostEstimate(
            flops=per * 2 * 8000000, bytes_accessed=per * 10000, transcendentals=0
        ),
    )(scalars, *ins)


MIX_SHAPES = (
    (NB, BS, 3 * BS),
    (NB, BS, BS),
    (NB, BS, BS),
    (NB, BS, BS),
    (D, LEN),
    (D, LEN),
    (D, LEN),
    (D, 2 * LEN),
)


def mixer_backward_kernel(
    s_ref,
    grad_middle,
    kept,
    scale,
    marks,
    cols,
    spec,
    fwd,
    inv,
    wil,
    wir,
    wol,
    wor,
    *refs,
    first,
    last,
    steps,
    share,
):
    if not first:
        prev = refs[:8]
        refs = refs[9:]
    if last:
        taps, feats, packed_dr = refs[:3]
        refs = refs[3:]
    out_own, out_send = refs[:2]
    refs = refs[2:]
    if last:
        packed = refs[0]
        refs = refs[1:]
    accs = refs[:8]
    refs = refs[8:]
    gir, gil, gol, gor, gmask, ggain, gskip, gspec = accs
    back, half, conv, inner_grad, proj, total = refs
    side = s_ref[0]

    @pl.when(pl.program_id(0) == 0)
    def _():
        if first:
            for acc in accs:
                acc[...] = jnp.zeros(acc.shape, f32)
        else:
            for acc, old in zip(accs, prev):
                acc[...] = old[...]

    valid = marks[0:1, :]
    masked = marks[1:2, :]
    half[...] = grad_middle[...].astype(bf16)
    for g in range(NB):
        grad = block(half, g)
        regroup(back, g, nn(wor[g], grad).astype(bf16))
        gor[g] += nt(block(kept.at[6], g), grad)
    for b in range(NB):
        rows = slice(b * BS, (b + 1) * BS)
        returned = block(back, b)
        grad_mixed = nn(wol[b], returned)
        gate = kept[3, rows, :].astype(f32)
        inner = kept[5, rows, :].astype(f32)
        gol[b] += nt((gate * inner).astype(bf16), returned)
        grad_inner = grad_mixed * gate
        inner_grad[rows, :] = grad_inner
        conv[rows, :] = grad_inner.astype(bf16)
        proj[b * 3 * BS + BS : b * 3 * BS + 2 * BS, :] = (grad_mixed * inner).astype(bf16)
        source = (
            kept[2, rows, :].astype(f32) * kept[4, rows, :].astype(f32) * valid
        ).astype(bf16)
        half[rows, :] = source
        gskip[rows, :] += fold(grad_inner * source.astype(f32))
    hc, hs = spec[:, :LEN], spec[:, LEN:]
    for s in range(TILE // LEN):
        lanes = slice(s * LEN, (s + 1) * LEN)
        wave = nn(conv[:, lanes], fwd[...])
        wc, ws = wave[:, :LEN], wave[:, LEN:]
        seen = nn(half[:, lanes], fwd[...])
        sc, ss = seen[:, :LEN], seen[:, LEN:]
        gspec[:, :LEN] += wc * sc + ws * ss
        gspec[:, LEN:] += ws * sc - wc * ss
        product = jnp.concatenate(
            [(wc * hc + ws * hs).astype(bf16), (ws * hc - wc * hs).astype(bf16)], axis=1
        )
        total[:, lanes] = nn(product, inv[...])
    for g in range(NB):
        rows = slice(g * BS, (g + 1) * BS)
        grad_source = (total[rows, :] + cols[rows, 3:4] * inner_grad[rows, :]) * valid
        start = g * 3 * BS
        proj[start : start + BS, :] = (grad_source * kept[4, rows, :].astype(f32)).astype(bf16)
        proj[start + 2 * BS : start + 3 * BS, :] = (
            grad_source * kept[2, rows, :].astype(f32)
        ).astype(bf16)
        grad = proj[start : start + 3 * BS, :]
        gir[g] += nt(block(kept.at[1], g), grad)
        regroup(back, g, nn(wir[g], grad).astype(bf16))
    gain = column(cols, 1)
    grads = []
    for b in range(NB):
        returned = block(back, b)
        grads.append(nn(wil[b], returned))
        gil[b] += nt(block(kept.at[0], b), returned)
    grad_in = jnp.concatenate(grads, axis=0)
    normed = kept[0].astype(f32) / gain
    ggain[...] += fold(grad_in * normed)
    entered = grad_middle[...] + norm_back(grad_in, normed, scale[0:1, :], gain)
    gmask[...] += fold(entered * masked)
    total[...] = entered * (1.0 - masked)
    out_own[...] = total[rows_of(side, HALF), :].T
    out_send[...] = total[rows_of(1 - side, HALF), :].T.astype(bf16)

    if last:

        @pl.when(pl.program_id(0) == steps - 1)
        def _():
            spectrum = gspec[...]
            high = spectrum.astype(bf16)
            low = (spectrum - high.astype(f32)).astype(bf16)
            grad_taps = nn(high, inv[...]) + nn(low, inv[...])
            tap = taps[...]
            grad_taps = grad_taps + tap * (2.0 * penalty_weight * share)
            positions = lax.broadcasted_iota(jnp.int32, (1, LEN), 1).astype(f32)
            decayed = grad_taps * jnp.exp(-column(cols, 4) * positions)
            high = decayed.astype(bf16)
            low = (decayed - high.astype(f32)).astype(bf16)
            grad_weight = (
                nt(feats[0], high) + nt(feats[1], high) + nt(feats[0], low)
            )
            grad_decay = grad_taps * tap * (-positions)
            ones = jnp.ones((16, LEN), f32)
            line = lax.broadcasted_iota(jnp.int32, (16, D), 0)
            vectors = jnp.zeros((16, D), f32)
            for index, item in enumerate((gmask[...], ggain[...], gskip[...], grad_decay)):
                vectors = jnp.where(line == index, exact_nt(ones, item), vectors)
            for y in range(2):
                lanes = slice(y * HALF, (y + 1) * HALF)
                a, b = 2 * y, 2 * y + 1
                packed[y, 0:BS, :] = gir[a, :, 0:HALF].astype(bf16)
                packed[y, BS : 2 * BS, 0:BS] = gir[a, :, HALF:].astype(bf16)
                packed[y, BS : 2 * BS, BS:HALF] = gir[b, :, 0:BS].astype(bf16)
                packed[y, 2 * BS : 3 * BS, :] = gir[b, :, BS:].astype(bf16)
                for slab, acc in ((3, gil), (4, gol), (5, gor)):
                    at = slice(slab * BS, (slab + 1) * BS)
                    packed[y, at, 0:BS] = acc[a].astype(bf16)
                    packed[y, at, BS:HALF] = acc[b].astype(bf16)
                packed[y, 6 * BS : 6 * BS + ORDER, :] = grad_weight[:, lanes].astype(bf16)
                at = 6 * BS + ORDER
                packed[y, at : at + 16, :] = vectors[:, lanes].astype(bf16)
                packed[y, at + 16 : at + 16 + BS, :] = packed_dr[y]
                packed[y, at + 16 + BS :, :] = jnp.zeros((MIX_G - at - 16 - BS, HALF), bf16)


def mixer_backward(
    chunk,
    chunks,
    share,
    scalars,
    row_count,
    streams,
    constants,
    weights,
    carried,
    buffer,
    finals,
):
    per = row_count // chunks
    steps = per // TILE
    whole_steps = row_count // TILE
    first, last = chunk == 0, chunk == chunks - 1
    offset = chunk * steps
    ins = list(streams) + list(constants) + list(weights)
    in_specs = [
        pl.BlockSpec((D, TILE), lambda i, s: (0, i)),
        pl.BlockSpec((7, D, TILE), lambda i, s: (0, 0, i)),
        pl.BlockSpec((8, TILE), lambda i, s: (0, i)),
        pl.BlockSpec((8, TILE), lambda i, s: (0, offset + i)),
    ]
    in_specs += [whole(item.shape) for item in ins[4:]]
    aliases = {}
    if not first:
        ins += list(carried)
        in_specs += [whole(item.shape) for item in carried]
        ins.append(buffer)
        in_specs.append(pl.BlockSpec(memory_space=pl.ANY))
        aliases = {len(ins): 0}
    if last:
        ins += list(finals)
        in_specs += [whole(item.shape) for item in finals]
    outs = [
        jax.ShapeDtypeStruct((2 * row_count, HALF), f32),
        jax.ShapeDtypeStruct((per, HALF), bf16),
    ]
    out_specs = [
        pl.BlockSpec((TILE, HALF), lambda i, s: (s[0] * whole_steps + offset + i, 0)),
        pl.BlockSpec((TILE, HALF), lambda i, s: (i, 0)),
    ]
    scratch = []
    if last:
        outs.append(jax.ShapeDtypeStruct((2, MIX_G, HALF), bf16))
        out_specs.append(whole((2, MIX_G, HALF)))
        scratch += [pltpu.VMEM(shape, f32) for shape in MIX_SHAPES]
    else:
        outs += [jax.ShapeDtypeStruct(shape, f32) for shape in MIX_SHAPES]
        out_specs += [whole(shape) for shape in MIX_SHAPES]
    scratch += [
        pltpu.VMEM((D, TILE), bf16),
        pltpu.VMEM((D, TILE), bf16),
        pltpu.VMEM((D, TILE), bf16),
        pltpu.VMEM((D, TILE), f32),
        pltpu.VMEM((3 * D, TILE), bf16),
        pltpu.VMEM((D, TILE), f32),
    ]
    return pl.pallas_call(
        functools.partial(
            mixer_backward_kernel, first=first, last=last, steps=steps, share=share
        ),
        out_shape=tuple(outs),
        grid_spec=pltpu.PrefetchScalarGridSpec(
            num_scalar_prefetch=1,
            grid=(steps,),
            in_specs=in_specs,
            out_specs=tuple(out_specs),
            scratch_shapes=scratch,
        ),
        input_output_aliases=aliases,
        compiler_params=pltpu.CompilerParams(vmem_limit_bytes=VMEM),
        name="mixer_backward",
        cost_estimate=pl.CostEstimate(
            flops=per * 2 * 3000000, bytes_accessed=per * 20000, transcendentals=0
        ),
    )(scalars, *ins)


def dense_unpack_kernel(src, gain, ul, ur, dl):
    gain[...] = src[13 * BS : 13 * BS + 16, :].astype(f32)
    for j in range(2):
        lanes = slice(j * BS, (j + 1) * BS)
        for c in range(4):
            ur[j, :, c * HALF : (c + 1) * HALF] = src[
                (4 * j + c) * BS : (4 * j + c + 1) * BS, :
            ].astype(f32)
        dl[j] = src[8 * BS : 12 * BS, lanes].astype(f32)
        ul[j] = src[12 * BS : 13 * BS, lanes].astype(f32)


def dense_unpack(summed):
    return pl.pallas_call(
        dense_unpack_kernel,
        out_shape=(
            jax.ShapeDtypeStruct((16, HALF), f32),
            jax.ShapeDtypeStruct((2, BS, BS), f32),
            jax.ShapeDtypeStruct((2, BS, 2 * FB), f32),
            jax.ShapeDtypeStruct((2, FB, BS), f32),
        ),
        compiler_params=pltpu.CompilerParams(vmem_limit_bytes=VMEM),
        name="dense_unpack",
    )(summed)


def mixer_unpack_kernel(src, vectors, weight, il, ir, ol, orr, dr):
    at = 6 * BS + ORDER
    weight[...] = src[6 * BS : at, :].astype(f32)
    vectors[...] = src[at : at + 16, :].astype(f32)
    ir[0, :, 0:HALF] = src[0:BS, :].astype(f32)
    ir[0, :, HALF:] = src[BS : 2 * BS, 0:BS].astype(f32)
    ir[1, :, 0:BS] = src[BS : 2 * BS, BS:HALF].astype(f32)
    ir[1, :, BS:] = src[2 * BS : 3 * BS, :].astype(f32)
    for start, dst in ((3 * BS, il), (4 * BS, ol), (5 * BS, orr), (at + 16, dr)):
        for j in range(2):
            dst[j] = src[start : start + BS, j * BS : (j + 1) * BS].astype(f32)


def mixer_unpack(summed):
    square = jax.ShapeDtypeStruct((2, BS, BS), f32)
    return pl.pallas_call(
        mixer_unpack_kernel,
        out_shape=(
            jax.ShapeDtypeStruct((16, HALF), f32),
            jax.ShapeDtypeStruct((ORDER, HALF), f32),
            square,
            jax.ShapeDtypeStruct((2, BS, 3 * BS), f32),
            square,
            square,
            square,
        ),
        compiler_params=pltpu.CompilerParams(vmem_limit_bytes=VMEM),
        name="mixer_unpack",
    )(summed)


def swap_narrow(values):
    return lax.ppermute(values, "narrow", [(0, 1), (1, 0)])


def swap_wide(values, bit, size):
    return lax.ppermute(values, "wide", [(i, i ^ (1 << bit)) for i in range(size)])


def take_half(values, which, axis):
    half = values.shape[axis] // 2
    return lax.dynamic_slice_in_dim(values, which * half, half, axis)


def add_low(a, b):
    return (a.astype(f32) + b.astype(f32)).astype(bf16)


def sum_gradients(packed, index, side, size, order):
    bits = [(index >> bit) & 1 for bit in range(size.bit_length() - 1)]
    extra = [bit for bit in range(len(bits)) if bit not in order]
    for bit in order:
        keep = take_half(packed, bits[bit], 1)
        sent = take_half(packed, 1 - bits[bit], 1)
        packed = add_low(keep, swap_wide(sent, bit, size))
    sent = take_half(packed, 1 - side, 0)
    packed = add_low(take_half(packed, side, 0), swap_narrow(sent))[0]
    for bit in extra:
        packed = add_low(packed, swap_wide(packed, bit, size))
    for bit in reversed(order):
        other = swap_wide(packed, bit, size)
        packed = jnp.where(
            bits[bit] == 0,
            jnp.concatenate([packed, other], axis=0),
            jnp.concatenate([other, packed], axis=0),
        )
    return packed


def gather_quarters(piece, size):
    first = swap_narrow(piece)
    second = swap_wide(first, 1, size)
    return (first, swap_wide(first, 0, size), second, swap_wide(second, 0, size))


def on_device(
    wide_size,
    tokens,
    lengths,
    mask_pos,
    mask_vector,
    norm1_gain,
    in_left,
    in_right,
    filter_weight,
    decay,
    skip_gain,
    out_left,
    out_right,
    norm2_gain,
    up_left,
    up_right,
    down_left,
    down_right,
    cotangent,
):
    index = lax.axis_index("wide")
    side = lax.axis_index("narrow")
    row_count = tokens.shape[0] // 2
    per = row_count // CHUNKS
    scalars = jnp.stack([side, index & 3]).astype(jnp.int32)
    share = 1.0 / (2 * wide_size)

    def sent_rows(values, chunk):
        return lax.dynamic_slice_in_dim(
            values, (1 - side) * row_count + chunk * per, per, 0
        )

    mixer_weights = (in_left, in_right, out_left, out_right)
    dense_weights = (up_left, up_right, down_left, down_right)
    mix_piece, ffn_piece = pack_weights(scalars[1:], mixer_weights + dense_weights)

    own_vectors = jnp.stack(
        [
            item.astype(f32)
            for item in (mask_vector, norm1_gain, norm2_gain, skip_gain, decay, decay, decay, decay)
        ]
    )
    other_vectors = swap_narrow(own_vectors)
    other_filter = swap_narrow(filter_weight)
    mix_pieces = gather_quarters(mix_piece, wide_size)
    tokens_other = []
    cot_other = []
    for chunk in range(CHUNKS):
        tokens_other.append(swap_narrow(sent_rows(tokens, chunk)))
        if chunk == 0:
            ffn_pieces = gather_quarters(ffn_piece, wide_size)
        cot_other.append(swap_narrow(sent_rows(cotangent, chunk)))

    cols = jnp.where(
        side == 0,
        jnp.concatenate([own_vectors, other_vectors], axis=1),
        jnp.concatenate([other_vectors, own_vectors], axis=1),
    ).T
    positions = jnp.arange(LEN, dtype=jnp.int32)
    valid = (positions[None, :] < lengths[:, None]).astype(f32)
    masked = jnp.any(mask_pos[:, :, None] == positions[None, None, :], axis=1).astype(f32)
    marks = jnp.stack([valid, masked]).reshape(2, 2, row_count)
    marks = lax.dynamic_index_in_dim(marks, side, 1, keepdims=False)
    marks = jnp.concatenate([marks, jnp.zeros((6, row_count), f32)], axis=0)

    fwd, inv = (jnp.asarray(item) for item in transform_tables())
    feats = jnp.asarray(feature_parts())
    taps, spec, penalty = filter_call(scalars, filter_weight, other_filter, cols, feats, fwd)

    kept = []
    scales = []
    grads_middle = []
    out_sends = []
    carried = None
    full_mixer = None
    full_dense = None
    output = None
    for chunk in range(CHUNKS):
        weights = mixer_weights + mix_pieces if chunk == 0 else full_mixer
        results = mixer_forward(
            chunk,
            CHUNKS,
            scalars,
            tokens,
            tokens_other[chunk],
            marks,
            cols,
            spec,
            fwd,
            inv,
            weights,
        )
        middle = results[0]
        kept.append(results[1])
        scales.append(results[2])
        if chunk == 0:
            full_mixer = results[3:]
        weights = dense_weights + ffn_pieces if chunk == 0 else full_dense
        results = dense(
            chunk,
            CHUNKS,
            scalars,
            middle,
            cotangent,
            cot_other[chunk],
            cols,
            weights,
            carried,
            output,
        )
        output = results[0]
        out_sends.append(swap_narrow(results[1]))
        grads_middle.append(results[2])
        rest = results[3:]
        if chunk == 0:
            full_dense = rest[:4]
            rest = rest[4:]
        carried = rest
    ffn_packed, dr_packed = carried

    carried = None
    tokens_grad = None
    grad_sends = []
    for chunk in range(CHUNKS):
        results = mixer_backward(
            chunk,
            CHUNKS,
            share,
            scalars,
            row_count,
            (grads_middle[chunk], kept[chunk], scales[chunk], marks),
            (cols, spec, fwd, inv),
            full_mixer,
            carried,
            tokens_grad,
            (taps, feats, dr_packed),
        )
        tokens_grad = results[0]
        grad_sends.append(swap_narrow(results[1]))
        carried = results[2:]
    (mix_packed,) = carried

    order = [1, 0] if wide_size < 16 else [0, 1, 2, 3]
    ffn_summed = sum_gradients(ffn_packed, index, side, wide_size, order)
    mix_summed = sum_gradients(mix_packed, index, side, wide_size, order)
    gain_two, g_ul, g_ur, g_dl = dense_unpack(ffn_summed)
    vectors, g_filter, g_il, g_ir, g_ol, g_or, g_dr = mixer_unpack(mix_summed)

    for chunk in range(CHUNKS):
        start = (1 - side) * row_count + chunk * per
        output = lax.dynamic_update_slice_in_dim(output, out_sends[chunk], start, 0)
        tokens_grad = lax.dynamic_update_slice_in_dim(
            tokens_grad, grad_sends[chunk].astype(f32), start, 0
        )
    return (
        output,
        tokens_grad,
        vectors[0],
        vectors[1],
        g_il,
        g_ir,
        g_filter,
        vectors[3],
        vectors[2],
        g_ol,
        g_or,
        gain_two[0],
        g_ul,
        g_ur,
        g_dl,
        g_dr,
        penalty[0, 0],
    )


def solution(mesh):
    placed = (
        P("wide", "narrow"),
        P("wide"),
        P("wide", None),
        P("narrow"),
        P("narrow"),
        P("narrow", None, None),
        P("narrow", None, None),
        P(None, "narrow"),
        P("narrow"),
        P("narrow"),
        P("narrow", None, None),
        P("narrow", None, None),
        P("narrow"),
        P("narrow", None, None),
        P("narrow", None, None),
        P("narrow", None, None),
        P("narrow", None, None),
        P("wide", "narrow"),
    )
    return jax.shard_map(
        functools.partial(on_device, mesh.shape["wide"]),
        mesh=mesh,
        in_specs=placed,
        out_specs=(
            P("wide", "narrow"),
            P("wide", "narrow"),
            P("narrow"),
            P("narrow"),
            P("narrow", None, None),
            P("narrow", None, None),
            P(None, "narrow"),
            P("narrow"),
            P("narrow"),
            P("narrow", None, None),
            P("narrow", None, None),
            P("narrow"),
            P("narrow", None, None),
            P("narrow", None, None),
            P("narrow", None, None),
            P("narrow", None, None),
            P(),
        ),
        check_vma=False,
    )
```

```python
import functools

import jax
import jax.numpy as jnp
import numpy as np
from jax import lax
from jax.experimental import pallas as pl
from jax.experimental.pallas import tpu as pltpu
from jax.sharding import PartitionSpec as P

D = 768
NB = 4
ORDER = 128
LEN = 128
BS = 192
FB = 768
GROUP = BS // NB
HALF = D // 2
QUARTER = BS // 4

epsilon = 1e-05
penalty_weight = 0.005

bf16 = jnp.bfloat16
f32 = jnp.float32

TILE = 512
BACK_TILE = 256
VMEM = 60 << 20

FILTER_ROW = 6 * QUARTER
VECTOR_ROW = FILTER_ROW + ORDER // 4
MIX_W = VECTOR_ROW + 16
FFN_W = 7 * QUARTER
FFN_G = 1280
MIX_G = 768


def transform_tables():
    t = np.arange(LEN, dtype=np.float64)[:, None]
    k = np.arange(LEN, dtype=np.float64)[None, :]
    angle = np.pi * (2 * k + 1) * t / (2 * LEN)
    forward = np.concatenate([np.cos(angle), np.sin(angle)], axis=1)
    return forward.astype(bf16), (forward.T / LEN).astype(bf16)


def feature_parts():
    t = np.arange(LEN, dtype=np.float64)[None, :]
    freqs = (np.arange(ORDER // 2, dtype=np.float64)[:, None] + 1.0) * (3.1 / (ORDER // 2))
    table = np.concatenate([np.sin(t * freqs), np.cos(t * freqs)], axis=0)
    parts = []
    for _ in range(3):
        part = table.astype(bf16)
        parts.append(part)
        table = table - part.astype(np.float64)
    return np.stack(parts)


def nn(a, b):
    return lax.dot_general(a, b, (((1,), (0,)), ((), ())), preferred_element_type=f32)


def nt(a, b):
    return lax.dot_general(a, b, (((1,), (1,)), ((), ())), preferred_element_type=f32)


def tn(a, b):
    return lax.dot_general(a, b, (((0,), (0,)), ((), ())), preferred_element_type=f32)


def exact_nt(a, b):
    return lax.dot_general(
        a,
        b,
        (((1,), (1,)), ((), ())),
        preferred_element_type=f32,
        precision=lax.Precision.HIGHEST,
    )


def fold(values):
    out = values[:, :LEN]
    for start in range(LEN, values.shape[1], LEN):
        out = out + values[:, start : start + LEN]
    return out


def rows_of(block, size):
    return pl.ds(pl.multiple_of(block * size, size), size)


def column(cols_ref, index):
    return cols_ref[:, index : index + 1]


def place_halves(dst_ref, side, own, other):
    dst_ref[rows_of(side, HALF), :] = own
    dst_ref[rows_of(1 - side, HALF), :] = other


def regroup(dst_ref, block, values):
    for g in range(NB):
        dst_ref[g * BS + block * GROUP : g * BS + (block + 1) * GROUP, :] = values[
            g * GROUP : (g + 1) * GROUP, :
        ]


def block(ref, index, size=BS):
    return ref[index * size : (index + 1) * size, :]


def norm_stats(values):
    center = values - jnp.sum(values, axis=0, keepdims=True) * (1.0 / D)
    spread = jnp.sum(center * center, axis=0, keepdims=True) * (1.0 / D)
    scale_row = lax.rsqrt(spread + epsilon)
    return center * scale_row, scale_row


def norm_back(grad, normed, scale_row, gain):
    scaled = grad * gain
    first = jnp.sum(scaled, axis=0, keepdims=True) * (1.0 / D)
    second = jnp.sum(scaled * normed, axis=0, keepdims=True) * (1.0 / D)
    return scale_row * (scaled - first - normed * second)


def pack_kernel(
    s_ref, il, ir, ol, orr, ul, ur, dl, dr, weight, mask, gain1, gain2, skip, decay, mix_ref, ffn_ref
):
    def pairs(ref):
        return jnp.concatenate([ref[0], ref[1]], axis=1)

    q = QUARTER
    mix_ref[0:q, :] = pairs(il)
    wide_in = pairs(ir)
    for c in range(3):
        mix_ref[(1 + c) * q : (2 + c) * q, :] = wide_in[:, c * HALF : (c + 1) * HALF]
    mix_ref[4 * q : 5 * q, :] = pairs(ol)
    mix_ref[5 * q : 6 * q, :] = pairs(orr)
    mix_ref[FILTER_ROW:VECTOR_ROW, :] = weight[...]
    rest = decay[...].reshape(1, HALF)
    rows = [item[...].reshape(1, HALF).astype(f32) for item in (mask, gain1, gain2, skip)]
    for _ in range(3):
        part = rest.astype(bf16).astype(f32)
        rows.append(part)
        rest = rest - part
    line = lax.broadcasted_iota(jnp.int32, (16, HALF), 0)
    vectors = jnp.zeros((16, HALF), f32)
    for index, row in enumerate(rows):
        vectors = jnp.where(line == index, row, vectors)
    mix_ref[VECTOR_ROW:, :] = vectors.astype(bf16)
    for c in range(4):
        ffn_ref[c * q : (c + 1) * q, :] = ur[0][:, c * HALF : (c + 1) * HALF]
    for c in range(2):
        ffn_ref[(4 + c) * q : (5 + c) * q, :] = dl[0][:, c * HALF : (c + 1) * HALF]
    ffn_ref[6 * q : 7 * q, :] = jnp.concatenate([ul[0], dr[0]], axis=1)


def pack_weights(scalars, mixer_weights, dense_weights, filter_weight, vectors):
    def quarter(item):
        return pl.BlockSpec((2, QUARTER, item.shape[2]), lambda i, s: (0, s[1], 0))

    def eighth(item):
        return pl.BlockSpec((1, QUARTER, item.shape[2]), lambda i, s: (s[2], s[1], 0))

    return pl.pallas_call(
        pack_kernel,
        out_shape=(
            jax.ShapeDtypeStruct((MIX_W, HALF), bf16),
            jax.ShapeDtypeStruct((FFN_W, HALF), bf16),
        ),
        grid_spec=pltpu.PrefetchScalarGridSpec(
            num_scalar_prefetch=1,
            grid=(1,),
            in_specs=[quarter(item) for item in mixer_weights]
            + [eighth(item) for item in dense_weights]
            + [pl.BlockSpec((ORDER // 4, HALF), lambda i, s: (s[1], 0))]
            + [whole(item.shape) for item in vectors],
            out_specs=(whole((MIX_W, HALF)), whole((FFN_W, HALF))),
        ),
        name="pack_weights",
    )(scalars, *mixer_weights, *dense_weights, filter_weight, *vectors)


def unpack_narrow(dst, other, row, piece, base):
    for j in range(2):
        dst[2 * other + j, pl.ds(row, QUARTER), :] = piece[
            base : base + QUARTER, j * BS : (j + 1) * BS
        ]


def own_blocks(dst, side, src):
    for j in range(2):
        dst[2 * side + j] = src[j]


def filter_kernel(
    s_ref, own, mine, p0, p1, p2, p3, feats, fwd, taps_ref, spec_ref, pen_ref, cols_ref, weight
):
    side = s_ref[0]
    q = ORDER // 4
    for p, piece in enumerate((p0, p1, p2, p3)):
        row = pl.multiple_of(jnp.bitwise_xor(s_ref[1], p) * q, q)
        weight[pl.ds(row, q), :] = piece[FILTER_ROW:VECTOR_ROW, :]
    for which, src, rows in ((side, own, mine), (1 - side, weight, p0)):
        table = src[...]
        basis = tn(table, feats[2]) + tn(table, feats[1]) + tn(table, feats[0])
        taps_ref[rows_of(which, HALF), :] = basis
        vectors = rows[VECTOR_ROW:, :].astype(f32)
        vectors = jnp.concatenate([vectors, jnp.zeros((LEN - 16, HALF), f32)], axis=0)
        vectors = vectors.T
        lane = lax.broadcasted_iota(jnp.int32, (HALF, LEN), 1)
        decay = vectors[:, 4:5] + vectors[:, 5:6] + vectors[:, 6:7]
        cols_ref[rows_of(which, HALF), :] = jnp.where(lane == 4, decay, vectors)
    positions = lax.broadcasted_iota(jnp.int32, (1, LEN), 1).astype(f32)
    taps = taps_ref[...] * jnp.exp(-column(cols_ref, 4) * positions)
    taps_ref[...] = taps
    spec_ref[...] = nn(taps.astype(bf16), fwd[...])
    total = jnp.sum(jnp.sum(taps * taps, axis=0, keepdims=True), axis=1, keepdims=True)
    pen_ref[...] = jnp.broadcast_to(total * penalty_weight, (8, LEN))


def whole(shape):
    return pl.BlockSpec(shape, lambda *_: (0,) * len(shape))


def filter_call(scalars, own, mine, pieces, feats, fwd):
    ins = (own, mine) + tuple(pieces) + (feats, fwd)
    outs = (
        jax.ShapeDtypeStruct((D, LEN), f32),
        jax.ShapeDtypeStruct((D, 2 * LEN), f32),
        jax.ShapeDtypeStruct((8, LEN), f32),
        jax.ShapeDtypeStruct((D, LEN), f32),
    )
    return pl.pallas_call(
        filter_kernel,
        out_shape=outs,
        grid_spec=pltpu.PrefetchScalarGridSpec(
            num_scalar_prefetch=1,
            grid=(1,),
            in_specs=[whole(item.shape) for item in ins],
            out_specs=tuple(whole(item.shape) for item in outs),
            scratch_shapes=[pltpu.VMEM((ORDER, HALF), bf16)],
        ),
        name="filter_spectrum",
    )(scalars, *ins)


def mixer_forward_kernel(
    s_ref,
    own,
    oth,
    marks,
    cols,
    spec,
    fwd,
    inv,
    il,
    ir,
    ol,
    orr,
    p0,
    p1,
    p2,
    p3,
    middle,
    first,
    kept,
    scale,
    wil,
    wir,
    wol,
    wor,
    enter,
    half,
    conv,
):
    side = s_ref[0]

    @pl.when(pl.program_id(0) == 0)
    def _():
        other = 1 - side
        own_blocks(wil, side, il)
        own_blocks(wir, side, ir)
        own_blocks(wol, side, ol)
        own_blocks(wor, side, orr)
        q = QUARTER
        for p, piece in enumerate((p0, p1, p2, p3)):
            row = pl.multiple_of(jnp.bitwise_xor(s_ref[1], p) * q, q)
            unpack_narrow(wil, other, row, piece, 0)
            at = pl.ds(row, q)
            wir[2 * other, at, 0:HALF] = piece[q : 2 * q, :]
            wir[2 * other, at, HALF : 3 * BS] = piece[2 * q : 3 * q, 0:BS]
            wir[2 * other + 1, at, 0:BS] = piece[2 * q : 3 * q, BS:HALF]
            wir[2 * other + 1, at, BS : 3 * BS] = piece[3 * q : 4 * q, :]
            unpack_narrow(wol, other, row, piece, 4 * q)
            unpack_narrow(wor, other, row, piece, 5 * q)

    place_halves(enter, side, own[...].T.astype(f32), oth[...].T.astype(f32))
    valid = marks[0:1, :]
    masked = marks[1:2, :]
    tokens = enter[...]
    entered = tokens + masked * (column(cols, 0) - tokens)
    enter[...] = entered
    normed, scale_row = norm_stats(entered)
    scale[...] = jnp.broadcast_to(scale_row, scale.shape)
    half[...] = (normed * column(cols, 1)).astype(bf16)
    first[0] = half[...]
    for b in range(NB):
        regroup(first.at[1], b, tn(wil[b], block(half, b)).astype(bf16))
    for g in range(NB):
        projected = tn(wir[g], block(first.at[1], g))
        rows = slice(g * BS, (g + 1) * BS)
        for part in range(3):
            kept[part, rows, :] = projected[part * BS : (part + 1) * BS, :].astype(bf16)
        source = (projected[:BS] * projected[2 * BS :] * valid).astype(bf16)
        half[rows, :] = source
    for s in range(TILE // LEN):
        lanes = slice(s * LEN, (s + 1) * LEN)
        wave = nn(half[:, lanes], fwd[...])
        wc, ws = wave[:, :LEN], wave[:, LEN:]
        hc, hs = spec[:, :LEN], spec[:, LEN:]
        product = jnp.concatenate(
            [(wc * hc - ws * hs).astype(bf16), (wc * hs + ws * hc).astype(bf16)], axis=1
        )
        conv[:, lanes] = nn(product, inv[...])
    inner = conv[...] + column(cols, 3) * half[...].astype(f32)
    kept[3] = inner.astype(bf16)
    half[...] = (kept[1].astype(f32) * inner).astype(bf16)
    for b in range(NB):
        regroup(kept.at[4], b, tn(wol[b], block(half, b)).astype(bf16))
    for g in range(NB):
        rows = slice(g * BS, (g + 1) * BS)
        middle[rows, :] = enter[rows, :] + tn(wor[g], block(kept.at[4], g))


def mixer_forward(scalars, own, oth, marks, cols, spec, fwd, inv, weights):
    row_count = own.shape[0] // 2
    steps = row_count // TILE
    ins = (own, oth, marks, cols, spec, fwd, inv) + tuple(weights)
    in_specs = [
        pl.BlockSpec((TILE, HALF), lambda i, s: (s[0] * steps + i, 0)),
        pl.BlockSpec((TILE, HALF), lambda i, s: (i, 0)),
        pl.BlockSpec((8, TILE), lambda i, s: (0, i)),
    ] + [whole(item.shape) for item in ins[3:]]
    full = [(NB, BS, BS), (NB, BS, 3 * BS), (NB, BS, BS), (NB, BS, BS)]
    outs = [
        jax.ShapeDtypeStruct((D, row_count), f32),
        jax.ShapeDtypeStruct((2, D, row_count), bf16),
        jax.ShapeDtypeStruct((5, D, row_count), bf16),
        jax.ShapeDtypeStruct((8, row_count), f32),
    ] + [jax.ShapeDtypeStruct(shape, bf16) for shape in full]
    out_specs = [
        pl.BlockSpec((D, TILE), lambda i, s: (0, i)),
        pl.BlockSpec((2, D, TILE), lambda i, s: (0, 0, i)),
        pl.BlockSpec((5, D, TILE), lambda i, s: (0, 0, i)),
        pl.BlockSpec((8, TILE), lambda i, s: (0, i)),
    ] + [whole(shape) for shape in full]
    return pl.pallas_call(
        mixer_forward_kernel,
        out_shape=tuple(outs),
        grid_spec=pltpu.PrefetchScalarGridSpec(
            num_scalar_prefetch=1,
            grid=(steps,),
            in_specs=in_specs,
            out_specs=tuple(out_specs),
            scratch_shapes=[
                pltpu.VMEM((D, TILE), f32),
                pltpu.VMEM((D, TILE), bf16),
                pltpu.VMEM((D, TILE), f32),
            ],
        ),
        compiler_params=pltpu.CompilerParams(vmem_limit_bytes=VMEM),
        name="mixer_forward",
        cost_estimate=pl.CostEstimate(
            flops=row_count * 2 * 1500000, bytes_accessed=row_count * 20000, transcendentals=0
        ),
    )(scalars, *ins)


ACC_SHAPES = ((NB, BS, 2 * FB), (NB, BS, FB), (NB, BS, BS), (NB, BS, BS), (D, LEN))


def dense_kernel(
    s_ref,
    middle,
    own,
    oth,
    cols,
    ul,
    ur,
    dl,
    dr,
    p0,
    p1,
    p2,
    p3,
    p4,
    p5,
    p6,
    p7,
    out_own,
    out_send,
    grad_middle,
    keep,
    send,
    packed_dr,
    wul,
    wur,
    wdl,
    wdr,
    gur,
    gdl,
    gul,
    gdr,
    ggain,
    top,
    half,
    moved3,
    moved4,
    hid,
    act,
    slope,
    gated,
    back,
    outs,
    *,
    steps,
):
    side = s_ref[0]

    @pl.when(pl.program_id(0) == 0)
    def _():
        other = 1 - side
        own_blocks(wul, side, ul)
        own_blocks(wur, side, ur)
        own_blocks(wdl, side, dl)
        own_blocks(wdr, side, dr)
        q = QUARTER
        for p, piece in enumerate((p0, p1, p2, p3, p4, p5, p6, p7)):
            row = pl.multiple_of(jnp.bitwise_xor(s_ref[1], p & 3) * q, q)
            at = pl.ds(row, q)
            blk = 2 * other + jnp.bitwise_xor(s_ref[2], p >> 2)
            for c in range(4):
                wur[blk, at, c * HALF : (c + 1) * HALF] = piece[c * q : (c + 1) * q, :]
            for c in range(2):
                wdl[blk, at, c * HALF : (c + 1) * HALF] = piece[(4 + c) * q : (5 + c) * q, :]
            wul[blk, at, :] = piece[6 * q : 7 * q, :BS]
            wdr[blk, at, :] = piece[6 * q : 7 * q, BS:]
        for acc in (gur, gdl, gul, gdr, ggain):
            acc[...] = jnp.zeros(acc.shape, f32)

    gain = column(cols, 2)
    normed, scale_row = norm_stats(middle[...])
    half[...] = (normed * gain).astype(bf16)
    for b in range(NB):
        regroup(moved3, b, tn(wul[b], block(half, b)).astype(bf16))
    for g in range(NB):
        rows = slice(g * FB, (g + 1) * FB)
        both = tn(wur[g], block(moved3, g))
        gate, up = both[:FB], both[FB:]
        chance = 0.5 + 0.5 * lax.erf(gate * 0.7071067811865476)
        density = jnp.exp(gate * gate * -0.5) * 0.3989422804014327
        active = gate * chance
        hid[rows, :] = (active * up).astype(bf16)
        act[rows, :] = active.astype(bf16)
        slope[rows, :] = (up * (chance + gate * density)).astype(bf16)
        regroup(moved4, g, nn(wdl[g], hid[rows, :]).astype(bf16))
    for g in range(NB):
        rows = slice(g * BS, (g + 1) * BS)
        outs[rows, :] = (middle[rows, :] + tn(wdr[g], block(moved4, g))).astype(bf16)
    out_own[...] = outs[rows_of(side, HALF), :].T
    out_send[...] = outs[rows_of(1 - side, HALF), :].T
    place_halves(top, side, own[...].T, oth[...].T)
    for g in range(NB):
        grad = block(top, g)
        regroup(back, g, nn(wdr[g], grad).astype(bf16))
        gdr[g] += nt(block(moved4, g), grad)
    for b in range(NB):
        rows = slice(b * FB, (b + 1) * FB)
        returned = block(back, b)
        grad_hidden = tn(wdl[b], returned)
        gdl[b] += nt(returned, hid[rows, :])
        gated[:FB, :] = (grad_hidden * slope[rows, :].astype(f32)).astype(bf16)
        gated[FB:, :] = (grad_hidden * act[rows, :].astype(f32)).astype(bf16)
        moved = block(moved3, b)
        gur[b] += nt(moved, gated[...])
        regroup(moved4, b, nn(wur[b], gated[...]).astype(bf16))
    grads = []
    for b in range(NB):
        returned = block(moved4, b)
        grads.append(nn(wul[b], returned))
        gul[b] += nt(block(half, b), returned)
    grad_in = jnp.concatenate(grads, axis=0)
    ggain[...] += fold(grad_in * normed)
    grad_middle[...] = top[...].astype(f32) + norm_back(grad_in, normed, scale_row, gain)

    @pl.when(pl.program_id(0) == steps - 1)
    def _():
        sums = exact_nt(jnp.ones((16, LEN), f32), ggain[...]).astype(bf16)

        def write(dst, j):
            part = BS // 2
            for y in range(2):
                b = 2 * y + j
                for c in range(4):
                    dst[y, c * BS : (c + 1) * BS, :] = gur[b, :, c * HALF : (c + 1) * HALF].astype(
                        bf16
                    )
                for c in range(2):
                    at = (4 + c) * BS
                    dst[y, at : at + BS, :] = gdl[b, :, c * HALF : (c + 1) * HALF].astype(bf16)
                at = 6 * BS
                for lane in range(2):
                    dst[y, at : at + part, lane * BS : (lane + 1) * BS] = gul[
                        2 * y + lane, j * part : (j + 1) * part, :
                    ].astype(bf16)
                at += part
                dst[y, at : at + 16, :] = sums[:, y * HALF : (y + 1) * HALF]
                dst[y, at + 16 :, :] = jnp.zeros((FFN_G - at - 16, HALF), bf16)

        core = s_ref[3]
        for c in range(2):

            @pl.when(core == c)
            def _():
                write(keep, c)
                write(send, 1 - c)

        for y in range(2):
            for j in range(2):
                packed_dr[y, :, j * BS : (j + 1) * BS] = gdr[2 * y + j].astype(bf16)


def dense(scalars, middle, own, oth, cols, weights):
    row_count = own.shape[0] // 2
    steps = row_count // TILE

    def own_rows(i, s):
        return (s[0] * steps + i, 0)

    ins = [middle, own, oth, cols] + list(weights)
    in_specs = [
        pl.BlockSpec((D, TILE), lambda i, s: (0, i)),
        pl.BlockSpec((TILE, HALF), own_rows),
        pl.BlockSpec((TILE, HALF), lambda i, s: (i, 0)),
        whole(cols.shape),
    ] + [whole(item.shape) for item in weights]
    half_shape = (2, FFN_G, HALF)
    outs = [
        jax.ShapeDtypeStruct((2 * row_count, HALF), bf16),
        jax.ShapeDtypeStruct((row_count, HALF), bf16),
        jax.ShapeDtypeStruct((D, row_count), f32),
        jax.ShapeDtypeStruct(half_shape, bf16),
        jax.ShapeDtypeStruct(half_shape, bf16),
        jax.ShapeDtypeStruct((2, BS, HALF), bf16),
    ]
    out_specs = [
        pl.BlockSpec((TILE, HALF), own_rows),
        pl.BlockSpec((TILE, HALF), lambda i, s: (i, 0)),
        pl.BlockSpec((D, TILE), lambda i, s: (0, i)),
        whole(half_shape),
        whole(half_shape),
        whole((2, BS, HALF)),
    ]
    full = [(NB, BS, BS), (NB, BS, 2 * FB), (NB, BS, FB), (NB, BS, BS)]
    scratch = [pltpu.VMEM(shape, bf16) for shape in full]
    scratch += [pltpu.VMEM(shape, f32) for shape in ACC_SHAPES]
    scratch += [pltpu.VMEM((D, TILE), bf16) for _ in range(4)]
    scratch += [pltpu.VMEM((NB * FB, TILE), bf16) for _ in range(3)]
    scratch += [pltpu.VMEM((2 * FB, TILE), bf16)]
    scratch += [pltpu.VMEM((D, TILE), bf16) for _ in range(2)]
    return pl.pallas_call(
        functools.partial(dense_kernel, steps=steps),
        out_shape=tuple(outs),
        grid_spec=pltpu.PrefetchScalarGridSpec(
            num_scalar_prefetch=1,
            grid=(steps,),
            in_specs=in_specs,
            out_specs=tuple(out_specs),
            scratch_shapes=scratch,
        ),
        compiler_params=pltpu.CompilerParams(vmem_limit_bytes=VMEM),
        name="dense",
        cost_estimate=pl.CostEstimate(
            flops=row_count * 2 * 8000000, bytes_accessed=row_count * 10000, transcendentals=0
        ),
    )(scalars, *ins)


BACK_SHAPES = (
    (NB, BS, BS),
    (NB, BS, BS),
    (D, LEN),
    (D, 2 * LEN),
    (NB, BS, 3 * BS),
    (NB, BS, BS),
    (D, LEN),
    (D, LEN),
)


def mixer_backward_kernel(
    s_ref,
    grad_middle,
    first,
    kept,
    scale,
    marks,
    cols,
    spec,
    fwd,
    inv,
    wil,
    wir,
    wol,
    wor,
    taps,
    feats,
    packed_dr,
    out_own,
    out_send,
    keep,
    send,
    gol,
    gor,
    gskip,
    gspec,
    gir,
    gil,
    gmask,
    ggain,
    back,
    half,
    conv,
    inner_grad,
    total,
    proj,
    *,
    steps,
    share,
):
    side = s_ref[0]

    @pl.when(pl.program_id(0) == 0)
    def _():
        for acc in (gol, gor, gskip, gspec, gir, gil, gmask, ggain):
            acc[...] = jnp.zeros(acc.shape, f32)

    valid = marks[0:1, :]
    half[...] = grad_middle[...].astype(bf16)
    for g in range(NB):
        grad = block(half, g)
        regroup(back, g, nn(wor[g], grad).astype(bf16))
        gor[g] += nt(block(kept.at[4], g), grad)
    for b in range(NB):
        rows = slice(b * BS, (b + 1) * BS)
        returned = block(back, b)
        grad_mixed = nn(wol[b], returned)
        gate = kept[1, rows, :].astype(f32)
        inner = kept[3, rows, :].astype(f32)
        gol[b] += nt((gate * inner).astype(bf16), returned)
        grad_inner = grad_mixed * gate
        inner_grad[rows, :] = grad_inner
        conv[rows, :] = grad_inner.astype(bf16)
        proj[b * 3 * BS + BS : b * 3 * BS + 2 * BS, :] = (grad_mixed * inner).astype(bf16)
        source = (
            kept[0, rows, :].astype(f32) * kept[2, rows, :].astype(f32) * valid
        ).astype(bf16)
        half[rows, :] = source
        gskip[rows, :] += fold(grad_inner * source.astype(f32))
    hc, hs = spec[:, :LEN], spec[:, LEN:]
    for s in range(BACK_TILE // LEN):
        lanes = slice(s * LEN, (s + 1) * LEN)
        wave = nn(conv[:, lanes], fwd[...])
        wc, ws = wave[:, :LEN], wave[:, LEN:]
        seen = nn(half[:, lanes], fwd[...])
        sc, ss = seen[:, :LEN], seen[:, LEN:]
        gspec[:, :LEN] += wc * sc + ws * ss
        gspec[:, LEN:] += ws * sc - wc * ss
        product = jnp.concatenate(
            [(wc * hc + ws * hs).astype(bf16), (ws * hc - wc * hs).astype(bf16)], axis=1
        )
        total[:, lanes] = nn(product, inv[...])
    for g in range(NB):
        rows = slice(g * BS, (g + 1) * BS)
        grad_source = (total[rows, :] + cols[rows, 3:4] * inner_grad[rows, :]) * valid
        start = g * 3 * BS
        proj[start : start + BS, :] = (grad_source * kept[2, rows, :].astype(f32)).astype(bf16)
        proj[start + 2 * BS : start + 3 * BS, :] = (
            grad_source * kept[0, rows, :].astype(f32)
        ).astype(bf16)

    masked = marks[1:2, :]
    for g in range(NB):
        grad = proj[g * 3 * BS : (g + 1) * 3 * BS, :]
        regroup(back, g, nn(wir[g], grad).astype(bf16))
        gir[g] += nt(block(first.at[1], g), grad)
    gain = column(cols, 1)
    grads = []
    for b in range(NB):
        returned = block(back, b)
        grads.append(nn(wil[b], returned))
        gil[b] += nt(block(first.at[0], b), returned)
    grad_in = jnp.concatenate(grads, axis=0)
    normed = first[0].astype(f32) * (1.0 / gain)
    ggain[...] += fold(grad_in * normed)
    entered = grad_middle[...] + norm_back(grad_in, normed, scale[0:1, :], gain)
    gmask[...] += fold(entered * masked)
    total[...] = entered * (1.0 - masked)
    out_own[...] = total[rows_of(side, HALF), :].T
    out_send[...] = total[rows_of(1 - side, HALF), :].astype(bf16).T

    @pl.when(pl.program_id(0) == steps - 1)
    def _():
        spectrum = gspec[...]
        high = spectrum.astype(bf16)
        low = (spectrum - high.astype(f32)).astype(bf16)
        grad_taps = nn(high, inv[...]) + nn(low, inv[...])
        tap = taps[...]
        grad_taps = grad_taps + tap * (2.0 * penalty_weight * share)
        positions = lax.broadcasted_iota(jnp.int32, (1, LEN), 1).astype(f32)
        decayed = grad_taps * jnp.exp(-column(cols, 4) * positions)
        high = decayed.astype(bf16)
        low = (decayed - high.astype(f32)).astype(bf16)
        sum_weight = (nt(feats[0], high) + nt(feats[1], high) + nt(feats[0], low)).astype(bf16)
        grad_decay = grad_taps * tap * (-positions)
        ones = jnp.ones((16, LEN), f32)
        line = lax.broadcasted_iota(jnp.int32, (16, D), 0)
        vectors = exact_nt(ones, gmask[...])
        vectors = jnp.where(line == 1, exact_nt(ones, ggain[...]), vectors)
        vectors = jnp.where(line == 2, exact_nt(ones, gskip[...]), vectors)
        vectors = jnp.where(line == 3, exact_nt(ones, grad_decay), vectors).astype(bf16)

        def write(dst, j):
            part = BS // 2
            few = ORDER // 2
            for y in range(2):
                lanes = slice(y * HALF, (y + 1) * HALF)
                b = 2 * y + j
                dst[y, 0:BS, :] = gir[b, :, :HALF].astype(bf16)
                dst[y, BS : 2 * BS, 0:BS] = gir[b, :, HALF:].astype(bf16)
                dst[y, BS : 2 * BS, BS:] = gil[b].astype(bf16)
                dst[y, 2 * BS : 3 * BS, 0:BS] = gol[b].astype(bf16)
                dst[y, 2 * BS : 3 * BS, BS:] = gor[b].astype(bf16)
                at = 3 * BS
                dst[y, at : at + part, :] = packed_dr[y, j * part : (j + 1) * part, :]
                at += part
                dst[y, at : at + few, :] = sum_weight[j * few : (j + 1) * few, lanes]
                at += few
                dst[y, at : at + 16, :] = vectors[:, lanes]
                dst[y, at + 16 :, :] = jnp.zeros((MIX_G - at - 16, HALF), bf16)

        core = s_ref[3]
        for c in range(2):

            @pl.when(core == c)
            def _():
                write(keep, c)
                write(send, 1 - c)


def mixer_backward(share, scalars, streams, constants, weights, finals):
    row_count = streams[0].shape[1]
    steps = row_count // BACK_TILE
    ins = list(streams) + list(constants) + list(weights) + list(finals)
    in_specs = [
        pl.BlockSpec((D, BACK_TILE), lambda i, s: (0, i)),
        pl.BlockSpec((2, D, BACK_TILE), lambda i, s: (0, 0, i)),
        pl.BlockSpec((5, D, BACK_TILE), lambda i, s: (0, 0, i)),
        pl.BlockSpec((8, BACK_TILE), lambda i, s: (0, i)),
        pl.BlockSpec((8, BACK_TILE), lambda i, s: (0, i)),
    ] + [whole(item.shape) for item in ins[5:]]
    half_shape = (2, MIX_G, HALF)
    outs = [
        jax.ShapeDtypeStruct((2 * row_count, HALF), f32),
        jax.ShapeDtypeStruct((row_count, HALF), bf16),
        jax.ShapeDtypeStruct(half_shape, bf16),
        jax.ShapeDtypeStruct(half_shape, bf16),
    ]
    out_specs = [
        pl.BlockSpec((BACK_TILE, HALF), lambda i, s: (s[0] * steps + i, 0)),
        pl.BlockSpec((BACK_TILE, HALF), lambda i, s: (i, 0)),
        whole(half_shape),
        whole(half_shape),
    ]
    scratch = [pltpu.VMEM(shape, f32) for shape in BACK_SHAPES]
    scratch += [
        pltpu.VMEM((D, BACK_TILE), bf16),
        pltpu.VMEM((D, BACK_TILE), bf16),
        pltpu.VMEM((D, BACK_TILE), bf16),
        pltpu.VMEM((D, BACK_TILE), f32),
        pltpu.VMEM((D, BACK_TILE), f32),
        pltpu.VMEM((3 * D, BACK_TILE), bf16),
    ]
    return pl.pallas_call(
        functools.partial(mixer_backward_kernel, steps=steps, share=share),
        out_shape=tuple(outs),
        grid_spec=pltpu.PrefetchScalarGridSpec(
            num_scalar_prefetch=1,
            grid=(steps,),
            in_specs=in_specs,
            out_specs=tuple(out_specs),
            scratch_shapes=scratch,
        ),
        compiler_params=pltpu.CompilerParams(vmem_limit_bytes=VMEM),
        name="mixer_backward",
        cost_estimate=pl.CostEstimate(
            flops=row_count * 2 * 6000000, bytes_accessed=row_count * 20000, transcendentals=0
        ),
    )(scalars, *ins)


def place_parts(s_ref, parts, halves):
    quarter = parts[0].shape[0]
    few = quarter // 4
    for where, part in enumerate(parts):
        core = jnp.bitwise_xor(s_ref[3], where >> 1)
        start = jnp.bitwise_xor(s_ref[4], where & 1) * quarter
        for k in range(4):
            row = pl.multiple_of(start + jnp.bitwise_xor(s_ref[5], k) * few, few)
            halves[core, pl.ds(row, few), :] = part[k * few : (k + 1) * few, :]


def dense_unpack_kernel(s_ref, p0, p1, p2, p3, gain, ul, ur, dl, halves):
    place_parts(s_ref, (p0, p1, p2, p3), halves)
    part = BS // 2
    at = 6 * BS
    gain[...] = halves[0, at + part : at + part + 16, :].astype(f32)[0]
    for j in range(2):
        for c in range(4):
            ur[j, :, c * HALF : (c + 1) * HALF] = halves[j, c * BS : (c + 1) * BS, :].astype(f32)
        for c in range(2):
            dl[j, :, c * HALF : (c + 1) * HALF] = halves[
                j, (4 + c) * BS : (5 + c) * BS, :
            ].astype(f32)
        for lane in range(2):
            ul[lane, j * part : (j + 1) * part, :] = halves[
                j, at : at + part, lane * BS : (lane + 1) * BS
            ].astype(f32)


def mixer_unpack_kernel(s_ref, p0, p1, p2, p3, mask, gain, skip, decay, weight, il, ir, ol, orr, dr, halves):
    place_parts(s_ref, (p0, p1, p2, p3), halves)
    part = BS // 2
    few = ORDER // 2
    at = 3 * BS
    vectors = halves[0, at + part + few : at + part + few + 16, :].astype(f32)
    for index, dst in enumerate((mask, gain, skip, decay)):
        dst[...] = vectors[index]
    for j in range(2):
        ir[j, :, :HALF] = halves[j, 0:BS, :].astype(f32)
        ir[j, :, HALF:] = halves[j, BS : 2 * BS, :BS].astype(f32)
        il[j] = halves[j, BS : 2 * BS, BS:].astype(f32)
        ol[j] = halves[j, 2 * BS : 3 * BS, :BS].astype(f32)
        orr[j] = halves[j, 2 * BS : 3 * BS, BS:].astype(f32)
        for lane in range(2):
            dr[lane, j * part : (j + 1) * part, :] = halves[
                j, at : at + part, lane * BS : (lane + 1) * BS
            ].astype(f32)
        weight[j * few : (j + 1) * few, :] = halves[
            j, at + part : at + part + few, :
        ].astype(f32)


def unpack(kernel, scalars, parts, shapes, name):
    outs = tuple(jax.ShapeDtypeStruct(shape, f32) for shape in shapes)
    rows = 2 * parts[0].shape[0]
    return pl.pallas_call(
        kernel,
        out_shape=outs,
        grid_spec=pltpu.PrefetchScalarGridSpec(
            num_scalar_prefetch=1,
            grid=(1,),
            in_specs=[whole(item.shape) for item in parts],
            out_specs=tuple(whole(shape) for shape in shapes),
            scratch_shapes=[pltpu.VMEM((2, rows, HALF), bf16)],
        ),
        compiler_params=pltpu.CompilerParams(vmem_limit_bytes=VMEM),
        name=name,
    )(scalars, *parts)


DENSE_OUTS = ((HALF,), (2, BS, BS), (2, BS, 2 * FB), (2, BS, FB))
MIXER_OUTS = (
    (HALF,),
    (HALF,),
    (HALF,),
    (HALF,),
    (ORDER, HALF),
    (2, BS, BS),
    (2, BS, 3 * BS),
    (2, BS, BS),
    (2, BS, BS),
    (2, BS, BS),
)


def corners_kernel(s_ref, *refs):
    for index in range(4):
        kept, got, out = refs[index], refs[4 + index], refs[8 + index]
        out[...] = (kept[...].astype(f32) + got[...].astype(f32)).astype(bf16)


def corners(scalars, kept, got):
    rows = kept.shape[1] // 2
    shape = jax.ShapeDtypeStruct((rows, HALF), bf16)

    def spec(over_y, over_x):
        def at(i, s):
            y = 1 - s[0] if over_y else s[0]
            x = 1 - s[4] if over_x else s[4]
            return (y, x, 0)

        return pl.BlockSpec((None, rows, HALF), at)

    specs = [spec(False, False), spec(False, True), spec(True, False), spec(True, True)]
    return pl.pallas_call(
        corners_kernel,
        out_shape=(shape,) * 4,
        grid_spec=pltpu.PrefetchScalarGridSpec(
            num_scalar_prefetch=1,
            grid=(1,),
            in_specs=specs + specs,
            out_specs=(whole((rows, HALF)),) * 4,
        ),
        compiler_params=pltpu.CompilerParams(vmem_limit_bytes=VMEM),
        name="sum_corners",
    )(scalars, *([kept] * 4 + [got] * 4))


def columns_kernel(s_ref, a, b, c, d, own, one, two, three, total):
    total[...] = (
        a[...].astype(f32) + b[...].astype(f32) + c[...].astype(f32) + d[...].astype(f32)
    )
    few = total.shape[0] // 4
    for k, out in enumerate((own, one, two, three)):
        row = pl.multiple_of(jnp.bitwise_xor(s_ref[5], k) * few, few)
        out[...] = total[pl.ds(row, few), :].astype(bf16)


def columns(scalars, parts):
    rows = parts[0].shape[0]
    shape = jax.ShapeDtypeStruct((rows // 4, HALF), bf16)
    return pl.pallas_call(
        columns_kernel,
        out_shape=(shape,) * 4,
        grid_spec=pltpu.PrefetchScalarGridSpec(
            num_scalar_prefetch=1,
            grid=(1,),
            in_specs=[whole((rows, HALF))] * 4,
            out_specs=(whole((rows // 4, HALF)),) * 4,
            scratch_shapes=[pltpu.VMEM((rows, HALF), f32)],
        ),
        compiler_params=pltpu.CompilerParams(vmem_limit_bytes=VMEM),
        name="sum_columns",
    )(scalars, *parts)


def swap_narrow(values):
    return lax.ppermute(values, "narrow", [(0, 1), (1, 0)])


def swap_wide(values, bit, size):
    return lax.ppermute(values, "wide", [(i, i ^ (1 << bit)) for i in range(size)])


def swap_both(values, bit, size):
    flip = 2 << bit
    return lax.ppermute(
        values, ("wide", "narrow"), [(i, i ^ flip ^ 1) for i in range(2 * size)]
    )


def shift_wide(values, flip, size):
    return lax.ppermute(values, "wide", [(i, i ^ flip) for i in range(size)])


def add_low(*items):
    total = items[0].astype(f32)
    for item in items[1:]:
        total = total + item.astype(f32)
    return total.astype(bf16)


def over_corners(parts, size):
    own, over_x, over_y, over_both = parts
    return (
        own,
        swap_wide(over_x, 1, size),
        swap_narrow(over_y),
        swap_both(over_both, 1, size),
    )


def over_columns(parts, size):
    own, *others = parts
    packed = add_low(
        own, *(shift_wide(item, (k + 1) << 2, size) for k, item in enumerate(others))
    )
    bit = 4
    while 1 << bit < size:
        packed = add_low(packed, swap_wide(packed, bit, size))
        bit += 1
    return jnp.concatenate(
        [packed] + [shift_wide(packed, k << 2, size) for k in (1, 2, 3)], axis=0
    )


def over_rows(near, size):
    far = swap_wide(near, 1, size)
    return (near, far, swap_wide(near, 0, size), swap_wide(far, 0, size))


def gather_pieces(piece, bits, size):
    pieces = [swap_narrow(piece)]
    for bit in bits:
        pieces = pieces + [swap_wide(item, bit, size) for item in pieces]
    return pieces


def on_device(
    wide_size,
    tokens,
    lengths,
    mask_pos,
    mask_vector,
    norm1_gain,
    in_left,
    in_right,
    filter_weight,
    decay,
    skip_gain,
    out_left,
    out_right,
    norm2_gain,
    up_left,
    up_right,
    down_left,
    down_right,
    cotangent,
):
    index = lax.axis_index("wide")
    side = lax.axis_index("narrow")
    row_count = tokens.shape[0] // 2
    scalars = jnp.stack(
        [side, index & 3, (index >> 2) & 1, index & 1, (index >> 1) & 1, (index >> 2) & 3]
    ).astype(jnp.int32)
    share = 1.0 / (2 * wide_size)

    def sent_rows(values):
        return lax.dynamic_slice_in_dim(values, (1 - side) * row_count, row_count, 0)

    mixer_weights = (in_left, in_right, out_left, out_right)
    dense_weights = (up_left, up_right, jnp.swapaxes(down_left, 1, 2), down_right)
    vectors = (mask_vector, norm1_gain, norm2_gain, skip_gain, decay)
    mix_piece, ffn_piece = pack_weights(
        scalars, mixer_weights, dense_weights, filter_weight, vectors
    )
    first, third = gather_pieces(mix_piece, (1,), wide_size)
    mix_pieces = (first, swap_wide(first, 0, wide_size), third, swap_wide(third, 0, wide_size))
    y0, z0, x0, xz0 = gather_pieces(ffn_piece, (2, 1), wide_size)
    ffn_pieces = tuple(
        piece
        for near in ((y0, x0), (z0, xz0))
        for item in near
        for piece in (item, swap_wide(item, 0, wide_size))
    )
    tokens_other = swap_narrow(sent_rows(tokens))
    cot_other = swap_narrow(sent_rows(cotangent))

    positions = jnp.arange(LEN, dtype=jnp.int32)
    valid = (positions[None, :] < lengths[:, None]).astype(f32)
    masked = jnp.any(mask_pos[:, :, None] == positions[None, None, :], axis=1).astype(f32)
    marks = jnp.stack([valid, masked]).reshape(2, 2, row_count)
    marks = lax.dynamic_index_in_dim(marks, side, 1, keepdims=False)
    marks = jnp.concatenate([marks, jnp.zeros((6, row_count), f32)], axis=0)

    fwd, inv = (jnp.asarray(item) for item in transform_tables())
    feats = jnp.asarray(feature_parts())
    taps, spec, penalty, cols = filter_call(
        scalars, filter_weight, mix_piece, mix_pieces, feats, fwd
    )

    middle, first, kept, scale, *full = mixer_forward(
        scalars, tokens, tokens_other, marks, cols, spec, fwd, inv, mixer_weights + mix_pieces
    )
    output, output_sent, grad_middle, ffn_keep, ffn_send, packed_dr = dense(
        scalars, middle, cotangent, cot_other, cols, dense_weights + ffn_pieces
    )
    output_other = swap_narrow(output_sent)
    ffn_parts = corners(scalars, ffn_keep, swap_wide(ffn_send, 0, wide_size))
    grad_middle, *ffn_parts = lax.optimization_barrier((grad_middle, *ffn_parts))
    ffn_parts = over_corners(ffn_parts, wide_size)
    tokens_grad, grad_sent, mix_keep, mix_send = mixer_backward(
        share,
        scalars,
        (grad_middle, first, kept, scale, marks),
        (cols, spec, fwd, inv),
        full,
        (taps, feats, packed_dr),
    )
    mix_keep, mix_send, output_other, *ffn_parts = lax.optimization_barrier(
        (mix_keep, mix_send, output_other, *ffn_parts)
    )
    mix_parts = corners(scalars, mix_keep, swap_wide(mix_send, 0, wide_size))
    ffn_parts = columns(scalars, ffn_parts)
    mix_parts = columns(scalars, over_corners(mix_parts, wide_size))
    grad_sent, *mix_parts = lax.optimization_barrier((grad_sent, *mix_parts))
    grad_other = swap_narrow(grad_sent)
    ffn_near = over_columns(ffn_parts, wide_size)
    mix_near = over_columns(mix_parts, wide_size)
    ffn_parts = over_rows(ffn_near, wide_size)
    mix_near, grad_other = lax.optimization_barrier((mix_near, grad_other))
    mix_parts = over_rows(mix_near, wide_size)
    gain_two, g_ul, g_ur, g_dl = unpack(
        dense_unpack_kernel, scalars, ffn_parts, DENSE_OUTS, "dense_unpack"
    )
    g_mask, g_gain, g_skip, g_decay, g_filter, g_il, g_ir, g_ol, g_or, g_dr = unpack(
        mixer_unpack_kernel, scalars, mix_parts, MIXER_OUTS, "mixer_unpack"
    )
    start = (1 - side) * row_count
    output = lax.dynamic_update_slice_in_dim(output, output_other, start, 0)
    tokens_grad = lax.dynamic_update_slice_in_dim(tokens_grad, grad_other.astype(f32), start, 0)
    return (
        output,
        tokens_grad,
        g_mask,
        g_gain,
        g_il,
        g_ir,
        g_filter,
        g_decay,
        g_skip,
        g_ol,
        g_or,
        gain_two,
        g_ul,
        g_ur,
        jnp.swapaxes(g_dl, 1, 2),
        g_dr,
        penalty[0, 0],
    )


def solution(mesh):
    placed = (
        P("wide", "narrow"),
        P("wide"),
        P("wide", None),
        P("narrow"),
        P("narrow"),
        P("narrow", None, None),
        P("narrow", None, None),
        P(None, "narrow"),
        P("narrow"),
        P("narrow"),
        P("narrow", None, None),
        P("narrow", None, None),
        P("narrow"),
        P("narrow", None, None),
        P("narrow", None, None),
        P("narrow", None, None),
        P("narrow", None, None),
        P("wide", "narrow"),
    )
    return jax.shard_map(
        functools.partial(on_device, mesh.shape["wide"]),
        mesh=mesh,
        in_specs=placed,
        out_specs=(
            P("wide", "narrow"),
            P("wide", "narrow"),
            P("narrow"),
            P("narrow"),
            P("narrow", None, None),
            P("narrow", None, None),
            P(None, "narrow"),
            P("narrow"),
            P("narrow"),
            P("narrow", None, None),
            P("narrow", None, None),
            P("narrow"),
            P("narrow", None, None),
            P("narrow", None, None),
            P("narrow", None, None),
            P("narrow", None, None),
            P(),
        ),
        check_vma=False,
    )
```

```python
import functools

import jax
import jax.numpy as jnp
import numpy as np
from jax import lax
from jax.experimental import pallas as pl
from jax.experimental.pallas import tpu as pltpu
from jax.sharding import PartitionSpec as P

D = 768
NB = 4
ORDER = 128
LEN = 128
BS = 192
FB = 768
GROUP = BS // NB
HALF = D // 2
QUARTER = BS // 4

epsilon = 1e-05
penalty_weight = 0.005

bf16 = jnp.bfloat16
f32 = jnp.float32

TILE = 512
BACK_TILE = 256
VMEM = 60 << 20

FILTER_ROW = 3 * QUARTER
VECTOR_ROW = FILTER_ROW + ORDER // 8
MIX_W = VECTOR_ROW + 16
FFN_W = 7 * QUARTER
FFN_G = 1280
MIX_G = 768


def transform_tables():
    t = np.arange(LEN, dtype=np.float64)[:, None]
    k = np.arange(LEN, dtype=np.float64)[None, :]
    angle = np.pi * (2 * k + 1) * t / (2 * LEN)
    forward = np.concatenate([np.cos(angle), np.sin(angle)], axis=1)
    return forward.astype(bf16), (forward.T / LEN).astype(bf16)


def feature_parts():
    t = np.arange(LEN, dtype=np.float64)[None, :]
    freqs = (np.arange(ORDER // 2, dtype=np.float64)[:, None] + 1.0) * (3.1 / (ORDER // 2))
    table = np.concatenate([np.sin(t * freqs), np.cos(t * freqs)], axis=0)
    parts = []
    for _ in range(3):
        part = table.astype(bf16)
        parts.append(part)
        table = table - part.astype(np.float64)
    return np.stack(parts)


def nn(a, b):
    return lax.dot_general(a, b, (((1,), (0,)), ((), ())), preferred_element_type=f32)


def nt(a, b):
    return lax.dot_general(a, b, (((1,), (1,)), ((), ())), preferred_element_type=f32)


def tn(a, b):
    return lax.dot_general(a, b, (((0,), (0,)), ((), ())), preferred_element_type=f32)


def exact_nt(a, b):
    return lax.dot_general(
        a,
        b,
        (((1,), (1,)), ((), ())),
        preferred_element_type=f32,
        precision=lax.Precision.HIGHEST,
    )


def fold(values):
    out = values[:, :LEN]
    for start in range(LEN, values.shape[1], LEN):
        out = out + values[:, start : start + LEN]
    return out


def light():
    return pl.CostEstimate(flops=0, bytes_accessed=1 << 20, transcendentals=0)


def rows_of(block, size):
    return pl.ds(pl.multiple_of(block * size, size), size)


def column(cols_ref, index):
    return cols_ref[:, index : index + 1]


def place_halves(dst_ref, side, own, other):
    dst_ref[rows_of(side, HALF), :] = own
    dst_ref[rows_of(1 - side, HALF), :] = other


def regroup(dst_ref, block, values):
    for g in range(NB):
        dst_ref[g * BS + block * GROUP : g * BS + (block + 1) * GROUP, :] = values[
            g * GROUP : (g + 1) * GROUP, :
        ]


def block(ref, index, size=BS):
    return ref[index * size : (index + 1) * size, :]


def norm_stats(values):
    center = values - jnp.sum(values, axis=0, keepdims=True) * (1.0 / D)
    spread = jnp.sum(center * center, axis=0, keepdims=True) * (1.0 / D)
    scale_row = lax.rsqrt(spread + epsilon)
    return center * scale_row, scale_row


def norm_back(grad, normed, scale_row, gain):
    scaled = grad * gain
    first = jnp.sum(scaled, axis=0, keepdims=True) * (1.0 / D)
    second = jnp.sum(scaled * normed, axis=0, keepdims=True) * (1.0 / D)
    return scale_row * (scaled - first - normed * second)


def pack_kernel(
    s_ref, il, ir, ol, orr, ul, ur, dl, dr, weight, mask, gain1, gain2, skip, decay, mix_ref, ffn_ref
):
    q = QUARTER
    mix_ref[0:q, :] = jnp.concatenate([il[0], ol[0]], axis=1)
    mix_ref[q : 2 * q, :] = ir[0][:, :HALF]
    mix_ref[2 * q : 3 * q, :] = jnp.concatenate([ir[0][:, HALF:], orr[0]], axis=1)
    mix_ref[FILTER_ROW:VECTOR_ROW, :] = weight[...]
    rest = decay[...].reshape(1, HALF)
    rows = [item[...].reshape(1, HALF).astype(f32) for item in (mask, gain1, gain2, skip)]
    for _ in range(3):
        part = rest.astype(bf16).astype(f32)
        rows.append(part)
        rest = rest - part
    line = lax.broadcasted_iota(jnp.int32, (16, HALF), 0)
    vectors = jnp.zeros((16, HALF), f32)
    for index, row in enumerate(rows):
        vectors = jnp.where(line == index, row, vectors)
    mix_ref[VECTOR_ROW:, :] = vectors.astype(bf16)
    for c in range(4):
        ffn_ref[c * q : (c + 1) * q, :] = ur[0][:, c * HALF : (c + 1) * HALF]
    for c in range(2):
        ffn_ref[(4 + c) * q : (5 + c) * q, :] = dl[0][:, c * HALF : (c + 1) * HALF]
    ffn_ref[6 * q : 7 * q, :] = jnp.concatenate([ul[0], dr[0]], axis=1)


def pack_weights(scalars, mixer_weights, dense_weights, filter_weight, vectors):
    def eighth(item):
        return pl.BlockSpec((1, QUARTER, item.shape[2]), lambda i, s: (s[2], s[1], 0))

    return pl.pallas_call(
        pack_kernel,
        out_shape=(
            jax.ShapeDtypeStruct((MIX_W, HALF), bf16),
            jax.ShapeDtypeStruct((FFN_W, HALF), bf16),
        ),
        grid_spec=pltpu.PrefetchScalarGridSpec(
            num_scalar_prefetch=1,
            grid=(1,),
            in_specs=[eighth(item) for item in mixer_weights + dense_weights]
            + [pl.BlockSpec((ORDER // 8, HALF), lambda i, s: (4 * s[2] + s[1], 0))]
            + [whole(item.shape) for item in vectors],
            out_specs=(whole((MIX_W, HALF)), whole((FFN_W, HALF))),
        ),
        name="pack_weights",
        cost_estimate=light(),
    )(scalars, *mixer_weights, *dense_weights, filter_weight, *vectors)


def own_blocks(dst, side, src):
    for j in range(2):
        dst[2 * side + j] = src[j]


def filter_kernel(
    s_ref, own, mine, *refs
):
    pieces = refs[:8]
    feats, fwd, taps_ref, spec_ref, pen_ref, cols_ref, weight = refs[8:]
    side = s_ref[0]
    q = ORDER // 8
    for p, piece in enumerate(pieces):
        place = 4 * jnp.bitwise_xor(s_ref[2], p >> 2) + jnp.bitwise_xor(s_ref[1], p & 3)
        weight[pl.ds(pl.multiple_of(place * q, q), q), :] = piece[FILTER_ROW:VECTOR_ROW, :]
    for which, src, rows in ((side, own, mine), (1 - side, weight, pieces[0])):
        table = src[...]
        basis = tn(table, feats[2]) + tn(table, feats[1]) + tn(table, feats[0])
        taps_ref[rows_of(which, HALF), :] = basis
        vectors = rows[VECTOR_ROW:, :].astype(f32)
        vectors = jnp.concatenate([vectors, jnp.zeros((LEN - 16, HALF), f32)], axis=0)
        vectors = vectors.T
        lane = lax.broadcasted_iota(jnp.int32, (HALF, LEN), 1)
        decay = vectors[:, 4:5] + vectors[:, 5:6] + vectors[:, 6:7]
        cols_ref[rows_of(which, HALF), :] = jnp.where(lane == 4, decay, vectors)
    positions = lax.broadcasted_iota(jnp.int32, (1, LEN), 1).astype(f32)
    taps = taps_ref[...] * jnp.exp(-column(cols_ref, 4) * positions)
    taps_ref[...] = taps
    spec_ref[...] = nn(taps.astype(bf16), fwd[...])
    total = jnp.sum(jnp.sum(taps * taps, axis=0, keepdims=True), axis=1, keepdims=True)
    pen_ref[...] = jnp.broadcast_to(total * penalty_weight, (8, LEN))


def whole(shape):
    return pl.BlockSpec(shape, lambda *_: (0,) * len(shape))


def filter_call(scalars, own, mine, pieces, feats, fwd):
    ins = (own, mine) + tuple(pieces) + (feats, fwd)
    outs = (
        jax.ShapeDtypeStruct((D, LEN), f32),
        jax.ShapeDtypeStruct((D, 2 * LEN), f32),
        jax.ShapeDtypeStruct((8, LEN), f32),
        jax.ShapeDtypeStruct((D, LEN), f32),
    )
    return pl.pallas_call(
        filter_kernel,
        out_shape=outs,
        grid_spec=pltpu.PrefetchScalarGridSpec(
            num_scalar_prefetch=1,
            grid=(1,),
            in_specs=[whole(item.shape) for item in ins],
            out_specs=tuple(whole(item.shape) for item in outs),
            scratch_shapes=[pltpu.VMEM((ORDER, HALF), bf16)],
        ),
        name="filter_spectrum",
        cost_estimate=light(),
    )(scalars, *ins)


def mixer_forward_kernel(
    s_ref,
    own,
    oth,
    marks,
    cols,
    spec,
    fwd,
    inv,
    il,
    ir,
    ol,
    orr,
    *refs,
):
    pieces = refs[:8]
    middle, first, kept, scale, wil, wir, wol, wor, enter, half, conv = refs[8:]
    side = s_ref[0]

    @pl.when(pl.program_id(0) == 0)
    def _():
        other = 1 - side
        own_blocks(wil, side, il)
        own_blocks(wir, side, ir)
        own_blocks(wol, side, ol)
        own_blocks(wor, side, orr)
        q = QUARTER
        for p, piece in enumerate(pieces):
            at = pl.ds(pl.multiple_of(jnp.bitwise_xor(s_ref[1], p & 3) * q, q), q)
            blk = 2 * other + jnp.bitwise_xor(s_ref[2], p >> 2)
            wil[blk, at, :] = piece[0:q, :BS]
            wol[blk, at, :] = piece[0:q, BS:]
            wir[blk, at, 0:HALF] = piece[q : 2 * q, :]
            wir[blk, at, HALF:] = piece[2 * q : 3 * q, :BS]
            wor[blk, at, :] = piece[2 * q : 3 * q, BS:]

    place_halves(enter, side, own[...].T.astype(f32), oth[...].T.astype(f32))
    valid = marks[0:1, :]
    masked = marks[1:2, :]
    tokens = enter[...]
    entered = tokens + masked * (column(cols, 0) - tokens)
    enter[...] = entered
    normed, scale_row = norm_stats(entered)
    scale[...] = jnp.broadcast_to(scale_row, scale.shape)
    half[...] = (normed * column(cols, 1)).astype(bf16)
    first[0] = half[...]
    for b in range(NB):
        regroup(first.at[1], b, tn(wil[b], block(half, b)).astype(bf16))
    for g in range(NB):
        projected = tn(wir[g], block(first.at[1], g))
        rows = slice(g * BS, (g + 1) * BS)
        for part in range(3):
            kept[part, rows, :] = projected[part * BS : (part + 1) * BS, :].astype(bf16)
        source = (projected[:BS] * projected[2 * BS :] * valid).astype(bf16)
        half[rows, :] = source
    for s in range(TILE // LEN):
        lanes = slice(s * LEN, (s + 1) * LEN)
        wave = nn(half[:, lanes], fwd[...])
        wc, ws = wave[:, :LEN], wave[:, LEN:]
        hc, hs = spec[:, :LEN], spec[:, LEN:]
        product = jnp.concatenate(
            [(wc * hc - ws * hs).astype(bf16), (wc * hs + ws * hc).astype(bf16)], axis=1
        )
        conv[:, lanes] = nn(product, inv[...])
    inner = conv[...] + column(cols, 3) * half[...].astype(f32)
    kept[3] = inner.astype(bf16)
    half[...] = (kept[1].astype(f32) * inner).astype(bf16)
    for b in range(NB):
        regroup(kept.at[4], b, tn(wol[b], block(half, b)).astype(bf16))
    for g in range(NB):
        rows = slice(g * BS, (g + 1) * BS)
        middle[rows, :] = (enter[rows, :] + tn(wor[g], block(kept.at[4], g))).astype(bf16)


def mixer_forward(scalars, own, oth, marks, cols, spec, fwd, inv, weights):
    row_count = own.shape[0] // 2
    steps = row_count // TILE
    ins = (own, oth, marks, cols, spec, fwd, inv) + tuple(weights)
    in_specs = [
        pl.BlockSpec((TILE, HALF), lambda i, s: (s[0] * steps + i, 0)),
        pl.BlockSpec((TILE, HALF), lambda i, s: (i, 0)),
        pl.BlockSpec((8, TILE), lambda i, s: (0, i)),
    ] + [whole(item.shape) for item in ins[3:]]
    full = [(NB, BS, BS), (NB, BS, 3 * BS), (NB, BS, BS), (NB, BS, BS)]
    outs = [
        jax.ShapeDtypeStruct((D, row_count), bf16),
        jax.ShapeDtypeStruct((2, D, row_count), bf16),
        jax.ShapeDtypeStruct((5, D, row_count), bf16),
        jax.ShapeDtypeStruct((8, row_count), f32),
    ] + [jax.ShapeDtypeStruct(shape, bf16) for shape in full]
    out_specs = [
        pl.BlockSpec((D, TILE), lambda i, s: (0, i)),
        pl.BlockSpec((2, D, TILE), lambda i, s: (0, 0, i)),
        pl.BlockSpec((5, D, TILE), lambda i, s: (0, 0, i)),
        pl.BlockSpec((8, TILE), lambda i, s: (0, i)),
    ] + [whole(shape) for shape in full]
    return pl.pallas_call(
        mixer_forward_kernel,
        out_shape=tuple(outs),
        grid_spec=pltpu.PrefetchScalarGridSpec(
            num_scalar_prefetch=1,
            grid=(steps,),
            in_specs=in_specs,
            out_specs=tuple(out_specs),
            scratch_shapes=[
                pltpu.VMEM((D, TILE), f32),
                pltpu.VMEM((D, TILE), bf16),
                pltpu.VMEM((D, TILE), f32),
            ],
        ),
        compiler_params=pltpu.CompilerParams(vmem_limit_bytes=VMEM),
        name="mixer_forward",
        cost_estimate=pl.CostEstimate(
            flops=row_count * 2 * 1500000, bytes_accessed=row_count * 20000, transcendentals=0
        ),
    )(scalars, *ins)


ACC_SHAPES = ((NB, BS, 2 * FB), (NB, BS, FB), (NB, BS, BS), (NB, BS, BS), (D, LEN))


def dense_kernel(
    s_ref,
    middle,
    own,
    oth,
    cols,
    ul,
    ur,
    dl,
    dr,
    p0,
    p1,
    p2,
    p3,
    p4,
    p5,
    p6,
    p7,
    out_own,
    out_send,
    grad_middle,
    keep,
    send,
    packed_dr,
    wul,
    wur,
    wdl,
    wdr,
    gur,
    gdl,
    gul,
    gdr,
    ggain,
    top,
    half,
    moved3,
    moved4,
    hid,
    act,
    slope,
    gated,
    back,
    outs,
    *,
    steps,
):
    side = s_ref[0]

    @pl.when(pl.program_id(0) == 0)
    def _():
        other = 1 - side
        own_blocks(wul, side, ul)
        own_blocks(wur, side, ur)
        own_blocks(wdl, side, dl)
        own_blocks(wdr, side, dr)
        q = QUARTER
        for p, piece in enumerate((p0, p1, p2, p3, p4, p5, p6, p7)):
            row = pl.multiple_of(jnp.bitwise_xor(s_ref[1], p & 3) * q, q)
            at = pl.ds(row, q)
            blk = 2 * other + jnp.bitwise_xor(s_ref[2], p >> 2)
            for c in range(4):
                wur[blk, at, c * HALF : (c + 1) * HALF] = piece[c * q : (c + 1) * q, :]
            for c in range(2):
                wdl[blk, at, c * HALF : (c + 1) * HALF] = piece[(4 + c) * q : (5 + c) * q, :]
            wul[blk, at, :] = piece[6 * q : 7 * q, :BS]
            wdr[blk, at, :] = piece[6 * q : 7 * q, BS:]
        for acc in (gur, gdl, gul, gdr, ggain):
            acc[...] = jnp.zeros(acc.shape, f32)

    gain = column(cols, 2)
    normed, scale_row = norm_stats(middle[...].astype(f32))
    half[...] = (normed * gain).astype(bf16)
    for b in range(NB):
        regroup(moved3, b, tn(wul[b], block(half, b)).astype(bf16))
    for g in range(NB):
        rows = slice(g * FB, (g + 1) * FB)
        both = tn(wur[g], block(moved3, g))
        gate, up = both[:FB], both[FB:]
        chance = 0.5 + 0.5 * lax.erf(gate * 0.7071067811865476)
        density = jnp.exp(gate * gate * -0.5 - 0.9189385332046727)
        active = gate * chance
        hid[rows, :] = (active * up).astype(bf16)
        act[rows, :] = active.astype(bf16)
        slope[rows, :] = (up * (chance + gate * density)).astype(bf16)
        regroup(moved4, g, nn(wdl[g], hid[rows, :]).astype(bf16))
    for g in range(NB):
        rows = slice(g * BS, (g + 1) * BS)
        outs[rows, :] = (middle[rows, :].astype(f32) + tn(wdr[g], block(moved4, g))).astype(bf16)
    out_own[...] = outs[rows_of(side, HALF), :].T
    out_send[...] = outs[rows_of(1 - side, HALF), :].T
    place_halves(top, side, own[...].T, oth[...].T)
    for g in range(NB):
        grad = block(top, g)
        regroup(back, g, nn(wdr[g], grad).astype(bf16))
        gdr[g] += nt(block(moved4, g), grad)
    for b in range(NB):
        rows = slice(b * FB, (b + 1) * FB)
        returned = block(back, b)
        grad_hidden = tn(wdl[b], returned)
        gdl[b] += nt(returned, hid[rows, :])
        lowered = grad_hidden.astype(bf16)
        gated[:FB, :] = lowered * slope[rows, :]
        gated[FB:, :] = lowered * act[rows, :]
        moved = block(moved3, b)
        gur[b] += nt(moved, gated[...])
        regroup(moved4, b, nn(wur[b], gated[...]).astype(bf16))
    grads = []
    for b in range(NB):
        returned = block(moved4, b)
        grads.append(nn(wul[b], returned))
        gul[b] += nt(block(half, b), returned)
    grad_in = jnp.concatenate(grads, axis=0)
    ggain[...] += fold(grad_in * normed)
    grad_middle[...] = (
        top[...].astype(f32) + norm_back(grad_in, normed, scale_row, gain)
    ).astype(bf16)

    @pl.when(pl.program_id(0) == steps - 1)
    def _():
        sums = exact_nt(jnp.ones((16, LEN), f32), ggain[...]).astype(bf16)

        def write(dst, j):
            part = BS // 2
            for y in range(2):
                b = 2 * y + j
                for c in range(4):
                    dst[y, c * BS : (c + 1) * BS, :] = gur[b, :, c * HALF : (c + 1) * HALF].astype(
                        bf16
                    )
                for c in range(2):
                    at = (4 + c) * BS
                    dst[y, at : at + BS, :] = gdl[b, :, c * HALF : (c + 1) * HALF].astype(bf16)
                at = 6 * BS
                for lane in range(2):
                    dst[y, at : at + part, lane * BS : (lane + 1) * BS] = gul[
                        2 * y + lane, j * part : (j + 1) * part, :
                    ].astype(bf16)
                at += part
                dst[y, at : at + 16, :] = sums[:, y * HALF : (y + 1) * HALF]
                dst[y, at + 16 :, :] = jnp.zeros((FFN_G - at - 16, HALF), bf16)

        core = s_ref[3]
        for c in range(2):

            @pl.when(core == c)
            def _():
                write(keep, c)
                write(send, 1 - c)

        for y in range(2):
            for j in range(2):
                packed_dr[y, :, j * BS : (j + 1) * BS] = gdr[2 * y + j].astype(bf16)


def dense(scalars, middle, own, oth, cols, weights):
    row_count = own.shape[0] // 2
    steps = row_count // TILE

    def own_rows(i, s):
        return (s[0] * steps + i, 0)

    ins = [middle, own, oth, cols] + list(weights)
    in_specs = [
        pl.BlockSpec((D, TILE), lambda i, s: (0, i)),
        pl.BlockSpec((TILE, HALF), own_rows),
        pl.BlockSpec((TILE, HALF), lambda i, s: (i, 0)),
        whole(cols.shape),
    ] + [whole(item.shape) for item in weights]
    half_shape = (2, FFN_G, HALF)
    outs = [
        jax.ShapeDtypeStruct((2 * row_count, HALF), bf16),
        jax.ShapeDtypeStruct((row_count, HALF), bf16),
        jax.ShapeDtypeStruct((D, row_count), bf16),
        jax.ShapeDtypeStruct(half_shape, bf16),
        jax.ShapeDtypeStruct(half_shape, bf16),
        jax.ShapeDtypeStruct((2, BS, HALF), bf16),
    ]
    out_specs = [
        pl.BlockSpec((TILE, HALF), own_rows),
        pl.BlockSpec((TILE, HALF), lambda i, s: (i, 0)),
        pl.BlockSpec((D, TILE), lambda i, s: (0, i)),
        whole(half_shape),
        whole(half_shape),
        whole((2, BS, HALF)),
    ]
    full = [(NB, BS, BS), (NB, BS, 2 * FB), (NB, BS, FB), (NB, BS, BS)]
    scratch = [pltpu.VMEM(shape, bf16) for shape in full]
    scratch += [pltpu.VMEM(shape, f32) for shape in ACC_SHAPES]
    scratch += [pltpu.VMEM((D, TILE), bf16) for _ in range(4)]
    scratch += [pltpu.VMEM((NB * FB, TILE), bf16) for _ in range(3)]
    scratch += [pltpu.VMEM((2 * FB, TILE), bf16)]
    scratch += [pltpu.VMEM((D, TILE), bf16) for _ in range(2)]
    return pl.pallas_call(
        functools.partial(dense_kernel, steps=steps),
        out_shape=tuple(outs),
        grid_spec=pltpu.PrefetchScalarGridSpec(
            num_scalar_prefetch=1,
            grid=(steps,),
            in_specs=in_specs,
            out_specs=tuple(out_specs),
            scratch_shapes=scratch,
        ),
        compiler_params=pltpu.CompilerParams(vmem_limit_bytes=46 << 20),
        name="dense",
        cost_estimate=pl.CostEstimate(
            flops=row_count * 2 * 8000000, bytes_accessed=row_count * 10000, transcendentals=0
        ),
    )(scalars, *ins)


BACK_SHAPES = (
    (NB, BS, BS),
    (NB, BS, BS),
    (D, LEN),
    (D, 2 * LEN),
    (NB, BS, 3 * BS),
    (NB, BS, BS),
    (D, LEN),
    (D, LEN),
)


def mixer_backward_kernel(
    s_ref,
    grad_middle,
    first,
    kept,
    scale,
    marks,
    cols,
    spec,
    fwd,
    inv,
    wil,
    wir,
    wol,
    wor,
    taps,
    feats,
    packed_dr,
    out_own,
    out_send,
    keep,
    send,
    gol,
    gor,
    gskip,
    gspec,
    gir,
    gil,
    gmask,
    ggain,
    back,
    half,
    conv,
    inner_grad,
    total,
    proj,
    *,
    steps,
    share,
):
    side = s_ref[0]

    @pl.when(pl.program_id(0) == 0)
    def _():
        for acc in (gol, gor, gskip, gspec, gir, gil, gmask, ggain):
            acc[...] = jnp.zeros(acc.shape, f32)

    valid = marks[0:1, :]
    for g in range(NB):
        grad = block(grad_middle, g)
        regroup(back, g, nn(wor[g], grad).astype(bf16))
        gor[g] += nt(block(kept.at[4], g), grad)
    for b in range(NB):
        rows = slice(b * BS, (b + 1) * BS)
        returned = block(back, b)
        grad_mixed = nn(wol[b], returned)
        gate = kept[1, rows, :].astype(f32)
        inner = kept[3, rows, :].astype(f32)
        gol[b] += nt((gate * inner).astype(bf16), returned)
        grad_inner = grad_mixed * gate
        inner_grad[rows, :] = grad_inner
        conv[rows, :] = grad_inner.astype(bf16)
        proj[b * 3 * BS + BS : b * 3 * BS + 2 * BS, :] = (grad_mixed * inner).astype(bf16)
        source = (
            kept[0, rows, :].astype(f32) * kept[2, rows, :].astype(f32) * valid
        ).astype(bf16)
        half[rows, :] = source
        gskip[rows, :] += fold(grad_inner * source.astype(f32))
    hc, hs = spec[:, :LEN], spec[:, LEN:]
    for s in range(BACK_TILE // LEN):
        lanes = slice(s * LEN, (s + 1) * LEN)
        wave = nn(conv[:, lanes], fwd[...])
        wc, ws = wave[:, :LEN], wave[:, LEN:]
        seen = nn(half[:, lanes], fwd[...])
        sc, ss = seen[:, :LEN], seen[:, LEN:]
        gspec[:, :LEN] += wc * sc + ws * ss
        gspec[:, LEN:] += ws * sc - wc * ss
        product = jnp.concatenate(
            [(wc * hc + ws * hs).astype(bf16), (ws * hc - wc * hs).astype(bf16)], axis=1
        )
        total[:, lanes] = nn(product, inv[...])
    for g in range(NB):
        rows = slice(g * BS, (g + 1) * BS)
        grad_source = (total[rows, :] + cols[rows, 3:4] * inner_grad[rows, :]) * valid
        start = g * 3 * BS
        proj[start : start + BS, :] = (grad_source * kept[2, rows, :].astype(f32)).astype(bf16)
        proj[start + 2 * BS : start + 3 * BS, :] = (
            grad_source * kept[0, rows, :].astype(f32)
        ).astype(bf16)

    masked = marks[1:2, :]
    for g in range(NB):
        grad = proj[g * 3 * BS : (g + 1) * 3 * BS, :]
        regroup(back, g, nn(wir[g], grad).astype(bf16))
        gir[g] += nt(block(first.at[1], g), grad)
    gain = column(cols, 1)
    grads = []
    for b in range(NB):
        returned = block(back, b)
        grads.append(nn(wil[b], returned))
        gil[b] += nt(block(first.at[0], b), returned)
    grad_in = jnp.concatenate(grads, axis=0)
    normed = first[0].astype(f32) * (1.0 / gain)
    ggain[...] += fold(grad_in * normed)
    entered = grad_middle[...].astype(f32) + norm_back(grad_in, normed, scale[0:1, :], gain)
    gmask[...] += fold(entered * masked)
    total[...] = entered * (1.0 - masked)
    out_own[...] = total[rows_of(side, HALF), :].T
    out_send[...] = total[rows_of(1 - side, HALF), :].astype(bf16).T

    @pl.when(pl.program_id(0) == steps - 1)
    def _():
        spectrum = gspec[...]
        high = spectrum.astype(bf16)
        low = (spectrum - high.astype(f32)).astype(bf16)
        grad_taps = nn(high, inv[...]) + nn(low, inv[...])
        tap = taps[...]
        grad_taps = grad_taps + tap * (2.0 * penalty_weight * share)
        positions = lax.broadcasted_iota(jnp.int32, (1, LEN), 1).astype(f32)
        decayed = grad_taps * jnp.exp(-column(cols, 4) * positions)
        high = decayed.astype(bf16)
        low = (decayed - high.astype(f32)).astype(bf16)
        sum_weight = (nt(feats[0], high) + nt(feats[1], high) + nt(feats[0], low)).astype(bf16)
        grad_decay = grad_taps * tap * (-positions)
        ones = jnp.ones((16, LEN), f32)
        line = lax.broadcasted_iota(jnp.int32, (16, D), 0)
        vectors = exact_nt(ones, gmask[...])
        vectors = jnp.where(line == 1, exact_nt(ones, ggain[...]), vectors)
        vectors = jnp.where(line == 2, exact_nt(ones, gskip[...]), vectors)
        vectors = jnp.where(line == 3, exact_nt(ones, grad_decay), vectors).astype(bf16)

        def write(dst, j):
            part = BS // 2
            few = ORDER // 2
            for y in range(2):
                lanes = slice(y * HALF, (y + 1) * HALF)
                b = 2 * y + j
                dst[y, 0:BS, :] = gir[b, :, :HALF].astype(bf16)
                dst[y, BS : 2 * BS, 0:BS] = gir[b, :, HALF:].astype(bf16)
                dst[y, BS : 2 * BS, BS:] = gil[b].astype(bf16)
                dst[y, 2 * BS : 3 * BS, 0:BS] = gol[b].astype(bf16)
                dst[y, 2 * BS : 3 * BS, BS:] = gor[b].astype(bf16)
                at = 3 * BS
                dst[y, at : at + part, :] = packed_dr[y, j * part : (j + 1) * part, :]
                at += part
                dst[y, at : at + few, :] = sum_weight[j * few : (j + 1) * few, lanes]
                at += few
                dst[y, at : at + 16, :] = vectors[:, lanes]
                dst[y, at + 16 :, :] = jnp.zeros((MIX_G - at - 16, HALF), bf16)

        core = s_ref[3]
        for c in range(2):

            @pl.when(core == c)
            def _():
                write(keep, c)
                write(send, 1 - c)


def mixer_backward(share, scalars, streams, constants, weights, finals):
    row_count = streams[0].shape[1]
    steps = row_count // BACK_TILE
    ins = list(streams) + list(constants) + list(weights) + list(finals)
    in_specs = [
        pl.BlockSpec((D, BACK_TILE), lambda i, s: (0, i)),
        pl.BlockSpec((2, D, BACK_TILE), lambda i, s: (0, 0, i)),
        pl.BlockSpec((5, D, BACK_TILE), lambda i, s: (0, 0, i)),
        pl.BlockSpec((8, BACK_TILE), lambda i, s: (0, i)),
        pl.BlockSpec((8, BACK_TILE), lambda i, s: (0, i)),
    ] + [whole(item.shape) for item in ins[5:]]
    half_shape = (2, MIX_G, HALF)
    outs = [
        jax.ShapeDtypeStruct((2 * row_count, HALF), f32),
        jax.ShapeDtypeStruct((row_count, HALF), bf16),
        jax.ShapeDtypeStruct(half_shape, bf16),
        jax.ShapeDtypeStruct(half_shape, bf16),
    ]
    out_specs = [
        pl.BlockSpec((BACK_TILE, HALF), lambda i, s: (s[0] * steps + i, 0)),
        pl.BlockSpec((BACK_TILE, HALF), lambda i, s: (i, 0)),
        whole(half_shape),
        whole(half_shape),
    ]
    scratch = [pltpu.VMEM(shape, f32) for shape in BACK_SHAPES]
    scratch += [
        pltpu.VMEM((D, BACK_TILE), bf16),
        pltpu.VMEM((D, BACK_TILE), bf16),
        pltpu.VMEM((D, BACK_TILE), bf16),
        pltpu.VMEM((D, BACK_TILE), f32),
        pltpu.VMEM((D, BACK_TILE), f32),
        pltpu.VMEM((3 * D, BACK_TILE), bf16),
    ]
    return pl.pallas_call(
        functools.partial(mixer_backward_kernel, steps=steps, share=share),
        out_shape=tuple(outs),
        grid_spec=pltpu.PrefetchScalarGridSpec(
            num_scalar_prefetch=1,
            grid=(steps,),
            in_specs=in_specs,
            out_specs=tuple(out_specs),
            scratch_shapes=scratch,
        ),
        compiler_params=pltpu.CompilerParams(vmem_limit_bytes=40 << 20),
        name="mixer_backward",
        cost_estimate=pl.CostEstimate(
            flops=row_count * 2 * 6000000, bytes_accessed=row_count * 20000, transcendentals=0
        ),
    )(scalars, *ins)


def place_parts(s_ref, parts, halves):
    quarter = parts[0].shape[0]
    few = quarter // 4
    for where, part in enumerate(parts):
        core = jnp.bitwise_xor(s_ref[3], where >> 1)
        start = jnp.bitwise_xor(s_ref[4], where & 1) * quarter
        for k in range(4):
            row = pl.multiple_of(start + jnp.bitwise_xor(s_ref[5], k) * few, few)
            halves[core, pl.ds(row, few), :] = part[k * few : (k + 1) * few, :]


def dense_unpack_kernel(s_ref, p0, p1, p2, p3, gain, ul, ur, dl, halves):
    place_parts(s_ref, (p0, p1, p2, p3), halves)
    part = BS // 2
    at = 6 * BS
    gain[...] = halves[0, at + part : at + part + 16, :].astype(f32)[0]
    for j in range(2):
        for c in range(4):
            ur[j, :, c * HALF : (c + 1) * HALF] = halves[j, c * BS : (c + 1) * BS, :].astype(f32)
        for c in range(2):
            dl[j, :, c * HALF : (c + 1) * HALF] = halves[
                j, (4 + c) * BS : (5 + c) * BS, :
            ].astype(f32)
        for lane in range(2):
            ul[lane, j * part : (j + 1) * part, :] = halves[
                j, at : at + part, lane * BS : (lane + 1) * BS
            ].astype(f32)


def mixer_unpack_kernel(s_ref, p0, p1, p2, p3, mask, gain, skip, decay, weight, il, ir, ol, orr, dr, halves):
    place_parts(s_ref, (p0, p1, p2, p3), halves)
    part = BS // 2
    few = ORDER // 2
    at = 3 * BS
    vectors = halves[0, at + part + few : at + part + few + 16, :].astype(f32)
    for index, dst in enumerate((mask, gain, skip, decay)):
        dst[...] = vectors[index]
    for j in range(2):
        ir[j, :, :HALF] = halves[j, 0:BS, :].astype(f32)
        ir[j, :, HALF:] = halves[j, BS : 2 * BS, :BS].astype(f32)
        il[j] = halves[j, BS : 2 * BS, BS:].astype(f32)
        ol[j] = halves[j, 2 * BS : 3 * BS, :BS].astype(f32)
        orr[j] = halves[j, 2 * BS : 3 * BS, BS:].astype(f32)
        for lane in range(2):
            dr[lane, j * part : (j + 1) * part, :] = halves[
                j, at : at + part, lane * BS : (lane + 1) * BS
            ].astype(f32)
        weight[j * few : (j + 1) * few, :] = halves[
            j, at + part : at + part + few, :
        ].astype(f32)


def unpack(kernel, scalars, parts, shapes, name):
    outs = tuple(jax.ShapeDtypeStruct(shape, f32) for shape in shapes)
    rows = 2 * parts[0].shape[0]
    return pl.pallas_call(
        kernel,
        out_shape=outs,
        grid_spec=pltpu.PrefetchScalarGridSpec(
            num_scalar_prefetch=1,
            grid=(1,),
            in_specs=[whole(item.shape) for item in parts],
            out_specs=tuple(whole(shape) for shape in shapes),
            scratch_shapes=[pltpu.VMEM((2, rows, HALF), bf16)],
        ),
        compiler_params=pltpu.CompilerParams(vmem_limit_bytes=16 << 20),
        name=name,
        cost_estimate=light(),
    )(scalars, *parts)


DENSE_OUTS = ((HALF,), (2, BS, BS), (2, BS, 2 * FB), (2, BS, FB))
MIXER_OUTS = (
    (HALF,),
    (HALF,),
    (HALF,),
    (HALF,),
    (ORDER, HALF),
    (2, BS, BS),
    (2, BS, 3 * BS),
    (2, BS, BS),
    (2, BS, BS),
    (2, BS, BS),
)


def corners_kernel(s_ref, *refs):
    for index in range(4):
        kept, got, out = refs[index], refs[4 + index], refs[8 + index]
        out[...] = (kept[...].astype(f32) + got[...].astype(f32)).astype(bf16)


def corners(scalars, kept, got):
    rows = kept.shape[1] // 2
    shape = jax.ShapeDtypeStruct((rows, HALF), bf16)

    def spec(over_y, over_x):
        def at(i, s):
            y = 1 - s[0] if over_y else s[0]
            x = 1 - s[4] if over_x else s[4]
            return (y, x, 0)

        return pl.BlockSpec((None, rows, HALF), at)

    specs = [spec(False, False), spec(False, True), spec(True, False), spec(True, True)]
    return pl.pallas_call(
        corners_kernel,
        out_shape=(shape,) * 4,
        grid_spec=pltpu.PrefetchScalarGridSpec(
            num_scalar_prefetch=1,
            grid=(1,),
            in_specs=specs + specs,
            out_specs=(whole((rows, HALF)),) * 4,
        ),
        compiler_params=pltpu.CompilerParams(vmem_limit_bytes=16 << 20),
        name="sum_corners",
        cost_estimate=light(),
    )(scalars, *([kept] * 4 + [got] * 4))


def columns_kernel(s_ref, a, b, c, d, own, one, two, three, total):
    total[...] = (
        a[...].astype(f32) + b[...].astype(f32) + c[...].astype(f32) + d[...].astype(f32)
    )
    few = total.shape[0] // 4
    for k, out in enumerate((own, one, two, three)):
        row = pl.multiple_of(jnp.bitwise_xor(s_ref[5], k) * few, few)
        out[...] = total[pl.ds(row, few), :].astype(bf16)


def columns(scalars, parts):
    rows = parts[0].shape[0]
    shape = jax.ShapeDtypeStruct((rows // 4, HALF), bf16)
    return pl.pallas_call(
        columns_kernel,
        out_shape=(shape,) * 4,
        grid_spec=pltpu.PrefetchScalarGridSpec(
            num_scalar_prefetch=1,
            grid=(1,),
            in_specs=[whole((rows, HALF))] * 4,
            out_specs=(whole((rows // 4, HALF)),) * 4,
            scratch_shapes=[pltpu.VMEM((rows, HALF), f32)],
        ),
        compiler_params=pltpu.CompilerParams(vmem_limit_bytes=12 << 20),
        name="sum_columns",
        cost_estimate=light(),
    )(scalars, *parts)


def swap_narrow(values):
    return lax.ppermute(values, "narrow", [(0, 1), (1, 0)])


def swap_wide(values, bit, size):
    return lax.ppermute(values, "wide", [(i, i ^ (1 << bit)) for i in range(size)])


def swap_both(values, bit, size):
    flip = 2 << bit
    return lax.ppermute(
        values, ("wide", "narrow"), [(i, i ^ flip ^ 1) for i in range(2 * size)]
    )


def shift_wide(values, flip, size):
    return lax.ppermute(values, "wide", [(i, i ^ flip) for i in range(size)])


def add_low(*items):
    total = items[0].astype(f32)
    for item in items[1:]:
        total = total + item.astype(f32)
    return total.astype(bf16)


def over_corners(parts, size):
    own, over_x, over_y, over_both = parts
    return (
        own,
        swap_wide(over_x, 1, size),
        swap_narrow(over_y),
        swap_both(over_both, 1, size),
    )


def over_columns(parts, size):
    own, *others = parts
    return (own,) + tuple(
        shift_wide(item, (k + 1) << 2, size) for k, item in enumerate(others)
    )


def sum_columns(parts, size):
    packed = add_low(*parts)
    bit = 4
    while 1 << bit < size:
        packed = add_low(packed, swap_wide(packed, bit, size))
        bit += 1
    return packed


def along_columns(packed, size):
    return (packed,) + tuple(shift_wide(packed, k << 2, size) for k in (1, 2, 3))


def tie(*groups):
    held = lax.optimization_barrier(groups)
    return held


def over_cores(near, far, size):
    return (near, far, swap_wide(near, 0, size), swap_wide(far, 0, size))


def gather_chips(piece, size):
    near = swap_narrow(piece)
    high = swap_wide(near, 2, size)
    return near, swap_wide(near, 1, size), high


def gather_cores(items, size):
    pieces = []
    for item in items:
        pieces += [item, swap_wide(item, 0, size)]
    return tuple(pieces)


def on_device(
    wide_size,
    tokens,
    lengths,
    mask_pos,
    mask_vector,
    norm1_gain,
    in_left,
    in_right,
    filter_weight,
    decay,
    skip_gain,
    out_left,
    out_right,
    norm2_gain,
    up_left,
    up_right,
    down_left,
    down_right,
    cotangent,
):
    index = lax.axis_index("wide")
    side = lax.axis_index("narrow")
    row_count = tokens.shape[0] // 2
    scalars = jnp.stack(
        [side, index & 3, (index >> 2) & 1, index & 1, (index >> 1) & 1, (index >> 2) & 3]
    ).astype(jnp.int32)
    share = 1.0 / (2 * wide_size)

    def sent_rows(values):
        return lax.dynamic_slice_in_dim(values, (1 - side) * row_count, row_count, 0)

    mixer_weights = (in_left, in_right, out_left, out_right)
    dense_weights = (up_left, up_right, jnp.swapaxes(down_left, 1, 2), down_right)
    vectors = (mask_vector, norm1_gain, norm2_gain, skip_gain, decay)
    mix_piece, ffn_piece = pack_weights(
        scalars, mixer_weights, dense_weights, filter_weight, vectors
    )
    mix_chips = gather_chips(mix_piece, wide_size)
    mix_chips += (swap_wide(mix_chips[2], 1, wide_size),)
    mix_pieces = gather_cores(mix_chips, wide_size)
    ffn_chips = gather_chips(ffn_piece, wide_size)
    tokens_other = swap_narrow(sent_rows(tokens))
    cot_other = swap_narrow(sent_rows(cotangent))

    positions = jnp.arange(LEN, dtype=jnp.int32)
    valid = (positions[None, :] < lengths[:, None]).astype(f32)
    masked = jnp.any(mask_pos[:, :, None] == positions[None, None, :], axis=1).astype(f32)
    marks = jnp.stack([valid, masked]).reshape(2, 2, row_count)
    marks = lax.dynamic_index_in_dim(marks, side, 1, keepdims=False)
    marks = jnp.concatenate([marks, jnp.zeros((6, row_count), f32)], axis=0)

    fwd, inv = (jnp.asarray(item) for item in transform_tables())
    feats = jnp.asarray(feature_parts())
    taps, spec, penalty, cols = filter_call(
        scalars, filter_weight, mix_piece, mix_pieces, feats, fwd
    )

    ffn_chips, spec = tie(ffn_chips, spec)
    ffn_last = swap_wide(ffn_chips[2], 1, wide_size)
    middle, first, kept, scale, *full = mixer_forward(
        scalars, tokens, tokens_other, marks, cols, spec, fwd, inv, mixer_weights + mix_pieces
    )
    middle, penalty, ffn_last = tie(middle, penalty, ffn_last)
    ffn_pieces = gather_cores(ffn_chips + (ffn_last,), wide_size)
    output, output_sent, grad_middle, ffn_keep, ffn_send, packed_dr = dense(
        scalars, middle, cotangent, cot_other, cols, dense_weights + ffn_pieces
    )
    ffn_parts = corners(scalars, ffn_keep, swap_wide(ffn_send, 0, wide_size))
    grad_middle, ffn_parts, penalty = tie(grad_middle, ffn_parts, penalty[0, 0])
    ffn_parts = over_corners(ffn_parts, wide_size)
    tokens_grad, grad_sent, mix_keep, mix_send = mixer_backward(
        share,
        scalars,
        (grad_middle, first, kept, scale, marks),
        (cols, spec, fwd, inv),
        full,
        (taps, feats, packed_dr),
    )
    mix_keep, mix_send, ffn_parts = tie(mix_keep, mix_send, ffn_parts)
    mix_got = swap_wide(mix_send, 0, wide_size)
    ffn_parts = columns(scalars, ffn_parts)
    mix_parts = corners(scalars, mix_keep, mix_got)

    ffn_parts = over_columns(ffn_parts, wide_size)
    mix_parts = over_corners(mix_parts, wide_size)
    ffn_sum = sum_columns(ffn_parts, wide_size)
    ffn_parts = along_columns(ffn_sum, wide_size)
    mix_parts = columns(scalars, mix_parts)
    mix_parts, grad_sent, output_sent = tie(mix_parts, grad_sent, output_sent)
    output_other = swap_narrow(output_sent)
    grad_other = swap_narrow(grad_sent)
    mix_parts = over_columns(mix_parts, wide_size)
    mix_sum = sum_columns(mix_parts, wide_size)
    ffn_near = jnp.concatenate(ffn_parts, axis=0)
    mix_sum, ffn_near, output_other = tie(mix_sum, ffn_near, output_other)
    mix_parts = along_columns(mix_sum, wide_size)
    ffn_far = swap_wide(ffn_near, 1, wide_size)
    mix_near = jnp.concatenate(mix_parts, axis=0)
    mix_far = swap_wide(mix_near, 1, wide_size)
    ffn_parts = over_cores(ffn_near, ffn_far, wide_size)
    gain_two, g_ul, g_ur, g_dl = unpack(
        dense_unpack_kernel, scalars, ffn_parts, DENSE_OUTS, "dense_unpack"
    )
    start = (1 - side) * row_count
    output = lax.dynamic_update_slice_in_dim(output, output_other, start, 0)
    tokens_grad = lax.dynamic_update_slice_in_dim(tokens_grad, grad_other.astype(f32), start, 0)
    mix_far, gain_two, g_ul, g_ur, g_dl, output, tokens_grad = tie(
        mix_far, gain_two, g_ul, g_ur, g_dl, output, tokens_grad
    )
    mix_parts = over_cores(mix_near, mix_far, wide_size)
    g_mask, g_gain, g_skip, g_decay, g_filter, g_il, g_ir, g_ol, g_or, g_dr = unpack(
        mixer_unpack_kernel, scalars, mix_parts, MIXER_OUTS, "mixer_unpack"
    )
    return (
        output,
        tokens_grad,
        g_mask,
        g_gain,
        g_il,
        g_ir,
        g_filter,
        g_decay,
        g_skip,
        g_ol,
        g_or,
        gain_two,
        g_ul,
        g_ur,
        jnp.swapaxes(g_dl, 1, 2),
        g_dr,
        penalty,
    )


def solution(mesh):
    placed = (
        P("wide", "narrow"),
        P("wide"),
        P("wide", None),
        P("narrow"),
        P("narrow"),
        P("narrow", None, None),
        P("narrow", None, None),
        P(None, "narrow"),
        P("narrow"),
        P("narrow"),
        P("narrow", None, None),
        P("narrow", None, None),
        P("narrow"),
        P("narrow", None, None),
        P("narrow", None, None),
        P("narrow", None, None),
        P("narrow", None, None),
        P("wide", "narrow"),
    )
    return jax.shard_map(
        functools.partial(on_device, mesh.shape["wide"]),
        mesh=mesh,
        in_specs=placed,
        out_specs=(
            P("wide", "narrow"),
            P("wide", "narrow"),
            P("narrow"),
            P("narrow"),
            P("narrow", None, None),
            P("narrow", None, None),
            P(None, "narrow"),
            P("narrow"),
            P("narrow"),
            P("narrow", None, None),
            P("narrow", None, None),
            P("narrow"),
            P("narrow", None, None),
            P("narrow", None, None),
            P("narrow", None, None),
            P("narrow", None, None),
            P(),
        ),
        check_vma=False,
    )
```

```python
import functools

import jax
import jax.numpy as jnp
import numpy as np
from jax import lax
from jax.experimental import pallas as pl
from jax.experimental.pallas import tpu as pltpu
from jax.sharding import PartitionSpec as P

D = 768
NB = 4
ORDER = 128
LEN = 128
BS = 192
FB = 768
GROUP = BS // NB
HALF = D // 2
QUARTER = BS // 4

epsilon = 1e-05
penalty_weight = 0.005

bf16 = jnp.bfloat16
f32 = jnp.float32

TILE = 512
BACK_TILE = 256
VMEM = 60 << 20

FILTER_ROW = 3 * QUARTER
VECTOR_ROW = FILTER_ROW + ORDER // 8
MIX_W = VECTOR_ROW + 16
FFN_W = 7 * QUARTER
FFN_G = 1280
MIX_G = 768


def transform_tables():
    t = np.arange(LEN, dtype=np.float64)[:, None]
    k = np.arange(LEN, dtype=np.float64)[None, :]
    angle = np.pi * (2 * k + 1) * t / (2 * LEN)
    forward = np.concatenate([np.cos(angle), np.sin(angle)], axis=1)
    return forward.astype(bf16), (forward.T / LEN).astype(bf16)


def feature_parts():
    t = np.arange(LEN, dtype=np.float64)[None, :]
    freqs = (np.arange(ORDER // 2, dtype=np.float64)[:, None] + 1.0) * (3.1 / (ORDER // 2))
    table = np.concatenate([np.sin(t * freqs), np.cos(t * freqs)], axis=0)
    parts = []
    for _ in range(3):
        part = table.astype(bf16)
        parts.append(part)
        table = table - part.astype(np.float64)
    return np.stack(parts)


def nn(a, b):
    return lax.dot_general(a, b, (((1,), (0,)), ((), ())), preferred_element_type=f32)


def nt(a, b):
    return lax.dot_general(a, b, (((1,), (1,)), ((), ())), preferred_element_type=f32)


def tn(a, b):
    return lax.dot_general(a, b, (((0,), (0,)), ((), ())), preferred_element_type=f32)


def exact_nt(a, b):
    return lax.dot_general(
        a,
        b,
        (((1,), (1,)), ((), ())),
        preferred_element_type=f32,
        precision=lax.Precision.HIGHEST,
    )


def fold(values):
    out = values[:, :LEN]
    for start in range(LEN, values.shape[1], LEN):
        out = out + values[:, start : start + LEN]
    return out


def light():
    return pl.CostEstimate(flops=0, bytes_accessed=1 << 20, transcendentals=0)


def rows_of(block, size):
    return pl.ds(pl.multiple_of(block * size, size), size)


def column(cols_ref, index):
    return cols_ref[:, index : index + 1]


def place_halves(dst_ref, side, own, other):
    dst_ref[rows_of(side, HALF), :] = own
    dst_ref[rows_of(1 - side, HALF), :] = other


def regroup(dst_ref, block, values):
    for g in range(NB):
        dst_ref[g * BS + block * GROUP : g * BS + (block + 1) * GROUP, :] = values[
            g * GROUP : (g + 1) * GROUP, :
        ]


def block(ref, index, size=BS):
    return ref[index * size : (index + 1) * size, :]


def norm_stats(values):
    center = values - jnp.sum(values, axis=0, keepdims=True) * (1.0 / D)
    spread = jnp.sum(center * center, axis=0, keepdims=True) * (1.0 / D)
    scale_row = lax.rsqrt(spread + epsilon)
    return center * scale_row, scale_row


def norm_back(grad, normed, scale_row, gain):
    scaled = grad * gain
    first = jnp.sum(scaled, axis=0, keepdims=True) * (1.0 / D)
    second = jnp.sum(scaled * normed, axis=0, keepdims=True) * (1.0 / D)
    return scale_row * (scaled - first - normed * second)


def pack_kernel(
    s_ref, il, ir, ol, orr, ul, ur, dl, dr, weight, mask, gain1, gain2, skip, decay, mix_ref, ffn_ref
):
    q = QUARTER
    mix_ref[0:q, :] = jnp.concatenate([il[0], ol[0]], axis=1)
    mix_ref[q : 2 * q, :] = ir[0][:, :HALF]
    mix_ref[2 * q : 3 * q, :] = jnp.concatenate([ir[0][:, HALF:], orr[0]], axis=1)
    mix_ref[FILTER_ROW:VECTOR_ROW, :] = weight[...]
    rest = decay[...].reshape(1, HALF)
    rows = [item[...].reshape(1, HALF).astype(f32) for item in (mask, gain1, gain2, skip)]
    for _ in range(3):
        part = rest.astype(bf16).astype(f32)
        rows.append(part)
        rest = rest - part
    line = lax.broadcasted_iota(jnp.int32, (16, HALF), 0)
    vectors = jnp.zeros((16, HALF), f32)
    for index, row in enumerate(rows):
        vectors = jnp.where(line == index, row, vectors)
    mix_ref[VECTOR_ROW:, :] = vectors.astype(bf16)
    for c in range(4):
        ffn_ref[c * q : (c + 1) * q, :] = ur[0][:, c * HALF : (c + 1) * HALF]
    for c in range(2):
        ffn_ref[(4 + c) * q : (5 + c) * q, :] = dl[0][:, c * HALF : (c + 1) * HALF]
    ffn_ref[6 * q : 7 * q, :] = jnp.concatenate([ul[0], dr[0]], axis=1)


def pack_weights(scalars, mixer_weights, dense_weights, filter_weight, vectors):
    def eighth(item):
        return pl.BlockSpec((1, QUARTER, item.shape[2]), lambda i, s: (s[2], s[1], 0))

    return pl.pallas_call(
        pack_kernel,
        out_shape=(
            jax.ShapeDtypeStruct((MIX_W, HALF), bf16),
            jax.ShapeDtypeStruct((FFN_W, HALF), bf16),
        ),
        grid_spec=pltpu.PrefetchScalarGridSpec(
            num_scalar_prefetch=1,
            grid=(1,),
            in_specs=[eighth(item) for item in mixer_weights + dense_weights]
            + [pl.BlockSpec((ORDER // 8, HALF), lambda i, s: (4 * s[2] + s[1], 0))]
            + [whole(item.shape) for item in vectors],
            out_specs=(whole((MIX_W, HALF)), whole((FFN_W, HALF))),
        ),
        name="pack_weights",
        cost_estimate=light(),
    )(scalars, *mixer_weights, *dense_weights, filter_weight, *vectors)


def own_blocks(dst, side, src):
    for j in range(2):
        dst[2 * side + j] = src[j]


def filter_kernel(
    s_ref, own, mine, *refs
):
    pieces = refs[:8]
    feats, fwd, taps_ref, spec_ref, pen_ref, cols_ref, weight = refs[8:]
    side = s_ref[0]
    q = ORDER // 8
    for p, piece in enumerate(pieces):
        place = 4 * jnp.bitwise_xor(s_ref[2], p >> 2) + jnp.bitwise_xor(s_ref[1], p & 3)
        weight[pl.ds(pl.multiple_of(place * q, q), q), :] = piece[FILTER_ROW:VECTOR_ROW, :]
    for which, src, rows in ((side, own, mine), (1 - side, weight, pieces[0])):
        table = src[...]
        basis = tn(table, feats[2]) + tn(table, feats[1]) + tn(table, feats[0])
        taps_ref[rows_of(which, HALF), :] = basis
        vectors = rows[VECTOR_ROW:, :].astype(f32)
        vectors = jnp.concatenate([vectors, jnp.zeros((LEN - 16, HALF), f32)], axis=0)
        vectors = vectors.T
        lane = lax.broadcasted_iota(jnp.int32, (HALF, LEN), 1)
        decay = vectors[:, 4:5] + vectors[:, 5:6] + vectors[:, 6:7]
        cols_ref[rows_of(which, HALF), :] = jnp.where(lane == 4, decay, vectors)
    positions = lax.broadcasted_iota(jnp.int32, (1, LEN), 1).astype(f32)
    taps = taps_ref[...] * jnp.exp(-column(cols_ref, 4) * positions)
    taps_ref[...] = taps
    spec_ref[...] = nn(taps.astype(bf16), fwd[...])
    total = jnp.sum(jnp.sum(taps * taps, axis=0, keepdims=True), axis=1, keepdims=True)
    pen_ref[...] = jnp.broadcast_to(total * penalty_weight, (8, LEN))


def whole(shape):
    return pl.BlockSpec(shape, lambda *_: (0,) * len(shape))


def filter_call(scalars, own, mine, pieces, feats, fwd):
    ins = (own, mine) + tuple(pieces) + (feats, fwd)
    outs = (
        jax.ShapeDtypeStruct((D, LEN), f32),
        jax.ShapeDtypeStruct((D, 2 * LEN), f32),
        jax.ShapeDtypeStruct((8, LEN), f32),
        jax.ShapeDtypeStruct((D, LEN), f32),
    )
    return pl.pallas_call(
        filter_kernel,
        out_shape=outs,
        grid_spec=pltpu.PrefetchScalarGridSpec(
            num_scalar_prefetch=1,
            grid=(1,),
            in_specs=[whole(item.shape) for item in ins],
            out_specs=tuple(whole(item.shape) for item in outs),
            scratch_shapes=[pltpu.VMEM((ORDER, HALF), bf16)],
        ),
        name="filter_spectrum",
        cost_estimate=light(),
    )(scalars, *ins)


def mixer_forward_kernel(
    s_ref,
    own,
    oth,
    marks,
    cols,
    spec,
    fwd,
    inv,
    il,
    ir,
    ol,
    orr,
    *refs,
):
    pieces = refs[:8]
    middle, first, kept, scale, wil, wir, wol, wor, enter, half, conv = refs[8:]
    side = s_ref[0]

    @pl.when(pl.program_id(0) == 0)
    def _():
        other = 1 - side
        own_blocks(wil, side, il)
        own_blocks(wir, side, ir)
        own_blocks(wol, side, ol)
        own_blocks(wor, side, orr)
        q = QUARTER
        for p, piece in enumerate(pieces):
            at = pl.ds(pl.multiple_of(jnp.bitwise_xor(s_ref[1], p & 3) * q, q), q)
            blk = 2 * other + jnp.bitwise_xor(s_ref[2], p >> 2)
            wil[blk, at, :] = piece[0:q, :BS]
            wol[blk, at, :] = piece[0:q, BS:]
            wir[blk, at, 0:HALF] = piece[q : 2 * q, :]
            wir[blk, at, HALF:] = piece[2 * q : 3 * q, :BS]
            wor[blk, at, :] = piece[2 * q : 3 * q, BS:]

    place_halves(enter, side, own[...].T.astype(f32), oth[...].T.astype(f32))
    valid = marks[0:1, :]
    masked = marks[1:2, :]
    tokens = enter[...]
    entered = tokens + masked * (column(cols, 0) - tokens)
    enter[...] = entered
    normed, scale_row = norm_stats(entered)
    scale[...] = jnp.broadcast_to(scale_row, scale.shape)
    half[...] = (normed * column(cols, 1)).astype(bf16)
    first[0] = half[...]
    for b in range(NB):
        regroup(first.at[1], b, tn(wil[b], block(half, b)).astype(bf16))
    for g in range(NB):
        projected = tn(wir[g], block(first.at[1], g))
        rows = slice(g * BS, (g + 1) * BS)
        for part in range(3):
            kept[part, rows, :] = projected[part * BS : (part + 1) * BS, :].astype(bf16)
        source = (projected[:BS] * projected[2 * BS :] * valid).astype(bf16)
        half[rows, :] = source
    for s in range(TILE // LEN):
        lanes = slice(s * LEN, (s + 1) * LEN)
        wave = nn(half[:, lanes], fwd[...])
        wc, ws = wave[:, :LEN], wave[:, LEN:]
        hc, hs = spec[:, :LEN], spec[:, LEN:]
        product = jnp.concatenate(
            [(wc * hc - ws * hs).astype(bf16), (wc * hs + ws * hc).astype(bf16)], axis=1
        )
        conv[:, lanes] = nn(product, inv[...])
    inner = conv[...] + column(cols, 3) * half[...].astype(f32)
    kept[3] = inner.astype(bf16)
    half[...] = (kept[1].astype(f32) * inner).astype(bf16)
    for b in range(NB):
        regroup(kept.at[4], b, tn(wol[b], block(half, b)).astype(bf16))
    for g in range(NB):
        rows = slice(g * BS, (g + 1) * BS)
        middle[rows, :] = (enter[rows, :] + tn(wor[g], block(kept.at[4], g))).astype(bf16)


def mixer_forward(scalars, own, oth, marks, cols, spec, fwd, inv, weights):
    row_count = own.shape[0] // 2
    steps = row_count // TILE
    ins = (own, oth, marks, cols, spec, fwd, inv) + tuple(weights)
    in_specs = [
        pl.BlockSpec((TILE, HALF), lambda i, s: (s[0] * steps + i, 0)),
        pl.BlockSpec((TILE, HALF), lambda i, s: (i, 0)),
        pl.BlockSpec((8, TILE), lambda i, s: (0, i)),
    ] + [whole(item.shape) for item in ins[3:]]
    full = [(NB, BS, BS), (NB, BS, 3 * BS), (NB, BS, BS), (NB, BS, BS)]
    outs = [
        jax.ShapeDtypeStruct((D, row_count), bf16),
        jax.ShapeDtypeStruct((2, D, row_count), bf16),
        jax.ShapeDtypeStruct((5, D, row_count), bf16),
        jax.ShapeDtypeStruct((8, row_count), f32),
    ] + [jax.ShapeDtypeStruct(shape, bf16) for shape in full]
    out_specs = [
        pl.BlockSpec((D, TILE), lambda i, s: (0, i)),
        pl.BlockSpec((2, D, TILE), lambda i, s: (0, 0, i)),
        pl.BlockSpec((5, D, TILE), lambda i, s: (0, 0, i)),
        pl.BlockSpec((8, TILE), lambda i, s: (0, i)),
    ] + [whole(shape) for shape in full]
    return pl.pallas_call(
        mixer_forward_kernel,
        out_shape=tuple(outs),
        grid_spec=pltpu.PrefetchScalarGridSpec(
            num_scalar_prefetch=1,
            grid=(steps,),
            in_specs=in_specs,
            out_specs=tuple(out_specs),
            scratch_shapes=[
                pltpu.VMEM((D, TILE), f32),
                pltpu.VMEM((D, TILE), bf16),
                pltpu.VMEM((D, TILE), f32),
            ],
        ),
        compiler_params=pltpu.CompilerParams(vmem_limit_bytes=VMEM),
        name="mixer_forward",
        cost_estimate=pl.CostEstimate(
            flops=row_count * 2 * 1500000, bytes_accessed=row_count * 20000, transcendentals=0
        ),
    )(scalars, *ins)


ACC_SHAPES = ((NB, BS, 2 * FB), (NB, BS, FB), (NB, BS, BS), (NB, BS, BS), (D, LEN))


def dense_kernel(
    s_ref,
    middle,
    own,
    oth,
    cols,
    ul,
    ur,
    dl,
    dr,
    p0,
    p1,
    p2,
    p3,
    p4,
    p5,
    p6,
    p7,
    out_own,
    out_send,
    grad_middle,
    keep,
    send,
    packed_dr,
    wul,
    wur,
    wdl,
    wdr,
    gur,
    gdl,
    gul,
    gdr,
    ggain,
    top,
    half,
    moved3,
    moved4,
    hid,
    act,
    slope,
    gated,
    back,
    outs,
    *,
    steps,
):
    side = s_ref[0]

    @pl.when(pl.program_id(0) == 0)
    def _():
        other = 1 - side
        own_blocks(wul, side, ul)
        own_blocks(wur, side, ur)
        own_blocks(wdl, side, dl)
        own_blocks(wdr, side, dr)
        q = QUARTER
        for p, piece in enumerate((p0, p1, p2, p3, p4, p5, p6, p7)):
            row = pl.multiple_of(jnp.bitwise_xor(s_ref[1], p & 3) * q, q)
            at = pl.ds(row, q)
            blk = 2 * other + jnp.bitwise_xor(s_ref[2], p >> 2)
            for c in range(4):
                wur[blk, at, c * HALF : (c + 1) * HALF] = piece[c * q : (c + 1) * q, :]
            for c in range(2):
                wdl[blk, at, c * HALF : (c + 1) * HALF] = piece[(4 + c) * q : (5 + c) * q, :]
            wul[blk, at, :] = piece[6 * q : 7 * q, :BS]
            wdr[blk, at, :] = piece[6 * q : 7 * q, BS:]
        for acc in (gur, gdl, gul, gdr, ggain):
            acc[...] = jnp.zeros(acc.shape, f32)

    gain = column(cols, 2)
    normed, scale_row = norm_stats(middle[...].astype(f32))
    half[...] = (normed * gain).astype(bf16)
    for b in range(NB):
        regroup(moved3, b, tn(wul[b], block(half, b)).astype(bf16))
    for g in range(NB):
        rows = slice(g * FB, (g + 1) * FB)
        both = tn(wur[g], block(moved3, g))
        gate, up = both[:FB], both[FB:]
        chance = 0.5 + 0.5 * lax.erf(gate * 0.7071067811865476)
        density = jnp.exp(gate * gate * -0.5 - 0.9189385332046727)
        active = gate * chance
        hid[rows, :] = (active * up).astype(bf16)
        act[rows, :] = active.astype(bf16)
        slope[rows, :] = (up * (chance + gate * density)).astype(bf16)
        regroup(moved4, g, nn(wdl[g], hid[rows, :]).astype(bf16))
    for g in range(NB):
        rows = slice(g * BS, (g + 1) * BS)
        outs[rows, :] = (middle[rows, :].astype(f32) + tn(wdr[g], block(moved4, g))).astype(bf16)
    out_own[...] = outs[rows_of(side, HALF), :].T
    out_send[...] = outs[rows_of(1 - side, HALF), :].T
    place_halves(top, side, own[...].T, oth[...].T)
    for g in range(NB):
        grad = block(top, g)
        regroup(back, g, nn(wdr[g], grad).astype(bf16))
        gdr[g] += nt(block(moved4, g), grad)
    for b in range(NB):
        rows = slice(b * FB, (b + 1) * FB)
        returned = block(back, b)
        grad_hidden = tn(wdl[b], returned)
        gdl[b] += nt(returned, hid[rows, :])
        lowered = grad_hidden.astype(bf16)
        gated[:FB, :] = lowered * slope[rows, :]
        gated[FB:, :] = lowered * act[rows, :]
        moved = block(moved3, b)
        gur[b] += nt(moved, gated[...])
        regroup(moved4, b, nn(wur[b], gated[...]).astype(bf16))
    grads = []
    for b in range(NB):
        returned = block(moved4, b)
        grads.append(nn(wul[b], returned))
        gul[b] += nt(block(half, b), returned)
    grad_in = jnp.concatenate(grads, axis=0)
    ggain[...] += fold(grad_in * normed)
    grad_middle[...] = (
        top[...].astype(f32) + norm_back(grad_in, normed, scale_row, gain)
    ).astype(bf16)

    @pl.when(pl.program_id(0) == steps - 1)
    def _():
        lane = lax.broadcasted_iota(jnp.int32, (D, LEN), 1)
        sums = jnp.where(lane == 0, jnp.sum(ggain[...], axis=1, keepdims=True), 0.0)
        sums = sums.T[:16, :].astype(bf16)

        def write(dst, j):
            part = BS // 2
            for y in range(2):
                b = 2 * y + j
                for c in range(4):
                    dst[y, c * BS : (c + 1) * BS, :] = gur[b, :, c * HALF : (c + 1) * HALF].astype(
                        bf16
                    )
                for c in range(2):
                    at = (4 + c) * BS
                    dst[y, at : at + BS, :] = gdl[b, :, c * HALF : (c + 1) * HALF].astype(bf16)
                at = 6 * BS
                for lane in range(2):
                    dst[y, at : at + part, lane * BS : (lane + 1) * BS] = gul[
                        2 * y + lane, j * part : (j + 1) * part, :
                    ].astype(bf16)
                at += part
                dst[y, at : at + 16, :] = sums[:, y * HALF : (y + 1) * HALF]
                dst[y, at + 16 :, :] = jnp.zeros((FFN_G - at - 16, HALF), bf16)

        core = s_ref[3]
        for c in range(2):

            @pl.when(core == c)
            def _():
                write(keep, c)
                write(send, 1 - c)

        for y in range(2):
            for j in range(2):
                packed_dr[y, :, j * BS : (j + 1) * BS] = gdr[2 * y + j].astype(bf16)


def dense(scalars, middle, own, oth, cols, weights):
    row_count = own.shape[0] // 2
    steps = row_count // TILE

    def own_rows(i, s):
        return (s[0] * steps + i, 0)

    ins = [middle, own, oth, cols] + list(weights)
    in_specs = [
        pl.BlockSpec((D, TILE), lambda i, s: (0, i)),
        pl.BlockSpec((TILE, HALF), own_rows),
        pl.BlockSpec((TILE, HALF), lambda i, s: (i, 0)),
        whole(cols.shape),
    ] + [whole(item.shape) for item in weights]
    half_shape = (2, FFN_G, HALF)
    outs = [
        jax.ShapeDtypeStruct((2 * row_count, HALF), bf16),
        jax.ShapeDtypeStruct((row_count, HALF), bf16),
        jax.ShapeDtypeStruct((D, row_count), bf16),
        jax.ShapeDtypeStruct(half_shape, bf16),
        jax.ShapeDtypeStruct(half_shape, bf16),
        jax.ShapeDtypeStruct((2, BS, HALF), bf16),
    ]
    out_specs = [
        pl.BlockSpec((TILE, HALF), own_rows),
        pl.BlockSpec((TILE, HALF), lambda i, s: (i, 0)),
        pl.BlockSpec((D, TILE), lambda i, s: (0, i)),
        whole(half_shape),
        whole(half_shape),
        whole((2, BS, HALF)),
    ]
    full = [(NB, BS, BS), (NB, BS, 2 * FB), (NB, BS, FB), (NB, BS, BS)]
    scratch = [pltpu.VMEM(shape, bf16) for shape in full]
    scratch += [pltpu.VMEM(shape, f32) for shape in ACC_SHAPES]
    scratch += [pltpu.VMEM((D, TILE), bf16) for _ in range(4)]
    scratch += [pltpu.VMEM((NB * FB, TILE), bf16) for _ in range(3)]
    scratch += [pltpu.VMEM((2 * FB, TILE), bf16)]
    scratch += [pltpu.VMEM((D, TILE), bf16) for _ in range(2)]
    return pl.pallas_call(
        functools.partial(dense_kernel, steps=steps),
        out_shape=tuple(outs),
        grid_spec=pltpu.PrefetchScalarGridSpec(
            num_scalar_prefetch=1,
            grid=(steps,),
            in_specs=in_specs,
            out_specs=tuple(out_specs),
            scratch_shapes=scratch,
        ),
        compiler_params=pltpu.CompilerParams(vmem_limit_bytes=46 << 20),
        name="dense",
        cost_estimate=pl.CostEstimate(
            flops=row_count * 2 * 8000000, bytes_accessed=row_count * 10000, transcendentals=0
        ),
    )(scalars, *ins)


BACK_SHAPES = (
    (NB, BS, BS),
    (NB, BS, BS),
    (D, LEN),
    (D, 2 * LEN),
    (NB, BS, 3 * BS),
    (NB, BS, BS),
    (D, LEN),
    (D, LEN),
)


def mixer_backward_kernel(
    s_ref,
    grad_middle,
    first,
    kept,
    scale,
    marks,
    cols,
    spec,
    fwd,
    inv,
    wil,
    wir,
    wol,
    wor,
    taps,
    feats,
    packed_dr,
    out_own,
    out_send,
    keep,
    send,
    gol,
    gor,
    gskip,
    gspec,
    gir,
    gil,
    gmask,
    ggain,
    back,
    half,
    conv,
    inner_grad,
    total,
    proj,
    *,
    steps,
    share,
):
    side = s_ref[0]

    @pl.when(pl.program_id(0) == 0)
    def _():
        for acc in (gol, gor, gskip, gspec, gir, gil, gmask, ggain):
            acc[...] = jnp.zeros(acc.shape, f32)

    valid = marks[0:1, :]
    for g in range(NB):
        grad = block(grad_middle, g)
        regroup(back, g, nn(wor[g], grad).astype(bf16))
        gor[g] += nt(block(kept.at[4], g), grad)
    for b in range(NB):
        rows = slice(b * BS, (b + 1) * BS)
        returned = block(back, b)
        grad_mixed = nn(wol[b], returned)
        gate = kept[1, rows, :].astype(f32)
        inner = kept[3, rows, :].astype(f32)
        gol[b] += nt(kept[1, rows, :] * kept[3, rows, :], returned)
        grad_inner = grad_mixed * gate
        inner_grad[rows, :] = grad_inner
        conv[rows, :] = grad_inner.astype(bf16)
        proj[b * 3 * BS + BS : b * 3 * BS + 2 * BS, :] = (grad_mixed * inner).astype(bf16)
        source = kept[0, rows, :] * kept[2, rows, :] * valid.astype(bf16)
        half[rows, :] = source
        gskip[rows, :] += fold(grad_inner * source.astype(f32))
    hc, hs = spec[:, :LEN], spec[:, LEN:]
    for s in range(BACK_TILE // LEN):
        lanes = slice(s * LEN, (s + 1) * LEN)
        wave = nn(jnp.concatenate([conv[:, lanes], half[:, lanes]], axis=0), fwd[...])
        wc, ws = wave[:D, :LEN], wave[:D, LEN:]
        seen = wave[D:]
        sc, ss = seen[:, :LEN], seen[:, LEN:]
        gspec[:, :LEN] += wc * sc + ws * ss
        gspec[:, LEN:] += ws * sc - wc * ss
        product = jnp.concatenate(
            [(wc * hc + ws * hs).astype(bf16), (ws * hc - wc * hs).astype(bf16)], axis=1
        )
        total[:, lanes] = nn(product, inv[...])
    for g in range(NB):
        rows = slice(g * BS, (g + 1) * BS)
        grad_source = ((total[rows, :] + cols[rows, 3:4] * inner_grad[rows, :]) * valid).astype(bf16)
        start = g * 3 * BS
        proj[start : start + BS, :] = grad_source * kept[2, rows, :]
        proj[start + 2 * BS : start + 3 * BS, :] = grad_source * kept[0, rows, :]

    masked = marks[1:2, :]
    for g in range(NB):
        grad = proj[g * 3 * BS : (g + 1) * 3 * BS, :]
        regroup(back, g, nn(wir[g], grad).astype(bf16))
        gir[g] += nt(block(first.at[1], g), grad)
    gain = column(cols, 1)
    grads = []
    for b in range(NB):
        returned = block(back, b)
        grads.append(nn(wil[b], returned))
        gil[b] += nt(block(first.at[0], b), returned)
    grad_in = jnp.concatenate(grads, axis=0)
    normed = first[0].astype(f32) * (1.0 / gain)
    ggain[...] += fold(grad_in * normed)
    entered = grad_middle[...].astype(f32) + norm_back(grad_in, normed, scale[0:1, :], gain)
    gmask[...] += fold(entered * masked)
    total[...] = entered * (1.0 - masked)
    out_own[...] = total[rows_of(side, HALF), :].T
    out_send[...] = total[rows_of(1 - side, HALF), :].astype(bf16).T

    @pl.when(pl.program_id(0) == steps - 1)
    def _():
        spectrum = gspec[...]
        high = spectrum.astype(bf16)
        low = (spectrum - high.astype(f32)).astype(bf16)
        grad_taps = nn(high, inv[...]) + nn(low, inv[...])
        tap = taps[...]
        grad_taps = grad_taps + tap * (2.0 * penalty_weight * share)
        positions = lax.broadcasted_iota(jnp.int32, (1, LEN), 1).astype(f32)
        decayed = grad_taps * jnp.exp(-column(cols, 4) * positions)
        high = decayed.astype(bf16)
        low = (decayed - high.astype(f32)).astype(bf16)
        sum_weight = (nt(feats[0], high) + nt(feats[1], high) + nt(feats[0], low)).astype(bf16)
        grad_decay = grad_taps * tap * (-positions)
        lane = lax.broadcasted_iota(jnp.int32, (D, LEN), 1)
        vectors = jnp.zeros((D, LEN), f32)
        for index, item in enumerate((gmask[...], ggain[...], gskip[...], grad_decay)):
            vectors = jnp.where(lane == index, jnp.sum(item, axis=1, keepdims=True), vectors)
        vectors = vectors.T[:16, :].astype(bf16)

        def write(dst, j):
            part = BS // 2
            few = ORDER // 2
            for y in range(2):
                lanes = slice(y * HALF, (y + 1) * HALF)
                b = 2 * y + j
                dst[y, 0:BS, :] = gir[b, :, :HALF].astype(bf16)
                dst[y, BS : 2 * BS, 0:BS] = gir[b, :, HALF:].astype(bf16)
                dst[y, BS : 2 * BS, BS:] = gil[b].astype(bf16)
                dst[y, 2 * BS : 3 * BS, 0:BS] = gol[b].astype(bf16)
                dst[y, 2 * BS : 3 * BS, BS:] = gor[b].astype(bf16)
                at = 3 * BS
                dst[y, at : at + part, :] = packed_dr[y, j * part : (j + 1) * part, :]
                at += part
                dst[y, at : at + few, :] = sum_weight[j * few : (j + 1) * few, lanes]
                at += few
                dst[y, at : at + 16, :] = vectors[:, lanes]
                dst[y, at + 16 :, :] = jnp.zeros((MIX_G - at - 16, HALF), bf16)

        core = s_ref[3]
        for c in range(2):

            @pl.when(core == c)
            def _():
                write(keep, c)
                write(send, 1 - c)


def mixer_backward(share, scalars, streams, constants, weights, finals):
    row_count = streams[0].shape[1]
    steps = row_count // BACK_TILE
    ins = list(streams) + list(constants) + list(weights) + list(finals)
    in_specs = [
        pl.BlockSpec((D, BACK_TILE), lambda i, s: (0, i)),
        pl.BlockSpec((2, D, BACK_TILE), lambda i, s: (0, 0, i)),
        pl.BlockSpec((5, D, BACK_TILE), lambda i, s: (0, 0, i)),
        pl.BlockSpec((8, BACK_TILE), lambda i, s: (0, i)),
        pl.BlockSpec((8, BACK_TILE), lambda i, s: (0, i)),
    ] + [whole(item.shape) for item in ins[5:]]
    half_shape = (2, MIX_G, HALF)
    outs = [
        jax.ShapeDtypeStruct((2 * row_count, HALF), f32),
        jax.ShapeDtypeStruct((row_count, HALF), bf16),
        jax.ShapeDtypeStruct(half_shape, bf16),
        jax.ShapeDtypeStruct(half_shape, bf16),
    ]
    out_specs = [
        pl.BlockSpec((BACK_TILE, HALF), lambda i, s: (s[0] * steps + i, 0)),
        pl.BlockSpec((BACK_TILE, HALF), lambda i, s: (i, 0)),
        whole(half_shape),
        whole(half_shape),
    ]
    scratch = [pltpu.VMEM(shape, f32) for shape in BACK_SHAPES]
    scratch += [
        pltpu.VMEM((D, BACK_TILE), bf16),
        pltpu.VMEM((D, BACK_TILE), bf16),
        pltpu.VMEM((D, BACK_TILE), bf16),
        pltpu.VMEM((D, BACK_TILE), f32),
        pltpu.VMEM((D, BACK_TILE), f32),
        pltpu.VMEM((3 * D, BACK_TILE), bf16),
    ]
    return pl.pallas_call(
        functools.partial(mixer_backward_kernel, steps=steps, share=share),
        out_shape=tuple(outs),
        grid_spec=pltpu.PrefetchScalarGridSpec(
            num_scalar_prefetch=1,
            grid=(steps,),
            in_specs=in_specs,
            out_specs=tuple(out_specs),
            scratch_shapes=scratch,
        ),
        compiler_params=pltpu.CompilerParams(vmem_limit_bytes=40 << 20),
        name="mixer_backward",
        cost_estimate=pl.CostEstimate(
            flops=row_count * 2 * 6000000, bytes_accessed=row_count * 20000, transcendentals=0
        ),
    )(scalars, *ins)


def place_parts(s_ref, parts, halves):
    quarter = parts[0].shape[0]
    few = quarter // 4
    for where, part in enumerate(parts):
        core = jnp.bitwise_xor(s_ref[3], where >> 1)
        start = jnp.bitwise_xor(s_ref[4], where & 1) * quarter
        for k in range(4):
            row = pl.multiple_of(start + jnp.bitwise_xor(s_ref[5], k) * few, few)
            halves[core, pl.ds(row, few), :] = part[k * few : (k + 1) * few, :]


def dense_unpack_kernel(s_ref, p0, p1, p2, p3, gain, ul, ur, dl, halves):
    place_parts(s_ref, (p0, p1, p2, p3), halves)
    part = BS // 2
    at = 6 * BS
    gain[...] = halves[0, at + part : at + part + 16, :].astype(f32)[0]
    for j in range(2):
        for c in range(4):
            ur[j, :, c * HALF : (c + 1) * HALF] = halves[j, c * BS : (c + 1) * BS, :].astype(f32)
        for c in range(2):
            dl[j, :, c * HALF : (c + 1) * HALF] = halves[
                j, (4 + c) * BS : (5 + c) * BS, :
            ].astype(f32)
        for lane in range(2):
            ul[lane, j * part : (j + 1) * part, :] = halves[
                j, at : at + part, lane * BS : (lane + 1) * BS
            ].astype(f32)


def mixer_unpack_kernel(s_ref, p0, p1, p2, p3, mask, gain, skip, decay, weight, il, ir, ol, orr, dr, halves):
    place_parts(s_ref, (p0, p1, p2, p3), halves)
    part = BS // 2
    few = ORDER // 2
    at = 3 * BS
    vectors = halves[0, at + part + few : at + part + few + 16, :].astype(f32)
    for index, dst in enumerate((mask, gain, skip, decay)):
        dst[...] = vectors[index]
    for j in range(2):
        ir[j, :, :HALF] = halves[j, 0:BS, :].astype(f32)
        ir[j, :, HALF:] = halves[j, BS : 2 * BS, :BS].astype(f32)
        il[j] = halves[j, BS : 2 * BS, BS:].astype(f32)
        ol[j] = halves[j, 2 * BS : 3 * BS, :BS].astype(f32)
        orr[j] = halves[j, 2 * BS : 3 * BS, BS:].astype(f32)
        for lane in range(2):
            dr[lane, j * part : (j + 1) * part, :] = halves[
                j, at : at + part, lane * BS : (lane + 1) * BS
            ].astype(f32)
        weight[j * few : (j + 1) * few, :] = halves[
            j, at + part : at + part + few, :
        ].astype(f32)


def unpack(kernel, scalars, parts, shapes, name):
    outs = tuple(jax.ShapeDtypeStruct(shape, f32) for shape in shapes)
    rows = 2 * parts[0].shape[0]
    return pl.pallas_call(
        kernel,
        out_shape=outs,
        grid_spec=pltpu.PrefetchScalarGridSpec(
            num_scalar_prefetch=1,
            grid=(1,),
            in_specs=[whole(item.shape) for item in parts],
            out_specs=tuple(whole(shape) for shape in shapes),
            scratch_shapes=[pltpu.VMEM((2, rows, HALF), bf16)],
        ),
        compiler_params=pltpu.CompilerParams(vmem_limit_bytes=16 << 20),
        name=name,
        cost_estimate=light(),
    )(scalars, *parts)


DENSE_OUTS = ((HALF,), (2, BS, BS), (2, BS, 2 * FB), (2, BS, FB))
MIXER_OUTS = (
    (HALF,),
    (HALF,),
    (HALF,),
    (HALF,),
    (ORDER, HALF),
    (2, BS, BS),
    (2, BS, 3 * BS),
    (2, BS, BS),
    (2, BS, BS),
    (2, BS, BS),
)


def corners_kernel(s_ref, *refs):
    for index in range(4):
        kept, got, out = refs[index], refs[4 + index], refs[8 + index]
        out[...] = (kept[...].astype(f32) + got[...].astype(f32)).astype(bf16)


def corners(scalars, kept, got):
    rows = kept.shape[1] // 2
    shape = jax.ShapeDtypeStruct((rows, HALF), bf16)

    def spec(over_y, over_x):
        def at(i, s):
            y = 1 - s[0] if over_y else s[0]
            x = 1 - s[4] if over_x else s[4]
            return (y, x, 0)

        return pl.BlockSpec((None, rows, HALF), at)

    specs = [spec(False, False), spec(False, True), spec(True, False), spec(True, True)]
    return pl.pallas_call(
        corners_kernel,
        out_shape=(shape,) * 4,
        grid_spec=pltpu.PrefetchScalarGridSpec(
            num_scalar_prefetch=1,
            grid=(1,),
            in_specs=specs + specs,
            out_specs=(whole((rows, HALF)),) * 4,
        ),
        compiler_params=pltpu.CompilerParams(vmem_limit_bytes=16 << 20),
        name="sum_corners",
        cost_estimate=light(),
    )(scalars, *([kept] * 4 + [got] * 4))


def columns_kernel(s_ref, a, b, c, d, own, one, two, three, total):
    total[...] = (
        a[...].astype(f32) + b[...].astype(f32) + c[...].astype(f32) + d[...].astype(f32)
    )
    few = total.shape[0] // 4
    for k, out in enumerate((own, one, two, three)):
        row = pl.multiple_of(jnp.bitwise_xor(s_ref[5], k) * few, few)
        out[...] = total[pl.ds(row, few), :].astype(bf16)


def columns(scalars, parts):
    rows = parts[0].shape[0]
    shape = jax.ShapeDtypeStruct((rows // 4, HALF), bf16)
    return pl.pallas_call(
        columns_kernel,
        out_shape=(shape,) * 4,
        grid_spec=pltpu.PrefetchScalarGridSpec(
            num_scalar_prefetch=1,
            grid=(1,),
            in_specs=[whole((rows, HALF))] * 4,
            out_specs=(whole((rows // 4, HALF)),) * 4,
            scratch_shapes=[pltpu.VMEM((rows, HALF), f32)],
        ),
        compiler_params=pltpu.CompilerParams(vmem_limit_bytes=12 << 20),
        name="sum_columns",
        cost_estimate=light(),
    )(scalars, *parts)


def swap_narrow(values):
    return lax.ppermute(values, "narrow", [(0, 1), (1, 0)])


def swap_wide(values, bit, size):
    return lax.ppermute(values, "wide", [(i, i ^ (1 << bit)) for i in range(size)])


def swap_both(values, bit, size):
    flip = 2 << bit
    return lax.ppermute(
        values, ("wide", "narrow"), [(i, i ^ flip ^ 1) for i in range(2 * size)]
    )


def shift_wide(values, flip, size):
    return lax.ppermute(values, "wide", [(i, i ^ flip) for i in range(size)])


def add_low(*items):
    total = items[0].astype(f32)
    for item in items[1:]:
        total = total + item.astype(f32)
    return total.astype(bf16)


def over_corners(parts, size):
    own, over_x, over_y, over_both = parts
    return (
        own,
        swap_wide(over_x, 1, size),
        swap_narrow(over_y),
        swap_both(over_both, 1, size),
    )


def over_columns(parts, size):
    own, *others = parts
    return (own,) + tuple(
        shift_wide(item, (k + 1) << 2, size) for k, item in enumerate(others)
    )


def sum_columns(parts, size):
    packed = add_low(*parts)
    bit = 4
    while 1 << bit < size:
        packed = add_low(packed, swap_wide(packed, bit, size))
        bit += 1
    return packed


def along_columns(packed, size):
    return (packed,) + tuple(shift_wide(packed, k << 2, size) for k in (1, 2, 3))


def tie(*groups):
    held = lax.optimization_barrier(groups)
    return held


def over_cores(near, far, size):
    return (near, far, swap_wide(near, 0, size), swap_wide(far, 0, size))


def gather_chips(piece, size):
    near = swap_narrow(piece)
    high = swap_wide(near, 2, size)
    return near, swap_wide(near, 1, size), high


def gather_cores(items, size):
    pieces = []
    for item in items:
        pieces += [item, swap_wide(item, 0, size)]
    return tuple(pieces)


def on_device(
    wide_size,
    tokens,
    lengths,
    mask_pos,
    mask_vector,
    norm1_gain,
    in_left,
    in_right,
    filter_weight,
    decay,
    skip_gain,
    out_left,
    out_right,
    norm2_gain,
    up_left,
    up_right,
    down_left,
    down_right,
    cotangent,
):
    index = lax.axis_index("wide")
    side = lax.axis_index("narrow")
    row_count = tokens.shape[0] // 2
    scalars = jnp.stack(
        [side, index & 3, (index >> 2) & 1, index & 1, (index >> 1) & 1, (index >> 2) & 3]
    ).astype(jnp.int32)
    share = 1.0 / (2 * wide_size)

    def sent_rows(values):
        return lax.dynamic_slice_in_dim(values, (1 - side) * row_count, row_count, 0)

    mixer_weights = (in_left, in_right, out_left, out_right)
    dense_weights = (up_left, up_right, jnp.swapaxes(down_left, 1, 2), down_right)
    vectors = (mask_vector, norm1_gain, norm2_gain, skip_gain, decay)
    mix_piece, ffn_piece = pack_weights(
        scalars, mixer_weights, dense_weights, filter_weight, vectors
    )
    mix_chips = gather_chips(mix_piece, wide_size)
    mix_chips += (swap_wide(mix_chips[2], 1, wide_size),)
    mix_pieces = gather_cores(mix_chips, wide_size)
    ffn_chips = gather_chips(ffn_piece, wide_size)
    tokens_other = swap_narrow(sent_rows(tokens))
    cot_other = swap_narrow(sent_rows(cotangent))

    positions = jnp.arange(LEN, dtype=jnp.int32)
    valid = (positions[None, :] < lengths[:, None]).astype(f32)
    masked = jnp.any(mask_pos[:, :, None] == positions[None, None, :], axis=1).astype(f32)
    marks = jnp.stack([valid, masked]).reshape(2, 2, row_count)
    marks = lax.dynamic_index_in_dim(marks, side, 1, keepdims=False)
    marks = jnp.concatenate([marks, jnp.zeros((6, row_count), f32)], axis=0)

    fwd, inv = (jnp.asarray(item) for item in transform_tables())
    feats = jnp.asarray(feature_parts())
    taps, spec, penalty, cols = filter_call(
        scalars, filter_weight, mix_piece, mix_pieces, feats, fwd
    )

    ffn_chips, spec = tie(ffn_chips, spec)
    ffn_last = swap_wide(ffn_chips[2], 1, wide_size)
    middle, first, kept, scale, *full = mixer_forward(
        scalars, tokens, tokens_other, marks, cols, spec, fwd, inv, mixer_weights + mix_pieces
    )
    middle, penalty, ffn_last = tie(middle, penalty, ffn_last)
    ffn_pieces = gather_cores(ffn_chips + (ffn_last,), wide_size)
    output, output_sent, grad_middle, ffn_keep, ffn_send, packed_dr = dense(
        scalars, middle, cotangent, cot_other, cols, dense_weights + ffn_pieces
    )
    ffn_parts = corners(scalars, ffn_keep, swap_wide(ffn_send, 0, wide_size))
    grad_middle, ffn_parts, penalty = tie(grad_middle, ffn_parts, penalty[0, 0])
    ffn_parts = over_corners(ffn_parts, wide_size)
    tokens_grad, grad_sent, mix_keep, mix_send = mixer_backward(
        share,
        scalars,
        (grad_middle, first, kept, scale, marks),
        (cols, spec, fwd, inv),
        full,
        (taps, feats, packed_dr),
    )
    mix_keep, mix_send, ffn_parts = tie(mix_keep, mix_send, ffn_parts)
    mix_got = swap_wide(mix_send, 0, wide_size)
    ffn_parts = columns(scalars, ffn_parts)
    mix_got, ffn_parts = tie(mix_got, ffn_parts)
    mix_parts = corners(scalars, mix_keep, mix_got)

    ffn_parts = over_columns(ffn_parts, wide_size)
    mix_parts = over_corners(mix_parts, wide_size)
    ffn_sum = sum_columns(ffn_parts, wide_size)
    ffn_parts = along_columns(ffn_sum, wide_size)
    mix_parts = columns(scalars, mix_parts)
    mix_parts, grad_sent, output_sent = tie(mix_parts, grad_sent, output_sent)
    output_other = swap_narrow(output_sent)
    grad_other = swap_narrow(grad_sent)
    mix_parts = over_columns(mix_parts, wide_size)
    mix_sum = sum_columns(mix_parts, wide_size)
    ffn_near = jnp.concatenate(ffn_parts, axis=0)
    mix_sum, ffn_near, output_other = tie(mix_sum, ffn_near, output_other)
    mix_parts = along_columns(mix_sum, wide_size)
    ffn_far = swap_wide(ffn_near, 1, wide_size)
    mix_near = jnp.concatenate(mix_parts, axis=0)
    mix_far = swap_wide(mix_near, 1, wide_size)
    ffn_parts = over_cores(ffn_near, ffn_far, wide_size)
    gain_two, g_ul, g_ur, g_dl = unpack(
        dense_unpack_kernel, scalars, ffn_parts, DENSE_OUTS, "dense_unpack"
    )
    start = (1 - side) * row_count
    output = lax.dynamic_update_slice_in_dim(output, output_other, start, 0)
    tokens_grad = lax.dynamic_update_slice_in_dim(tokens_grad, grad_other.astype(f32), start, 0)
    mix_far, gain_two, g_ul, g_ur, g_dl, output, tokens_grad = tie(
        mix_far, gain_two, g_ul, g_ur, g_dl, output, tokens_grad
    )
    mix_parts = over_cores(mix_near, mix_far, wide_size)
    g_mask, g_gain, g_skip, g_decay, g_filter, g_il, g_ir, g_ol, g_or, g_dr = unpack(
        mixer_unpack_kernel, scalars, mix_parts, MIXER_OUTS, "mixer_unpack"
    )
    return (
        output,
        tokens_grad,
        g_mask,
        g_gain,
        g_il,
        g_ir,
        g_filter,
        g_decay,
        g_skip,
        g_ol,
        g_or,
        gain_two,
        g_ul,
        g_ur,
        jnp.swapaxes(g_dl, 1, 2),
        g_dr,
        penalty,
    )


def solution(mesh):
    placed = (
        P("wide", "narrow"),
        P("wide"),
        P("wide", None),
        P("narrow"),
        P("narrow"),
        P("narrow", None, None),
        P("narrow", None, None),
        P(None, "narrow"),
        P("narrow"),
        P("narrow"),
        P("narrow", None, None),
        P("narrow", None, None),
        P("narrow"),
        P("narrow", None, None),
        P("narrow", None, None),
        P("narrow", None, None),
        P("narrow", None, None),
        P("wide", "narrow"),
    )
    return jax.shard_map(
        functools.partial(on_device, mesh.shape["wide"]),
        mesh=mesh,
        in_specs=placed,
        out_specs=(
            P("wide", "narrow"),
            P("wide", "narrow"),
            P("narrow"),
            P("narrow"),
            P("narrow", None, None),
            P("narrow", None, None),
            P(None, "narrow"),
            P("narrow"),
            P("narrow"),
            P("narrow", None, None),
            P("narrow", None, None),
            P("narrow"),
            P("narrow", None, None),
            P("narrow", None, None),
            P("narrow", None, None),
            P("narrow", None, None),
            P(),
        ),
        check_vma=False,
    )
```

```python
import functools

import jax
import jax.numpy as jnp
import numpy as np
from jax import lax
from jax.experimental import pallas as pl
from jax.experimental.pallas import tpu as pltpu
from jax.sharding import PartitionSpec as P

D = 768
NB = 4
ORDER = 128
LEN = 128
BS = 192
FB = 768
GROUP = BS // NB
HALF = D // 2
QUARTER = BS // 4

epsilon = 1e-05
penalty_weight = 0.005

bf16 = jnp.bfloat16
f32 = jnp.float32

TILE = 512
BACK_TILE = 256
VMEM = 60 << 20

FILTER_ROW = 3 * QUARTER
VECTOR_ROW = FILTER_ROW + ORDER // 8
MIX_W = VECTOR_ROW + 16
FFN_W = 7 * QUARTER
FFN_G = 1280
MIX_G = 768


def transform_tables():
    t = np.arange(LEN, dtype=np.float64)[:, None]
    k = np.arange(LEN, dtype=np.float64)[None, :]
    angle = np.pi * (2 * k + 1) * t / (2 * LEN)
    forward = np.concatenate([np.cos(angle), np.sin(angle)], axis=1)
    return forward.astype(bf16), (forward.T / LEN).astype(bf16)


def feature_parts():
    t = np.arange(LEN, dtype=np.float64)[None, :]
    freqs = (np.arange(ORDER // 2, dtype=np.float64)[:, None] + 1.0) * (3.1 / (ORDER // 2))
    table = np.concatenate([np.sin(t * freqs), np.cos(t * freqs)], axis=0)
    parts = []
    for _ in range(3):
        part = table.astype(bf16)
        parts.append(part)
        table = table - part.astype(np.float64)
    return np.stack(parts)


def nn(a, b):
    return lax.dot_general(a, b, (((1,), (0,)), ((), ())), preferred_element_type=f32)


def nt(a, b):
    return lax.dot_general(a, b, (((1,), (1,)), ((), ())), preferred_element_type=f32)


def tn(a, b):
    return lax.dot_general(a, b, (((0,), (0,)), ((), ())), preferred_element_type=f32)


def exact_nt(a, b):
    return lax.dot_general(
        a,
        b,
        (((1,), (1,)), ((), ())),
        preferred_element_type=f32,
        precision=lax.Precision.HIGHEST,
    )


def fold(values):
    out = values[:, :LEN]
    for start in range(LEN, values.shape[1], LEN):
        out = out + values[:, start : start + LEN]
    return out


def light():
    return pl.CostEstimate(flops=0, bytes_accessed=1 << 20, transcendentals=0)


def rows_of(block, size):
    return pl.ds(pl.multiple_of(block * size, size), size)


def column(cols_ref, index):
    return cols_ref[:, index : index + 1]


def place_halves(dst_ref, side, own, other):
    dst_ref[rows_of(side, HALF), :] = own
    dst_ref[rows_of(1 - side, HALF), :] = other


def regroup(dst_ref, block, values):
    for g in range(NB):
        dst_ref[g * BS + block * GROUP : g * BS + (block + 1) * GROUP, :] = values[
            g * GROUP : (g + 1) * GROUP, :
        ]


def block(ref, index, size=BS):
    return ref[index * size : (index + 1) * size, :]


def norm_stats(values):
    center = values - jnp.sum(values, axis=0, keepdims=True) * (1.0 / D)
    spread = jnp.sum(center * center, axis=0, keepdims=True) * (1.0 / D)
    scale_row = lax.rsqrt(spread + epsilon)
    return center * scale_row, scale_row


def norm_back(grad, normed, scale_row, gain):
    scaled = grad * gain
    first = jnp.sum(scaled, axis=0, keepdims=True) * (1.0 / D)
    second = jnp.sum(scaled * normed, axis=0, keepdims=True) * (1.0 / D)
    return scale_row * (scaled - first - normed * second)


def pack_kernel(
    s_ref, il, ir, ol, orr, ul, ur, dl, dr, weight, mask, gain1, gain2, skip, decay, mix_ref, ffn_ref
):
    q = QUARTER
    mix_ref[0:q, :] = jnp.concatenate([il[0], ol[0]], axis=1)
    mix_ref[q : 2 * q, :] = ir[0][:, :HALF]
    mix_ref[2 * q : 3 * q, :] = jnp.concatenate([ir[0][:, HALF:], orr[0]], axis=1)
    mix_ref[FILTER_ROW:VECTOR_ROW, :] = weight[...]
    rest = decay[...].reshape(1, HALF)
    rows = [item[...].reshape(1, HALF).astype(f32) for item in (mask, gain1, gain2, skip)]
    for _ in range(3):
        part = rest.astype(bf16).astype(f32)
        rows.append(part)
        rest = rest - part
    line = lax.broadcasted_iota(jnp.int32, (16, HALF), 0)
    vectors = jnp.zeros((16, HALF), f32)
    for index, row in enumerate(rows):
        vectors = jnp.where(line == index, row, vectors)
    mix_ref[VECTOR_ROW:, :] = vectors.astype(bf16)
    for c in range(4):
        ffn_ref[c * q : (c + 1) * q, :] = ur[0][:, c * HALF : (c + 1) * HALF]
    for c in range(2):
        ffn_ref[(4 + c) * q : (5 + c) * q, :] = dl[0][:, c * HALF : (c + 1) * HALF]
    ffn_ref[6 * q : 7 * q, :] = jnp.concatenate([ul[0], dr[0]], axis=1)


def pack_weights(scalars, mixer_weights, dense_weights, filter_weight, vectors):
    def eighth(item):
        return pl.BlockSpec((1, QUARTER, item.shape[2]), lambda i, s: (s[2], s[1], 0))

    return pl.pallas_call(
        pack_kernel,
        out_shape=(
            jax.ShapeDtypeStruct((MIX_W, HALF), bf16),
            jax.ShapeDtypeStruct((FFN_W, HALF), bf16),
        ),
        grid_spec=pltpu.PrefetchScalarGridSpec(
            num_scalar_prefetch=1,
            grid=(1,),
            in_specs=[eighth(item) for item in mixer_weights + dense_weights]
            + [pl.BlockSpec((ORDER // 8, HALF), lambda i, s: (4 * s[2] + s[1], 0))]
            + [whole(item.shape) for item in vectors],
            out_specs=(whole((MIX_W, HALF)), whole((FFN_W, HALF))),
        ),
        name="pack_weights",
        cost_estimate=light(),
    )(scalars, *mixer_weights, *dense_weights, filter_weight, *vectors)


def own_blocks(dst, side, src):
    for j in range(2):
        dst[2 * side + j] = src[j]


def filter_kernel(
    s_ref, own, mine, *refs
):
    pieces = refs[:8]
    feats, fwd, taps_ref, spec_ref, pen_ref, cols_ref, weight = refs[8:]
    side = s_ref[0]
    q = ORDER // 8
    for p, piece in enumerate(pieces):
        place = 4 * jnp.bitwise_xor(s_ref[2], p >> 2) + jnp.bitwise_xor(s_ref[1], p & 3)
        weight[pl.ds(pl.multiple_of(place * q, q), q), :] = piece[FILTER_ROW:VECTOR_ROW, :]
    for which, src, rows in ((side, own, mine), (1 - side, weight, pieces[0])):
        table = src[...]
        basis = tn(table, feats[2]) + tn(table, feats[1]) + tn(table, feats[0])
        taps_ref[rows_of(which, HALF), :] = basis
        vectors = rows[VECTOR_ROW:, :].astype(f32)
        vectors = jnp.concatenate([vectors, jnp.zeros((LEN - 16, HALF), f32)], axis=0)
        vectors = vectors.T
        lane = lax.broadcasted_iota(jnp.int32, (HALF, LEN), 1)
        decay = vectors[:, 4:5] + vectors[:, 5:6] + vectors[:, 6:7]
        cols_ref[rows_of(which, HALF), :] = jnp.where(lane == 4, decay, vectors)
    positions = lax.broadcasted_iota(jnp.int32, (1, LEN), 1).astype(f32)
    taps = taps_ref[...] * jnp.exp(-column(cols_ref, 4) * positions)
    taps_ref[...] = taps
    spec_ref[...] = nn(taps.astype(bf16), fwd[...])
    total = jnp.sum(jnp.sum(taps * taps, axis=0, keepdims=True), axis=1, keepdims=True)
    pen_ref[...] = jnp.broadcast_to(total * penalty_weight, (8, LEN))


def whole(shape):
    return pl.BlockSpec(shape, lambda *_: (0,) * len(shape))


def filter_call(scalars, own, mine, pieces, feats, fwd):
    ins = (own, mine) + tuple(pieces) + (feats, fwd)
    outs = (
        jax.ShapeDtypeStruct((D, LEN), f32),
        jax.ShapeDtypeStruct((D, 2 * LEN), f32),
        jax.ShapeDtypeStruct((8, LEN), f32),
        jax.ShapeDtypeStruct((D, LEN), f32),
    )
    return pl.pallas_call(
        filter_kernel,
        out_shape=outs,
        grid_spec=pltpu.PrefetchScalarGridSpec(
            num_scalar_prefetch=1,
            grid=(1,),
            in_specs=[whole(item.shape) for item in ins],
            out_specs=tuple(whole(item.shape) for item in outs),
            scratch_shapes=[pltpu.VMEM((ORDER, HALF), bf16)],
        ),
        name="filter_spectrum",
        cost_estimate=light(),
    )(scalars, *ins)


def mixer_forward_kernel(
    s_ref,
    own,
    oth,
    marks,
    cols,
    spec,
    fwd,
    inv,
    il,
    ir,
    ol,
    orr,
    *refs,
):
    pieces = refs[:8]
    middle, first, kept, scale, wil, wir, wol, wor, enter, half, conv = refs[8:]
    side = s_ref[0]

    @pl.when(pl.program_id(0) == 0)
    def _():
        other = 1 - side
        own_blocks(wil, side, il)
        own_blocks(wir, side, ir)
        own_blocks(wol, side, ol)
        own_blocks(wor, side, orr)
        q = QUARTER
        for p, piece in enumerate(pieces):
            at = pl.ds(pl.multiple_of(jnp.bitwise_xor(s_ref[1], p & 3) * q, q), q)
            blk = 2 * other + jnp.bitwise_xor(s_ref[2], p >> 2)
            wil[blk, at, :] = piece[0:q, :BS]
            wol[blk, at, :] = piece[0:q, BS:]
            wir[blk, at, 0:HALF] = piece[q : 2 * q, :]
            wir[blk, at, HALF:] = piece[2 * q : 3 * q, :BS]
            wor[blk, at, :] = piece[2 * q : 3 * q, BS:]

    place_halves(enter, side, own[...].T.astype(f32), oth[...].T.astype(f32))
    valid = marks[0:1, :]
    masked = marks[1:2, :]
    tokens = enter[...]
    entered = tokens + masked * (column(cols, 0) - tokens)
    enter[...] = entered
    normed, scale_row = norm_stats(entered)
    scale[...] = jnp.broadcast_to(scale_row, scale.shape)
    half[...] = (normed * column(cols, 1)).astype(bf16)
    first[0] = half[...]
    for b in range(NB):
        regroup(first.at[1], b, tn(wil[b], block(half, b)).astype(bf16))
    for g in range(NB):
        projected = tn(wir[g], block(first.at[1], g))
        rows = slice(g * BS, (g + 1) * BS)
        for part in range(3):
            kept[part, rows, :] = projected[part * BS : (part + 1) * BS, :].astype(bf16)
        source = (projected[:BS] * projected[2 * BS :] * valid).astype(bf16)
        half[rows, :] = source
    for s in range(TILE // LEN):
        lanes = slice(s * LEN, (s + 1) * LEN)
        wave = nn(half[:, lanes], fwd[...])
        wc, ws = wave[:, :LEN], wave[:, LEN:]
        hc, hs = spec[:, :LEN], spec[:, LEN:]
        product = jnp.concatenate(
            [(wc * hc - ws * hs).astype(bf16), (wc * hs + ws * hc).astype(bf16)], axis=1
        )
        conv[:, lanes] = nn(product, inv[...])
    inner = conv[...] + column(cols, 3) * half[...].astype(f32)
    kept[3] = inner.astype(bf16)
    half[...] = (kept[1].astype(f32) * inner).astype(bf16)
    for b in range(NB):
        regroup(kept.at[4], b, tn(wol[b], block(half, b)).astype(bf16))
    for g in range(NB):
        rows = slice(g * BS, (g + 1) * BS)
        middle[rows, :] = (enter[rows, :] + tn(wor[g], block(kept.at[4], g))).astype(bf16)


def mixer_forward(scalars, own, oth, marks, cols, spec, fwd, inv, weights):
    row_count = own.shape[0] // 2
    steps = row_count // TILE
    ins = (own, oth, marks, cols, spec, fwd, inv) + tuple(weights)
    in_specs = [
        pl.BlockSpec((TILE, HALF), lambda i, s: (s[0] * steps + i, 0)),
        pl.BlockSpec((TILE, HALF), lambda i, s: (i, 0)),
        pl.BlockSpec((8, TILE), lambda i, s: (0, i)),
    ] + [whole(item.shape) for item in ins[3:]]
    full = [(NB, BS, BS), (NB, BS, 3 * BS), (NB, BS, BS), (NB, BS, BS)]
    outs = [
        jax.ShapeDtypeStruct((D, row_count), bf16),
        jax.ShapeDtypeStruct((2, D, row_count), bf16),
        jax.ShapeDtypeStruct((5, D, row_count), bf16),
        jax.ShapeDtypeStruct((8, row_count), f32),
    ] + [jax.ShapeDtypeStruct(shape, bf16) for shape in full]
    out_specs = [
        pl.BlockSpec((D, TILE), lambda i, s: (0, i)),
        pl.BlockSpec((2, D, TILE), lambda i, s: (0, 0, i)),
        pl.BlockSpec((5, D, TILE), lambda i, s: (0, 0, i)),
        pl.BlockSpec((8, TILE), lambda i, s: (0, i)),
    ] + [whole(shape) for shape in full]
    return pl.pallas_call(
        mixer_forward_kernel,
        out_shape=tuple(outs),
        grid_spec=pltpu.PrefetchScalarGridSpec(
            num_scalar_prefetch=1,
            grid=(steps,),
            in_specs=in_specs,
            out_specs=tuple(out_specs),
            scratch_shapes=[
                pltpu.VMEM((D, TILE), f32),
                pltpu.VMEM((D, TILE), bf16),
                pltpu.VMEM((D, TILE), f32),
            ],
        ),
        compiler_params=pltpu.CompilerParams(vmem_limit_bytes=VMEM),
        name="mixer_forward",
        cost_estimate=pl.CostEstimate(
            flops=row_count * 2 * 1500000, bytes_accessed=row_count * 20000, transcendentals=0
        ),
    )(scalars, *ins)


ACC_SHAPES = ((NB, BS, 2 * FB), (NB, BS, FB), (NB, BS, BS), (NB, BS, BS), (D, LEN))


def dense_kernel(
    s_ref,
    middle,
    own,
    oth,
    cols,
    ul,
    ur,
    dl,
    dr,
    p0,
    p1,
    p2,
    p3,
    p4,
    p5,
    p6,
    p7,
    out_own,
    out_send,
    grad_middle,
    keep,
    send,
    packed_dr,
    wul,
    wur,
    wdl,
    wdr,
    gur,
    gdl,
    gul,
    gdr,
    ggain,
    top,
    half,
    moved3,
    moved4,
    hid,
    act,
    slope,
    gated,
    back,
    outs,
    *,
    steps,
):
    side = s_ref[0]

    @pl.when(pl.program_id(0) == 0)
    def _():
        other = 1 - side
        own_blocks(wul, side, ul)
        own_blocks(wur, side, ur)
        own_blocks(wdl, side, dl)
        own_blocks(wdr, side, dr)
        q = QUARTER
        for p, piece in enumerate((p0, p1, p2, p3, p4, p5, p6, p7)):
            row = pl.multiple_of(jnp.bitwise_xor(s_ref[1], p & 3) * q, q)
            at = pl.ds(row, q)
            blk = 2 * other + jnp.bitwise_xor(s_ref[2], p >> 2)
            for c in range(4):
                wur[blk, at, c * HALF : (c + 1) * HALF] = piece[c * q : (c + 1) * q, :]
            for c in range(2):
                wdl[blk, at, c * HALF : (c + 1) * HALF] = piece[(4 + c) * q : (5 + c) * q, :]
            wul[blk, at, :] = piece[6 * q : 7 * q, :BS]
            wdr[blk, at, :] = piece[6 * q : 7 * q, BS:]
        for acc in (gur, gdl, gul, gdr, ggain):
            acc[...] = jnp.zeros(acc.shape, f32)

    place_halves(top, side, own[...].T, oth[...].T)
    gain = column(cols, 2)
    normed, scale_row = norm_stats(middle[...].astype(f32))
    half[...] = (normed * gain).astype(bf16)
    for b in range(NB):
        regroup(moved3, b, tn(wul[b], block(half, b)).astype(bf16))
    for g in range(NB):
        rows = slice(g * FB, (g + 1) * FB)
        both = tn(wur[g], block(moved3, g))
        gate, up = both[:FB], both[FB:]
        chance = 0.5 + 0.5 * lax.erf(gate * 0.7071067811865476)
        density = jnp.exp(gate * gate * -0.5 - 0.9189385332046727)
        active = gate * chance
        active, up = active.astype(bf16), up.astype(bf16)
        hid[rows, :] = active * up
        act[rows, :] = active
        slope[rows, :] = up * (chance + gate * density).astype(bf16)
        regroup(moved4, g, nn(wdl[g], hid[rows, :]).astype(bf16))
    for g in range(NB):
        rows = slice(g * BS, (g + 1) * BS)
        outs[rows, :] = (middle[rows, :].astype(f32) + tn(wdr[g], block(moved4, g))).astype(bf16)
    out_own[...] = outs[rows_of(side, HALF), :].T
    out_send[...] = outs[rows_of(1 - side, HALF), :].T
    for g in range(NB):
        grad = block(top, g)
        regroup(back, g, nn(wdr[g], grad).astype(bf16))
        gdr[g] += nt(block(moved4, g), grad)
    for b in range(NB):
        rows = slice(b * FB, (b + 1) * FB)
        returned = block(back, b)
        grad_hidden = tn(wdl[b], returned)
        gdl[b] += nt(returned, hid[rows, :])
        lowered = grad_hidden.astype(bf16)
        gated[:FB, :] = lowered * slope[rows, :]
        gated[FB:, :] = lowered * act[rows, :]
        moved = block(moved3, b)
        gur[b] += nt(moved, gated[...])
        regroup(moved4, b, nn(wur[b], gated[...]).astype(bf16))
    grads = []
    for b in range(NB):
        returned = block(moved4, b)
        grads.append(nn(wul[b], returned))
        gul[b] += nt(block(half, b), returned)
    grad_in = jnp.concatenate(grads, axis=0)
    ggain[...] += fold(grad_in * normed)
    grad_middle[...] = (
        top[...].astype(f32) + norm_back(grad_in, normed, scale_row, gain)
    ).astype(bf16)

    @pl.when(pl.program_id(0) == steps - 1)
    def _():
        lane = lax.broadcasted_iota(jnp.int32, (D, LEN), 1)
        sums = jnp.where(lane == 0, jnp.sum(ggain[...], axis=1, keepdims=True), 0.0)
        sums = sums.T[:16, :].astype(bf16)

        def write(dst, j):
            part = BS // 2
            for y in range(2):
                b = 2 * y + j
                for c in range(4):
                    dst[y, c * BS : (c + 1) * BS, :] = gur[b, :, c * HALF : (c + 1) * HALF].astype(
                        bf16
                    )
                for c in range(2):
                    at = (4 + c) * BS
                    dst[y, at : at + BS, :] = gdl[b, :, c * HALF : (c + 1) * HALF].astype(bf16)
                at = 6 * BS
                for lane in range(2):
                    dst[y, at : at + part, lane * BS : (lane + 1) * BS] = gul[
                        2 * y + lane, j * part : (j + 1) * part, :
                    ].astype(bf16)
                at += part
                dst[y, at : at + 16, :] = sums[:, y * HALF : (y + 1) * HALF]
                dst[y, at + 16 :, :] = jnp.zeros((FFN_G - at - 16, HALF), bf16)

        core = s_ref[3]
        for c in range(2):

            @pl.when(core == c)
            def _():
                write(keep, c)
                write(send, 1 - c)

        for y in range(2):
            for j in range(2):
                packed_dr[y, :, j * BS : (j + 1) * BS] = gdr[2 * y + j].astype(bf16)


def dense(scalars, middle, own, oth, cols, weights):
    row_count = own.shape[0] // 2
    steps = row_count // TILE

    def own_rows(i, s):
        return (s[0] * steps + i, 0)

    ins = [middle, own, oth, cols] + list(weights)
    in_specs = [
        pl.BlockSpec((D, TILE), lambda i, s: (0, i)),
        pl.BlockSpec((TILE, HALF), own_rows),
        pl.BlockSpec((TILE, HALF), lambda i, s: (i, 0)),
        whole(cols.shape),
    ] + [whole(item.shape) for item in weights]
    half_shape = (2, FFN_G, HALF)
    outs = [
        jax.ShapeDtypeStruct((2 * row_count, HALF), bf16),
        jax.ShapeDtypeStruct((row_count, HALF), bf16),
        jax.ShapeDtypeStruct((D, row_count), bf16),
        jax.ShapeDtypeStruct(half_shape, bf16),
        jax.ShapeDtypeStruct(half_shape, bf16),
        jax.ShapeDtypeStruct((2, BS, HALF), bf16),
    ]
    out_specs = [
        pl.BlockSpec((TILE, HALF), own_rows),
        pl.BlockSpec((TILE, HALF), lambda i, s: (i, 0)),
        pl.BlockSpec((D, TILE), lambda i, s: (0, i)),
        whole(half_shape),
        whole(half_shape),
        whole((2, BS, HALF)),
    ]
    full = [(NB, BS, BS), (NB, BS, 2 * FB), (NB, BS, FB), (NB, BS, BS)]
    scratch = [pltpu.VMEM(shape, bf16) for shape in full]
    scratch += [pltpu.VMEM(shape, f32) for shape in ACC_SHAPES]
    scratch += [pltpu.VMEM((D, TILE), bf16) for _ in range(4)]
    scratch += [pltpu.VMEM((NB * FB, TILE), bf16) for _ in range(3)]
    scratch += [pltpu.VMEM((2 * FB, TILE), bf16)]
    scratch += [pltpu.VMEM((D, TILE), bf16) for _ in range(2)]
    return pl.pallas_call(
        functools.partial(dense_kernel, steps=steps),
        out_shape=tuple(outs),
        grid_spec=pltpu.PrefetchScalarGridSpec(
            num_scalar_prefetch=1,
            grid=(steps,),
            in_specs=in_specs,
            out_specs=tuple(out_specs),
            scratch_shapes=scratch,
        ),
        compiler_params=pltpu.CompilerParams(vmem_limit_bytes=46 << 20),
        name="dense",
        cost_estimate=pl.CostEstimate(
            flops=row_count * 2 * 8000000, bytes_accessed=row_count * 10000, transcendentals=0
        ),
    )(scalars, *ins)


BACK_SHAPES = (
    (NB, BS, BS),
    (NB, BS, BS),
    (D, LEN),
    (D, 2 * LEN),
    (NB, BS, 3 * BS),
    (NB, BS, BS),
    (D, LEN),
    (D, LEN),
)


def mixer_backward_kernel(
    s_ref,
    grad_middle,
    first,
    kept,
    scale,
    marks,
    cols,
    spec,
    fwd,
    inv,
    wil,
    wir,
    wol,
    wor,
    taps,
    feats,
    packed_dr,
    out_own,
    out_send,
    keep,
    send,
    gol,
    gor,
    gskip,
    gspec,
    gir,
    gil,
    gmask,
    ggain,
    back,
    half,
    conv,
    inner_grad,
    total,
    proj,
    *,
    steps,
    share,
):
    side = s_ref[0]

    @pl.when(pl.program_id(0) == 0)
    def _():
        for acc in (gol, gor, gskip, gspec, gir, gil, gmask, ggain):
            acc[...] = jnp.zeros(acc.shape, f32)

    valid = marks[0:1, :]
    for g in range(NB):
        grad = block(grad_middle, g)
        regroup(back, g, nn(wor[g], grad).astype(bf16))
        gor[g] += nt(block(kept.at[4], g), grad)
    for b in range(NB):
        rows = slice(b * BS, (b + 1) * BS)
        returned = block(back, b)
        grad_mixed = nn(wol[b], returned)
        gate = kept[1, rows, :].astype(f32)
        inner = kept[3, rows, :].astype(f32)
        gol[b] += nt(kept[1, rows, :] * kept[3, rows, :], returned)
        grad_inner = grad_mixed * gate
        inner_grad[rows, :] = grad_inner
        conv[rows, :] = grad_inner.astype(bf16)
        proj[b * 3 * BS + BS : b * 3 * BS + 2 * BS, :] = (grad_mixed * inner).astype(bf16)
        source = kept[0, rows, :] * kept[2, rows, :] * valid.astype(bf16)
        half[rows, :] = source
        gskip[rows, :] += fold(grad_inner * source.astype(f32))
    hc, hs = spec[:, :LEN], spec[:, LEN:]
    for s in range(BACK_TILE // LEN):
        lanes = slice(s * LEN, (s + 1) * LEN)
        wave = nn(jnp.concatenate([conv[:, lanes], half[:, lanes]], axis=0), fwd[...])
        wc, ws = wave[:D, :LEN], wave[:D, LEN:]
        seen = wave[D:]
        sc, ss = seen[:, :LEN], seen[:, LEN:]
        gspec[:, :LEN] += wc * sc + ws * ss
        gspec[:, LEN:] += ws * sc - wc * ss
        product = jnp.concatenate(
            [(wc * hc + ws * hs).astype(bf16), (ws * hc - wc * hs).astype(bf16)], axis=1
        )
        total[:, lanes] = nn(product, inv[...])
    for g in range(NB):
        rows = slice(g * BS, (g + 1) * BS)
        grad_source = ((total[rows, :] + cols[rows, 3:4] * inner_grad[rows, :]) * valid).astype(bf16)
        start = g * 3 * BS
        proj[start : start + BS, :] = grad_source * kept[2, rows, :]
        proj[start + 2 * BS : start + 3 * BS, :] = grad_source * kept[0, rows, :]

    masked = marks[1:2, :]
    for g in range(NB):
        grad = proj[g * 3 * BS : (g + 1) * 3 * BS, :]
        regroup(back, g, nn(wir[g], grad).astype(bf16))
        gir[g] += nt(block(first.at[1], g), grad)
    gain = column(cols, 1)
    grads = []
    for b in range(NB):
        returned = block(back, b)
        grads.append(nn(wil[b], returned))
        gil[b] += nt(block(first.at[0], b), returned)
    grad_in = jnp.concatenate(grads, axis=0)
    normed = first[0].astype(f32) * (1.0 / gain)
    ggain[...] += fold(grad_in * normed)
    entered = grad_middle[...].astype(f32) + norm_back(grad_in, normed, scale[0:1, :], gain)
    gmask[...] += fold(entered * masked)
    total[...] = entered * (1.0 - masked)
    out_own[...] = total[rows_of(side, HALF), :].T
    out_send[...] = total[rows_of(1 - side, HALF), :].astype(bf16).T

    @pl.when(pl.program_id(0) == steps - 1)
    def _():
        spectrum = gspec[...]
        high = spectrum.astype(bf16)
        low = (spectrum - high.astype(f32)).astype(bf16)
        grad_taps = nn(high, inv[...]) + nn(low, inv[...])
        tap = taps[...]
        grad_taps = grad_taps + tap * (2.0 * penalty_weight * share)
        positions = lax.broadcasted_iota(jnp.int32, (1, LEN), 1).astype(f32)
        decayed = grad_taps * jnp.exp(-column(cols, 4) * positions)
        high = decayed.astype(bf16)
        low = (decayed - high.astype(f32)).astype(bf16)
        sum_weight = (nt(feats[0], high) + nt(feats[1], high) + nt(feats[0], low)).astype(bf16)
        grad_decay = grad_taps * tap * (-positions)
        lane = lax.broadcasted_iota(jnp.int32, (D, LEN), 1)
        vectors = jnp.zeros((D, LEN), f32)
        for index, item in enumerate((gmask[...], ggain[...], gskip[...], grad_decay)):
            vectors = jnp.where(lane == index, jnp.sum(item, axis=1, keepdims=True), vectors)
        vectors = vectors.T[:16, :].astype(bf16)

        def write(dst, j):
            part = BS // 2
            few = ORDER // 2
            for y in range(2):
                lanes = slice(y * HALF, (y + 1) * HALF)
                b = 2 * y + j
                dst[y, 0:BS, :] = gir[b, :, :HALF].astype(bf16)
                dst[y, BS : 2 * BS, 0:BS] = gir[b, :, HALF:].astype(bf16)
                dst[y, BS : 2 * BS, BS:] = gil[b].astype(bf16)
                dst[y, 2 * BS : 3 * BS, 0:BS] = gol[b].astype(bf16)
                dst[y, 2 * BS : 3 * BS, BS:] = gor[b].astype(bf16)
                at = 3 * BS
                dst[y, at : at + part, :] = packed_dr[y, j * part : (j + 1) * part, :]
                at += part
                dst[y, at : at + few, :] = sum_weight[j * few : (j + 1) * few, lanes]
                at += few
                dst[y, at : at + 16, :] = vectors[:, lanes]
                dst[y, at + 16 :, :] = jnp.zeros((MIX_G - at - 16, HALF), bf16)

        core = s_ref[3]
        for c in range(2):

            @pl.when(core == c)
            def _():
                write(keep, c)
                write(send, 1 - c)


def mixer_backward(share, scalars, streams, constants, weights, finals):
    row_count = streams[0].shape[1]
    steps = row_count // BACK_TILE
    ins = list(streams) + list(constants) + list(weights) + list(finals)
    in_specs = [
        pl.BlockSpec((D, BACK_TILE), lambda i, s: (0, i)),
        pl.BlockSpec((2, D, BACK_TILE), lambda i, s: (0, 0, i)),
        pl.BlockSpec((5, D, BACK_TILE), lambda i, s: (0, 0, i)),
        pl.BlockSpec((8, BACK_TILE), lambda i, s: (0, i)),
        pl.BlockSpec((8, BACK_TILE), lambda i, s: (0, i)),
    ] + [whole(item.shape) for item in ins[5:]]
    half_shape = (2, MIX_G, HALF)
    outs = [
        jax.ShapeDtypeStruct((2 * row_count, HALF), f32),
        jax.ShapeDtypeStruct((row_count, HALF), bf16),
        jax.ShapeDtypeStruct(half_shape, bf16),
        jax.ShapeDtypeStruct(half_shape, bf16),
    ]
    out_specs = [
        pl.BlockSpec((BACK_TILE, HALF), lambda i, s: (s[0] * steps + i, 0)),
        pl.BlockSpec((BACK_TILE, HALF), lambda i, s: (i, 0)),
        whole(half_shape),
        whole(half_shape),
    ]
    scratch = [pltpu.VMEM(shape, f32) for shape in BACK_SHAPES]
    scratch += [
        pltpu.VMEM((D, BACK_TILE), bf16),
        pltpu.VMEM((D, BACK_TILE), bf16),
        pltpu.VMEM((D, BACK_TILE), bf16),
        pltpu.VMEM((D, BACK_TILE), f32),
        pltpu.VMEM((D, BACK_TILE), f32),
        pltpu.VMEM((3 * D, BACK_TILE), bf16),
    ]
    return pl.pallas_call(
        functools.partial(mixer_backward_kernel, steps=steps, share=share),
        out_shape=tuple(outs),
        grid_spec=pltpu.PrefetchScalarGridSpec(
            num_scalar_prefetch=1,
            grid=(steps,),
            in_specs=in_specs,
            out_specs=tuple(out_specs),
            scratch_shapes=scratch,
        ),
        compiler_params=pltpu.CompilerParams(vmem_limit_bytes=40 << 20),
        name="mixer_backward",
        cost_estimate=pl.CostEstimate(
            flops=row_count * 2 * 6000000, bytes_accessed=row_count * 20000, transcendentals=0
        ),
    )(scalars, *ins)


def place_parts(s_ref, parts, halves):
    quarter = parts[0].shape[0]
    few = quarter // 4
    for where, part in enumerate(parts):
        core = jnp.bitwise_xor(s_ref[3], where >> 1)
        start = jnp.bitwise_xor(s_ref[4], where & 1) * quarter
        for k in range(4):
            row = pl.multiple_of(start + jnp.bitwise_xor(s_ref[5], k) * few, few)
            halves[core, pl.ds(row, few), :] = part[k * few : (k + 1) * few, :]


def dense_unpack_kernel(s_ref, p0, p1, p2, p3, gain, ul, ur, dl, halves):
    place_parts(s_ref, (p0, p1, p2, p3), halves)
    part = BS // 2
    at = 6 * BS
    gain[...] = halves[0, at + part : at + part + 16, :].astype(f32)[0]
    for j in range(2):
        for c in range(4):
            ur[j, :, c * HALF : (c + 1) * HALF] = halves[j, c * BS : (c + 1) * BS, :].astype(f32)
        for c in range(2):
            dl[j, :, c * HALF : (c + 1) * HALF] = halves[
                j, (4 + c) * BS : (5 + c) * BS, :
            ].astype(f32)
        for lane in range(2):
            ul[lane, j * part : (j + 1) * part, :] = halves[
                j, at : at + part, lane * BS : (lane + 1) * BS
            ].astype(f32)


def mixer_unpack_kernel(s_ref, p0, p1, p2, p3, mask, gain, skip, decay, weight, il, ir, ol, orr, dr, halves):
    place_parts(s_ref, (p0, p1, p2, p3), halves)
    part = BS // 2
    few = ORDER // 2
    at = 3 * BS
    vectors = halves[0, at + part + few : at + part + few + 16, :].astype(f32)
    for index, dst in enumerate((mask, gain, skip, decay)):
        dst[...] = vectors[index]
    for j in range(2):
        ir[j, :, :HALF] = halves[j, 0:BS, :].astype(f32)
        ir[j, :, HALF:] = halves[j, BS : 2 * BS, :BS].astype(f32)
        il[j] = halves[j, BS : 2 * BS, BS:].astype(f32)
        ol[j] = halves[j, 2 * BS : 3 * BS, :BS].astype(f32)
        orr[j] = halves[j, 2 * BS : 3 * BS, BS:].astype(f32)
        for lane in range(2):
            dr[lane, j * part : (j + 1) * part, :] = halves[
                j, at : at + part, lane * BS : (lane + 1) * BS
            ].astype(f32)
        weight[j * few : (j + 1) * few, :] = halves[
            j, at + part : at + part + few, :
        ].astype(f32)


def unpack(kernel, scalars, parts, shapes, name):
    outs = tuple(jax.ShapeDtypeStruct(shape, f32) for shape in shapes)
    rows = 2 * parts[0].shape[0]
    return pl.pallas_call(
        kernel,
        out_shape=outs,
        grid_spec=pltpu.PrefetchScalarGridSpec(
            num_scalar_prefetch=1,
            grid=(1,),
            in_specs=[whole(item.shape) for item in parts],
            out_specs=tuple(whole(shape) for shape in shapes),
            scratch_shapes=[pltpu.VMEM((2, rows, HALF), bf16)],
        ),
        compiler_params=pltpu.CompilerParams(vmem_limit_bytes=16 << 20),
        name=name,
        cost_estimate=light(),
    )(scalars, *parts)


DENSE_OUTS = ((HALF,), (2, BS, BS), (2, BS, 2 * FB), (2, BS, FB))
MIXER_OUTS = (
    (HALF,),
    (HALF,),
    (HALF,),
    (HALF,),
    (ORDER, HALF),
    (2, BS, BS),
    (2, BS, 3 * BS),
    (2, BS, BS),
    (2, BS, BS),
    (2, BS, BS),
)


def corners_kernel(s_ref, *refs):
    for index in range(4):
        kept, got, out = refs[index], refs[4 + index], refs[8 + index]
        out[...] = (kept[...].astype(f32) + got[...].astype(f32)).astype(bf16)


def corners(scalars, kept, got):
    rows = kept.shape[1] // 2
    shape = jax.ShapeDtypeStruct((rows, HALF), bf16)

    def spec(over_y, over_x):
        def at(i, s):
            y = 1 - s[0] if over_y else s[0]
            x = 1 - s[4] if over_x else s[4]
            return (y, x, 0)

        return pl.BlockSpec((None, rows, HALF), at)

    specs = [spec(False, False), spec(False, True), spec(True, False), spec(True, True)]
    return pl.pallas_call(
        corners_kernel,
        out_shape=(shape,) * 4,
        grid_spec=pltpu.PrefetchScalarGridSpec(
            num_scalar_prefetch=1,
            grid=(1,),
            in_specs=specs + specs,
            out_specs=(whole((rows, HALF)),) * 4,
        ),
        compiler_params=pltpu.CompilerParams(vmem_limit_bytes=16 << 20),
        name="sum_corners",
        cost_estimate=light(),
    )(scalars, *([kept] * 4 + [got] * 4))


def columns_kernel(s_ref, a, b, c, d, own, one, two, three, total):
    total[...] = (
        a[...].astype(f32) + b[...].astype(f32) + c[...].astype(f32) + d[...].astype(f32)
    )
    few = total.shape[0] // 4
    for k, out in enumerate((own, one, two, three)):
        row = pl.multiple_of(jnp.bitwise_xor(s_ref[5], k) * few, few)
        out[...] = total[pl.ds(row, few), :].astype(bf16)


def columns(scalars, parts):
    rows = parts[0].shape[0]
    shape = jax.ShapeDtypeStruct((rows // 4, HALF), bf16)
    return pl.pallas_call(
        columns_kernel,
        out_shape=(shape,) * 4,
        grid_spec=pltpu.PrefetchScalarGridSpec(
            num_scalar_prefetch=1,
            grid=(1,),
            in_specs=[whole((rows, HALF))] * 4,
            out_specs=(whole((rows // 4, HALF)),) * 4,
            scratch_shapes=[pltpu.VMEM((rows, HALF), f32)],
        ),
        compiler_params=pltpu.CompilerParams(vmem_limit_bytes=12 << 20),
        name="sum_columns",
        cost_estimate=light(),
    )(scalars, *parts)


def swap_narrow(values):
    return lax.ppermute(values, "narrow", [(0, 1), (1, 0)])


def swap_wide(values, bit, size):
    return lax.ppermute(values, "wide", [(i, i ^ (1 << bit)) for i in range(size)])


def swap_both(values, bit, size):
    flip = 2 << bit
    return lax.ppermute(
        values, ("wide", "narrow"), [(i, i ^ flip ^ 1) for i in range(2 * size)]
    )


def shift_wide(values, flip, size):
    return lax.ppermute(values, "wide", [(i, i ^ flip) for i in range(size)])


def add_low(*items):
    total = items[0].astype(f32)
    for item in items[1:]:
        total = total + item.astype(f32)
    return total.astype(bf16)


def over_corners(parts, size):
    own, over_x, over_y, over_both = parts
    return (
        own,
        swap_wide(over_x, 1, size),
        swap_narrow(over_y),
        swap_both(over_both, 1, size),
    )


def over_columns(parts, size):
    own, *others = parts
    return (own,) + tuple(
        shift_wide(item, (k + 1) << 2, size) for k, item in enumerate(others)
    )


def sum_columns(parts, size):
    packed = add_low(*parts)
    bit = 4
    while 1 << bit < size:
        packed = add_low(packed, swap_wide(packed, bit, size))
        bit += 1
    return packed


def along_columns(packed, size):
    return (packed,) + tuple(shift_wide(packed, k << 2, size) for k in (1, 2, 3))


def tie(*groups):
    held = lax.optimization_barrier(groups)
    return held


def over_cores(near, far, size):
    return (near, far, swap_wide(near, 0, size), swap_wide(far, 0, size))


def gather_chips(piece, size):
    near = swap_narrow(piece)
    high = swap_wide(near, 2, size)
    return near, swap_wide(near, 1, size), high


def gather_cores(items, size):
    pieces = []
    for item in items:
        pieces += [item, swap_wide(item, 0, size)]
    return tuple(pieces)


def on_device(
    wide_size,
    tokens,
    lengths,
    mask_pos,
    mask_vector,
    norm1_gain,
    in_left,
    in_right,
    filter_weight,
    decay,
    skip_gain,
    out_left,
    out_right,
    norm2_gain,
    up_left,
    up_right,
    down_left,
    down_right,
    cotangent,
):
    index = lax.axis_index("wide")
    side = lax.axis_index("narrow")
    row_count = tokens.shape[0] // 2
    scalars = jnp.stack(
        [side, index & 3, (index >> 2) & 1, index & 1, (index >> 1) & 1, (index >> 2) & 3]
    ).astype(jnp.int32)
    share = 1.0 / (2 * wide_size)

    def sent_rows(values):
        return lax.dynamic_slice_in_dim(values, (1 - side) * row_count, row_count, 0)

    mixer_weights = (in_left, in_right, out_left, out_right)
    dense_weights = (up_left, up_right, jnp.swapaxes(down_left, 1, 2), down_right)
    vectors = (mask_vector, norm1_gain, norm2_gain, skip_gain, decay)
    mix_piece, ffn_piece = pack_weights(
        scalars, mixer_weights, dense_weights, filter_weight, vectors
    )
    mix_chips = gather_chips(mix_piece, wide_size)
    mix_chips += (swap_wide(mix_chips[2], 1, wide_size),)
    mix_pieces = gather_cores(mix_chips, wide_size)
    ffn_chips = gather_chips(ffn_piece, wide_size)
    tokens_other = swap_narrow(sent_rows(tokens))
    cot_other = swap_narrow(sent_rows(cotangent))

    positions = jnp.arange(LEN, dtype=jnp.int32)
    valid = (positions[None, :] < lengths[:, None]).astype(f32)
    masked = jnp.any(mask_pos[:, :, None] == positions[None, None, :], axis=1).astype(f32)
    marks = jnp.stack([valid, masked]).reshape(2, 2, row_count)
    marks = lax.dynamic_index_in_dim(marks, side, 1, keepdims=False)
    marks = jnp.concatenate([marks, jnp.zeros((6, row_count), f32)], axis=0)

    fwd, inv = (jnp.asarray(item) for item in transform_tables())
    feats = jnp.asarray(feature_parts())
    taps, spec, penalty, cols = filter_call(
        scalars, filter_weight, mix_piece, mix_pieces, feats, fwd
    )

    ffn_chips, spec = tie(ffn_chips, spec)
    ffn_last = swap_wide(ffn_chips[2], 1, wide_size)
    middle, first, kept, scale, *full = mixer_forward(
        scalars, tokens, tokens_other, marks, cols, spec, fwd, inv, mixer_weights + mix_pieces
    )
    middle, penalty, ffn_last = tie(middle, penalty, ffn_last)
    ffn_pieces = gather_cores(ffn_chips + (ffn_last,), wide_size)
    output, output_sent, grad_middle, ffn_keep, ffn_send, packed_dr = dense(
        scalars, middle, cotangent, cot_other, cols, dense_weights + ffn_pieces
    )
    ffn_parts = corners(scalars, ffn_keep, swap_wide(ffn_send, 0, wide_size))
    grad_middle, ffn_parts, penalty = tie(grad_middle, ffn_parts, penalty[0, 0])
    ffn_parts = over_corners(ffn_parts, wide_size)
    tokens_grad, grad_sent, mix_keep, mix_send = mixer_backward(
        share,
        scalars,
        (grad_middle, first, kept, scale, marks),
        (cols, spec, fwd, inv),
        full,
        (taps, feats, packed_dr),
    )
    mix_keep, mix_send, ffn_parts = tie(mix_keep, mix_send, ffn_parts)
    mix_got = swap_wide(mix_send, 0, wide_size)
    ffn_parts = columns(scalars, ffn_parts)
    mix_got, ffn_parts = tie(mix_got, ffn_parts)
    mix_parts = corners(scalars, mix_keep, mix_got)

    ffn_parts = over_columns(ffn_parts, wide_size)
    mix_parts = over_corners(mix_parts, wide_size)
    ffn_sum = sum_columns(ffn_parts, wide_size)
    ffn_parts = along_columns(ffn_sum, wide_size)
    mix_parts = columns(scalars, mix_parts)
    mix_parts, grad_sent, output_sent = tie(mix_parts, grad_sent, output_sent)
    output_other = swap_narrow(output_sent)
    grad_other = swap_narrow(grad_sent)
    mix_parts = over_columns(mix_parts, wide_size)
    mix_sum = sum_columns(mix_parts, wide_size)
    ffn_near = jnp.concatenate(ffn_parts, axis=0)
    mix_sum, ffn_near, output_other = tie(mix_sum, ffn_near, output_other)
    mix_parts = along_columns(mix_sum, wide_size)
    ffn_far = swap_wide(ffn_near, 1, wide_size)
    mix_near = jnp.concatenate(mix_parts, axis=0)
    mix_far = swap_wide(mix_near, 1, wide_size)
    ffn_parts = over_cores(ffn_near, ffn_far, wide_size)
    gain_two, g_ul, g_ur, g_dl = unpack(
        dense_unpack_kernel, scalars, ffn_parts, DENSE_OUTS, "dense_unpack"
    )
    start = (1 - side) * row_count
    output = lax.dynamic_update_slice_in_dim(output, output_other, start, 0)
    tokens_grad = lax.dynamic_update_slice_in_dim(tokens_grad, grad_other.astype(f32), start, 0)
    mix_far, gain_two, g_ul, g_ur, g_dl, output, tokens_grad = tie(
        mix_far, gain_two, g_ul, g_ur, g_dl, output, tokens_grad
    )
    mix_parts = over_cores(mix_near, mix_far, wide_size)
    g_mask, g_gain, g_skip, g_decay, g_filter, g_il, g_ir, g_ol, g_or, g_dr = unpack(
        mixer_unpack_kernel, scalars, mix_parts, MIXER_OUTS, "mixer_unpack"
    )
    return (
        output,
        tokens_grad,
        g_mask,
        g_gain,
        g_il,
        g_ir,
        g_filter,
        g_decay,
        g_skip,
        g_ol,
        g_or,
        gain_two,
        g_ul,
        g_ur,
        jnp.swapaxes(g_dl, 1, 2),
        g_dr,
        penalty,
    )


def solution(mesh):
    placed = (
        P("wide", "narrow"),
        P("wide"),
        P("wide", None),
        P("narrow"),
        P("narrow"),
        P("narrow", None, None),
        P("narrow", None, None),
        P(None, "narrow"),
        P("narrow"),
        P("narrow"),
        P("narrow", None, None),
        P("narrow", None, None),
        P("narrow"),
        P("narrow", None, None),
        P("narrow", None, None),
        P("narrow", None, None),
        P("narrow", None, None),
        P("wide", "narrow"),
    )
    return jax.shard_map(
        functools.partial(on_device, mesh.shape["wide"]),
        mesh=mesh,
        in_specs=placed,
        out_specs=(
            P("wide", "narrow"),
            P("wide", "narrow"),
            P("narrow"),
            P("narrow"),
            P("narrow", None, None),
            P("narrow", None, None),
            P(None, "narrow"),
            P("narrow"),
            P("narrow"),
            P("narrow", None, None),
            P("narrow", None, None),
            P("narrow"),
            P("narrow", None, None),
            P("narrow", None, None),
            P("narrow", None, None),
            P("narrow", None, None),
            P(),
        ),
        check_vma=False,
    )
```
